256 devices in a mesh: gx: 8 (over x, y_lo), gy: 8 (over z), gz: 4 (over y_hi, core).
Axes of the slice: x: 4, y: 4 (y_hi: 2, y_lo: 2; y = y_hi * 2 + y_lo), z: 8, core: 2. Of those that a mesh axis runs over, the one named last changes fastest.
Arguments:
- tokens: bfloat16 [32, 64, 64, 256], P('gx', 'gy', 'gz'), may hold values from -6 to 6
- cotangent: bfloat16 [16, 32, 32, 512], P('gx', 'gy', 'gz'), may hold values from -6 to 6
- gain_attn: float32 [256], replicated, may hold values from 0.1 to 1.9
- w_qkv: bfloat16 [256, 768], replicated, may hold values from -1 to 1
- w_proj: bfloat16 [256, 256], replicated, may hold values from -0.375 to 0.375
- gain_merge: float32 [2048], replicated, may hold values from 0.1 to 1.9
- w_merge: bfloat16 [2048, 512], replicated, may hold values from -0.125 to 0.125
Outputs:
- merged: bfloat16 [16, 32, 32, 512], P('gx', 'gy', 'gz')
- d_tokens: bfloat16 [32, 64, 64, 256], P('gx', 'gy', 'gz')
- d_gain_attn: float32 [256], replicated
- d_qkv: bfloat16 [256, 768], replicated
- d_proj: bfloat16 [256, 256], replicated
- d_gain_merge: float32 [2048], replicated
- d_merge: bfloat16 [2048, 512], replicated
The draws below stay inside these ranges and needn't reach their ends.
All inputs are finite; a program needn't handle non-finite values.
Results may differ from the reference program's by a relative error of at most 0.014.
The reference program's roundings to bfloat16 on the way count: a program that leaves them out, or rounds other values in their place, can miss the bound.
Values may be sent and summed in bfloat16 or wider, within the bound.
A program may use at most 64 MiB of HBM per device.

```python
import math
import jax
import jax.numpy as jnp
from jax import lax

WIDTH = 256
HEADS = 8
WINDOW = 4
MERGE_WIDTH = 512
NX = 32
NY = 64
NZ = 64
TOKENS = 131072
MERGED_TOKENS = 16384


def draw_w_qkv(key, part):
    key = jax.random.fold_in(key, 7)
    first = jax.random.fold_in(key, 0)
    matrix = jax.random.normal(first, (WIDTH, 3 * WIDTH), jnp.float32) / math.sqrt(WIDTH)
    return jnp.clip(matrix, -1.0, 1.0).astype(jnp.bfloat16)


def block_scale(own_key, shape, cuts, low, largest):
    level, own = 1.0, jax.random.fold_in(own_key, 6)
    for axis_at, parts in cuts:
        heights = jnp.exp(jax.random.uniform(jax.random.fold_in(own, axis_at), (parts,), jnp.float32, low / len(cuts), largest / len(cuts)))
        level = level * jnp.repeat(heights, shape[axis_at] // parts).reshape([-1 if axis == axis_at else 1 for axis in range(len(shape))])
    return level


def scatter_about(stream_key, dims, deviation, most, cuts=(), kind=jnp.bfloat16):
    gain = block_scale(stream_key, dims, cuts, -0.22, 0.18) if cuts else 1.0
    values = jax.random.normal(stream_key, dims, jnp.float32) * deviation * gain
    return jnp.minimum(jnp.maximum(values, -most), most).astype(kind)


def setup_inputs(seed: int = 0) -> dict:
    key_of = jax.random.split(jax.random.key(seed), 8)
    return {
        "tokens": scatter_about(key_of[0], (NX, NY, NZ, WIDTH), 1.0, 6.0, ((0, 8), (1, 8), (2, 4))),
        "cotangent": scatter_about(key_of[1], (NX // 2, NY // 2, NZ // 2, MERGE_WIDTH), 1.0, 6.0, ((0, 8), (1, 8), (2, 4))),
        "gain_attn": jnp.clip(1.0 + 0.18 * jax.random.normal(key_of[2], (WIDTH,), jnp.float32), 0.1, 1.9),
        "w_qkv": draw_w_qkv(jax.random.fold_in(key_of[7], 71), 0),
        "w_proj": scatter_about(key_of[4], (WIDTH, WIDTH), WIDTH ** -0.5, 0.375),
        "gain_merge": jnp.clip(1.0 + 0.18 * jax.random.normal(key_of[5], (8 * WIDTH,), jnp.float32), 0.1, 1.9),
        "w_merge": scatter_about(key_of[6], (8 * WIDTH, MERGE_WIDTH), (8 * WIDTH) ** -0.5, 0.125),
    }


epsilon = 1e-05

def normed(values, scaling):
    average = lax.optimization_barrier(jnp.mean(values, axis=-1, keepdims=True))
    centred = values - average
    variance = lax.optimization_barrier(jnp.mean(centred * centred, axis=-1, keepdims=True))
    return centred * lax.rsqrt(variance + epsilon) * scaling

def to_windows(volume, window_side):
    extent_a, extent_b, extent_c, features = volume.shape
    shaped = volume.reshape(extent_a // window_side, window_side, extent_b // window_side, window_side, extent_c // window_side, window_side, features)
    return shaped.transpose(0, 2, 4, 1, 3, 5, 6).reshape(-1, window_side * window_side * window_side, features)

def from_windows(windows, extent_a, extent_b, extent_c, window_side):
    features = windows.shape[-1]
    shaped = windows.reshape(extent_a // window_side, extent_b // window_side, extent_c // window_side, window_side, window_side, window_side, features)
    return shaped.transpose(0, 3, 1, 4, 2, 5, 6).reshape(extent_a, extent_b, extent_c, features)

def group_pairs(volume):
    extent_a, extent_b, extent_c, features = volume.shape
    shaped = volume.reshape(extent_a // 2, 2, extent_b // 2, 2, extent_c // 2, 2, features)
    return shaped.transpose(0, 2, 4, 1, 3, 5, 6).reshape(extent_a // 2, extent_b // 2, extent_c // 2, 8 * features)

def split_pairs(grouped, features):
    extent_a, extent_b, extent_c = grouped.shape[:3]
    shaped = grouped.reshape(extent_a, extent_b, extent_c, 2, 2, 2, features)
    return shaped.transpose(0, 3, 1, 4, 2, 5, 6).reshape(2 * extent_a, 2 * extent_b, 2 * extent_c, features)

def inner_rows(left_rows, right_rows):
    return lax.dot_general(left_rows, right_rows, (((0,), (0,)), ((), ())), preferred_element_type=jnp.float32)

def times_t(left_rows, matrix):
    return lax.dot_general(left_rows, matrix, (((1,), (1,)), ((), ())), preferred_element_type=jnp.float32)

def batched(form, left_side, right_side):
    return jnp.einsum(form, left_side.astype(jnp.float32), right_side.astype(jnp.float32))

def attend_forward(rolled, gain_attn, w_qkv, w_proj, head_count):
    extent_a, extent_b, extent_c, channels = rolled.shape
    windows = to_windows(rolled, WINDOW)
    windows_count, window_cells = (windows.shape[0], windows.shape[1])
    flat_rows = windows.reshape(-1, channels).astype(jnp.float32)
    normal_rows = normed(flat_rows, gain_attn).astype(jnp.bfloat16)
    project = jnp.dot(normal_rows, w_qkv, preferred_element_type=jnp.float32).astype(jnp.bfloat16)
    project = project.reshape(windows_count, window_cells, 3, head_count, channels // head_count)
    queries = project[:, :, 0]
    keys_all = project[:, :, 1]
    values_all = project[:, :, 2]
    factor = (channels // head_count) ** (-0.5)
    scores = batched('wqhd,wkhd->whqk', queries, keys_all) * factor
    weights = jax.nn.softmax(scores, axis=-1)
    rounded = weights.astype(jnp.bfloat16)
    mixed_rows = batched('whqk,wkhd->wqhd', rounded, values_all).astype(jnp.bfloat16).reshape(-1, channels)
    output = jnp.dot(mixed_rows, w_proj, preferred_element_type=jnp.float32)
    summed_rows = (flat_rows + output).astype(jnp.bfloat16)
    result = from_windows(summed_rows.reshape(windows_count, window_cells, channels), extent_a, extent_b, extent_c, WINDOW)
    saved_state = (flat_rows, normal_rows, queries, keys_all, values_all, weights, rounded, mixed_rows)
    return (result, saved_state)

def attend_backward(saved_state, grad_sum, gain_attn, w_qkv, w_proj, head_count):
    flat_rows, normal_rows, queries, keys_all, values_all, weights, rounded, mixed_rows = saved_state
    windows_count, window_cells = (queries.shape[0], queries.shape[1])
    extent_a, extent_b, extent_c, channels = grad_sum.shape
    factor = (channels // head_count) ** (-0.5)
    grad_rows = to_windows(grad_sum, WINDOW).reshape(-1, channels)
    grad_proj = inner_rows(mixed_rows, grad_rows)
    grad_mixed = times_t(grad_rows, w_proj).astype(jnp.bfloat16)
    grad_mixed = grad_mixed.reshape(windows_count, window_cells, head_count, channels // head_count)
    grad_weights = batched('wqhd,wkhd->whqk', grad_mixed, values_all)
    grad_values = batched('whqk,wqhd->wkhd', rounded, grad_mixed)
    grad_scores = weights * (grad_weights - lax.optimization_barrier(jnp.sum(grad_weights * weights, axis=-1, keepdims=True)))
    grad_scaled = (grad_scores * factor).astype(jnp.bfloat16)
    grad_queries = batched('whqk,wkhd->wqhd', grad_scaled, keys_all)
    grad_keys = batched('whqk,wqhd->wkhd', grad_scaled, queries)
    grad_project = jnp.stack([grad_queries, grad_keys, grad_values], axis=2).astype(jnp.bfloat16).reshape(-1, 3 * channels)
    grad_qkv = inner_rows(normal_rows, grad_project)
    grad_normal = times_t(grad_project, w_qkv)
    ignored, pullback = jax.vjp(normed, flat_rows, gain_attn)
    grad_flat, grad_gain = pullback(grad_normal)
    grad_total = (grad_rows.astype(jnp.float32) + grad_flat).astype(jnp.bfloat16)
    result = from_windows(grad_total.reshape(windows_count, window_cells, channels), extent_a, extent_b, extent_c, WINDOW)
    return (result, grad_gain, grad_qkv, grad_proj)

def merge_pass(volume, gain_merge, w_merge, grad_out):
    channels = volume.shape[-1]
    grouped = group_pairs(volume)
    flat_rows = grouped.reshape(-1, grouped.shape[-1]).astype(jnp.float32)
    normal_rows = normed(flat_rows, gain_merge).astype(jnp.bfloat16)
    output = jnp.dot(normal_rows, w_merge, preferred_element_type=jnp.float32).astype(jnp.bfloat16)
    output = output.reshape(grouped.shape[:3] + (w_merge.shape[1],))
    grad_rows = grad_out.reshape(-1, grad_out.shape[-1])
    grad_weight = inner_rows(normal_rows, grad_rows)
    grad_normal = times_t(grad_rows, w_merge)
    ignored, pullback = jax.vjp(normed, flat_rows, gain_merge)
    grad_flat, grad_gain = pullback(grad_normal)
    grad_volume = split_pairs(grad_flat.astype(jnp.bfloat16).reshape(grouped.shape), channels)
    return (output, grad_volume, grad_gain, grad_weight)

def reference(tokens, cotangent, gain_attn, w_qkv, w_proj, gain_merge, w_merge):
    half_window = WINDOW // 2
    rolled = jnp.roll(tokens, (-half_window, -half_window, -half_window), axis=(0, 1, 2))
    grad_rolled = jnp.roll(cotangent, (-(half_window // 2), -(half_window // 2), -(half_window // 2)), axis=(0, 1, 2))
    slab_stack = rolled.reshape(NX // WINDOW, WINDOW, NY, NZ, WIDTH)
    grad_stack = grad_rolled.reshape(NX // WINDOW, WINDOW // 2, NY // 2, NZ // 2, MERGE_WIDTH)

    def slab_pass(running, pieces):
        slab_tokens, slab_grad = pieces
        summed, saved_state = attend_forward(slab_tokens, gain_attn, w_qkv, w_proj, HEADS)
        merged_slab, grad_sum, grad_gm, grad_wm = merge_pass(summed, gain_merge, w_merge, slab_grad)
        grad_slab, grad_ga, grad_wq, grad_wp = attend_backward(saved_state, grad_sum, gain_attn, w_qkv, w_proj, HEADS)
        running = (running[0] + grad_ga, running[1] + grad_wq, running[2] + grad_wp, running[3] + grad_gm, running[4] + grad_wm)
        return (running, (merged_slab, grad_slab))
    initial = (jnp.zeros((WIDTH,), jnp.float32), jnp.zeros((WIDTH, 3 * WIDTH), jnp.float32), jnp.zeros((WIDTH, WIDTH), jnp.float32), jnp.zeros((8 * WIDTH,), jnp.float32), jnp.zeros((8 * WIDTH, MERGE_WIDTH), jnp.float32))
    totals, outputs = lax.scan(slab_pass, initial, (slab_stack, grad_stack))
    merged = jnp.roll(outputs[0].reshape(NX // 2, NY // 2, NZ // 2, MERGE_WIDTH), (half_window // 2, half_window // 2, half_window // 2), axis=(0, 1, 2))
    d_tokens = jnp.roll(outputs[1].reshape(NX, NY, NZ, WIDTH), (half_window, half_window, half_window), axis=(0, 1, 2))
    token_scale = TOKENS ** (-0.5)
    merge_scale = MERGED_TOKENS ** (-0.5)
    return (merged, d_tokens, totals[0] * token_scale, (totals[1] * token_scale).astype(jnp.bfloat16), (totals[2] * token_scale).astype(jnp.bfloat16), totals[3] * merge_scale, (totals[4] * merge_scale).astype(jnp.bfloat16))
```

```python
import functools

import jax
import jax.numpy as jnp
import numpy as np
from jax import lax
from jax.experimental import pallas as pl
from jax.experimental.pallas import tpu as pltpu
from jax.sharding import PartitionSpec as P

MESH = pl.DeviceIdType.MESH
HEADS = 8
WIDTH = 256
CELLS = 512
GROUPS = 64
ROWS = CELLS + 2 * GROUPS
FACTOR = 32 ** -0.5
EPSILON = 1e-05
TOKENS = 131072
TOKEN_SCALE = float(TOKENS) ** (-0.5)
MERGE_SCALE = float(TOKENS // 8) ** (-0.5)
BF16, F32 = jnp.bfloat16, jnp.float32

KINDS = [(a, b, c) for a in (0, 1) for b in (0, 1) for c in (0, 1)]


def kind_groups(kind):
    a, b, c = kind
    return [
        (i, j, k)
        for i in ([0] if a else [1])
        for j in ([0] if b else [1, 2, 3])
        for k in ([0] if c else list(range(1, 8)))
    ]


SIZES = [-(-10 * len(kind_groups(kind)) // 16) * 16 for kind in KINDS]
STARTS = [sum(SIZES[:i]) for i in range(8)]
HALO = sum(SIZES)


def orderings():
    leave, enter = np.zeros((HALO, ROWS), np.float32), np.zeros((ROWS, HALO), np.float32)
    for kind, start in zip(KINDS, STARTS):
        for at, (i, j, k) in enumerate(kind_groups(kind)):
            si, sj, sk = (i - 1) % 2, (j - 1) % 4, (k - 1) % 8
            window, place = (sj // 2) * 4 + sk // 2, si * 4 + (sj % 2) * 2 + sk % 2
            for o in range(8):
                cell = ((2 * i + o // 4) * 8 + 2 * j + o // 2 % 2) * 16 + 2 * k + o % 2
                leave[start + at * 10 + o, cell] = 1
                enter[window * 64 + o * 8 + place, start + at * 10 + o] = 1
            for t in range(2):
                leave[start + at * 10 + 8 + t, CELLS + t * GROUPS + (i * 4 + j) * 8 + k] = 1
                enter[CELLS + t * GROUPS + window * 8 + place, start + at * 10 + 8 + t] = 1
    return leave, enter


def dot(left, right, left_dim=1, right_dim=0):
    return lax.dot_general(
        left, right, (((left_dim,), (right_dim,)), ((), ())), preferred_element_type=F32
    )


def norm_parts(parts, count):
    average = sum(jnp.sum(p, axis=-1, keepdims=True) for p in parts) * (1.0 / count)
    centred = [p - average for p in parts]
    variance = sum(jnp.sum(p * p, axis=-1, keepdims=True) for p in centred) * (1.0 / count)
    return centred, lax.rsqrt(variance + EPSILON)


def norm_back(hats, grads, inverse, count):
    first = sum(jnp.sum(g, axis=-1, keepdims=True) for g in grads) * (1.0 / count)
    second = sum(jnp.sum(g * h, axis=-1, keepdims=True) for g, h in zip(grads, hats)) * (1.0 / count)
    return [inverse * (g - first - h * second) for g, h in zip(grads, hats)]


def kernel(
    tokens, cotangent, gain_attn, gain_merge, w_qkv_hbm, w_proj_hbm, w_merge_hbm,
    leave_hbm, enter_hbm, back_hbm, home_hbm,
    merged_out, d_tokens_out, d_gain_attn_out, d_qkv_out, d_proj_out, d_gain_merge_out, d_merge_out,
    w_qkv, w_proj, w_merge, leave, enter, back, home, local_sem,
    stacked, halo_send, halo_recv, back_send, back_recv,
    flat, hat, normal, inverse_a, qkv, probs, attended, summed, d_summed, d_attended, d_qkv, heads,
    cot, nm, hat_m, nm_near, cot_near, pair_rows, pair_cot,
    m_sum, m_in1, m_acc1, m_in2, m_acc2, m_in3,
    q_sum, q_near, q_half, q_in1, q_acc1, q_in2, q_acc2, q_in3, q_out,
    g_sum, g_near, g_in1, g_in2, g_in3,
    send_sem, recv_sem,
):
    gx, gy, gz = lax.axis_index("gx"), lax.axis_index("gy"), lax.axis_index("gz")
    x, y_low, z = lax.div(gx, 2), lax.rem(gx, 2), gy
    y_high, core = lax.div(gz, 2), lax.rem(gz, 2)
    y = y_high * 2 + y_low

    def device(x_at, y_at, z_at, core_at):
        return (x_at * 2 + lax.rem(y_at, 2), z_at, lax.div(y_at, 2) * 2 + core_at)

    def along(axis, step):
        if axis == "x":
            return device(lax.rem(x + step, 4), y, z, core)
        if axis == "y":
            return device(x, lax.rem(y + step, 4), z, core)
        return device(x, y, lax.rem(z + step, 8), core)

    other_core = 1 - core
    partner = device(x, y, z, other_core)
    coordinate = {"x": x, "y": y, "z": z}

    def neighbour(kind, sign):
        a, b, c = kind
        return (
            lax.rem(gx + (8 + sign * a), 8),
            lax.rem(gy + (8 + sign * b), 8),
            lax.rem(gz + (4 + sign * c), 4),
        )

    started = []

    def send(source, target, to):
        at = len(started)
        copy = pltpu.make_async_remote_copy(
            src_ref=source, dst_ref=target, send_sem=send_sem.at[at], recv_sem=recv_sem.at[at],
            device_id=to, device_id_type=MESH,
        )
        copy.start()
        started.append(copy)
        return copy

    def arrive(copies):
        for copy in copies:
            copy.wait_recv()

    def rows(at, count):
        return pl.ds(pl.multiple_of(at * count, count), count)

    barrier = pltpu.get_barrier_semaphore()
    partners = [neighbour(kind, sign) for kind in KINDS[1:] for sign in (-1, 1)]
    partners += [partner]
    partners += [along(axis, step) for axis in "xy" for step in (1, 2, 3)]
    partners += [along("z", step) for step in range(1, 8)]
    for there in partners:
        pl.semaphore_signal(barrier, inc=1, device_id=there, device_id_type=MESH)

    loads = {}
    for at, (name, source, target) in enumerate((
        ("leave", leave_hbm, leave), ("enter", enter_hbm, enter), ("w_qkv", w_qkv_hbm, w_qkv),
        ("w_proj", w_proj_hbm, w_proj), ("w_merge", w_merge_hbm, w_merge),
        ("back", back_hbm, back), ("home", home_hbm, home),
    )):
        loads[name] = pltpu.make_async_copy(source, target, local_sem.at[at])
        loads[name].start()

    stacked[0:CELLS, :] = tokens[...]
    stacked[CELLS : CELLS + GROUPS, :] = cotangent[:, 0:WIDTH]
    stacked[CELLS + GROUPS :, :] = cotangent[:, WIDTH:]
    loads["leave"].wait()
    halo_send[...] = dot(leave[...], stacked[...]).astype(BF16)

    pl.semaphore_wait(barrier, len(partners))
    halo = []
    for kind, start, size in list(zip(KINDS, STARTS, SIZES))[1:]:
        block = pl.ds(start, size)
        halo.append(send(halo_send.at[block], halo_recv.at[block], neighbour(kind, -1)))
    halo_recv[0 : SIZES[0], :] = halo_send[0 : SIZES[0], :]
    head_of_lane = lax.div(lax.broadcasted_iota(jnp.int32, (64, WIDTH), 1), 32)
    for h in range(HEADS):
        heads[h * 64 : (h + 1) * 64, :] = jnp.where(head_of_lane == h, 1.0, 0.0).astype(BF16)
    loads["enter"].wait()
    loads["w_qkv"].wait()
    arrive(halo)

    flat[...] = dot(enter[0:CELLS, :], halo_recv[...])
    for t in range(2):
        part = dot(enter[CELLS + t * GROUPS : CELLS + (t + 1) * GROUPS, :], halo_recv[...])
        cot[:, t * WIDTH : (t + 1) * WIDTH] = part.astype(BF16)
    chip = [send(cot, cot_near, partner)]
    (centred,), inverse = norm_parts([flat[...]], WIDTH)
    inverse_a[...] = inverse
    hat[...] = centred * inverse
    normal[...] = (hat[...] * gain_attn[...]).astype(BF16)
    qkv[...] = dot(normal[...], w_qkv[...]).astype(BF16)

    def spread(block):
        return jnp.concatenate([block] * HEADS, axis=0) * heads[...]

    def gather(wide):
        total = wide[0:64]
        for h in range(1, HEADS):
            total = jnp.where(head_of_lane == h, wide[h * 64 : (h + 1) * 64], total)
        return total

    def forward(w, carry):
        here = rows(w, 64)
        query, key, value = (qkv[here, i * WIDTH : (i + 1) * WIDTH] for i in range(3))
        scores = dot(key, spread(query), 1, 1) * FACTOR
        powers = jnp.exp(scores - jnp.max(scores, axis=0, keepdims=True))
        weights = powers * (1.0 / jnp.sum(powers, axis=0, keepdims=True))
        probs[here, :] = weights
        attended[here, :] = gather(dot(weights.astype(BF16), value, 0, 0)).astype(BF16)
        return carry

    lax.fori_loop(0, 8, forward, 0)
    loads["w_proj"].wait()
    summed[...] = (flat[...] + dot(attended[...], w_proj[...])).astype(BF16).astype(F32)

    shaped = summed[...].reshape(8, 8, 8, WIDTH)
    slabs = [shaped[:, o].reshape(GROUPS, WIDTH) for o in range(8)]
    centred, inverse = norm_parts(slabs, 8 * WIDTH)
    for o in range(8):
        lanes = slice(o * WIDTH, (o + 1) * WIDTH)
        hat_m[:, lanes] = centred[o] * inverse
        nm[:, lanes] = (hat_m[:, lanes] * gain_merge[:, lanes]).astype(BF16)
    chip.append(send(nm.at[:, rows(other_core, 1024)], nm_near, partner))
    loads["w_merge"].wait()
    result = dot(nm[...], w_merge[...]).astype(BF16)
    for t in range(2):
        stacked[CELLS + t * GROUPS : CELLS + (t + 1) * GROUPS, :] = result[:, t * WIDTH : (t + 1) * WIDTH]
    hats, grads = [], []
    for o in range(8):
        lanes = slice(o * WIDTH, (o + 1) * WIDTH)
        grad = dot(cot[...], w_merge[lanes, :], 1, 1)
        hats.append(hat_m[:, lanes])
        grads.append(grad * gain_merge[:, lanes])
        g_sum[o : o + 1, :] = jnp.sum(grad * hats[o], axis=0, keepdims=True)
    grads = norm_back(hats, grads, inverse, 8 * WIDTH)
    joined = jnp.stack([g.reshape(8, 8, WIDTH) for g in grads], axis=1).reshape(CELLS, WIDTH)
    d_summed[...] = joined.astype(BF16)

    arrive(chip)
    pair_rows[0:64, :] = nm[:, rows(core, 1024)]
    pair_rows[64:128, :] = nm_near[...]
    pair_cot[0:64, :] = cot[...]
    pair_cot[64:128, :] = cot_near[...]

    def m_block(i, carry):
        here = rows(i, 128)
        m_sum[here, :] = dot(pair_rows[:, here], pair_cot[...], 0, 0)
        return carry

    lax.fori_loop(0, 8, m_block, 0)
    orders = (("x", "y"), ("y", "x"))

    def m_first(half):
        axis = orders[half][0]
        copies = []
        for step in (1, 2, 3):
            chunk = half * 4 + lax.rem(coordinate[axis] + step, 4)
            copies.append(send(m_sum.at[rows(chunk, 128)], m_in1.at[half, step - 1], along(axis, step)))
        return copies

    m_copies = [m_first(0), m_first(1)]

    q_sum[:, 3 * WIDTH :] = dot(attended[...], d_summed[...], 0, 0)
    d_attended[...] = dot(d_summed[...], w_proj[...], 1, 1).astype(BF16)

    def backward(w, carry):
        here = rows(w, 64)
        query, key, value = (qkv[here, i * WIDTH : (i + 1) * WIDTH] for i in range(3))
        weights = probs[here, :]
        wide = spread(d_attended[here, :])
        d_probs = dot(value, wide, 1, 1)
        d_value = dot(weights.astype(BF16), wide)
        inner = jnp.sum(d_probs * weights, axis=0, keepdims=True)
        d_scores = (weights * (d_probs - inner) * FACTOR).astype(BF16)
        d_key = dot(d_scores, spread(query))
        d_query = gather(dot(d_scores, key, 0, 0))
        d_qkv[here, 0:WIDTH] = d_query.astype(BF16)
        d_qkv[here, WIDTH : 2 * WIDTH] = d_key.astype(BF16)
        d_qkv[here, 2 * WIDTH :] = d_value.astype(BF16)
        return carry

    lax.fori_loop(0, 4, backward, 0)

    def m_second(half):
        first, second = orders[half]
        arrive(m_copies[half])
        own = m_sum[rows(half * 4 + coordinate[first], 128), :]
        m_acc1[half] = own + m_in1[half, 0] + m_in1[half, 1] + m_in1[half, 2]
        copies = []
        for step in (1, 2, 3):
            chunk = rows(lax.rem(coordinate[second] + step, 4), 32)
            copies.append(send(m_acc1.at[half, chunk], m_in2.at[half, step - 1], along(second, step)))
        return copies

    m_copies = [m_second(0), m_second(1)]
    lax.fori_loop(4, 8, backward, 0)

    def m_third(half):
        second = orders[half][1]
        arrive(m_copies[half])
        own = m_acc1[half, rows(coordinate[second], 32), :]
        m_acc2[half] = own + m_in2[half, 0] + m_in2[half, 1] + m_in2[half, 2]
        copies = []
        for step in range(1, 8):
            there = lax.rem(z + step, 8)
            chunk = m_acc2.at[half, rows(lax.div(there, 4), 16), rows(lax.rem(there, 4), 128)]
            copies.append(send(chunk, m_in3.at[half, step - 1], along("z", step)))
        return copies

    m_copies = [m_third(0), m_third(1)]

    q_sum[:, 0 : 3 * WIDTH] = dot(normal[...], d_qkv[...], 0, 0)
    q_chip = send(q_sum.at[:, rows(other_core, 512)], q_near, partner)
    d_normal = dot(d_qkv[...], w_qkv[...], 1, 1)
    g_sum[8:16, :] = jnp.zeros((8, WIDTH), F32)
    g_sum[8:9, :] = jnp.sum(d_normal * hat[...], axis=0, keepdims=True)
    g_chip = send(g_sum, g_near, partner)
    (d_flat,) = norm_back([hat[...]], [d_normal * gain_attn[...]], inverse_a[...], WIDTH)
    stacked[0:CELLS, :] = (d_summed[...].astype(F32) + d_flat).astype(BF16)
    loads["back"].wait()
    back_send[...] = dot(back[...], stacked[...]).astype(BF16)
    halo = []
    for kind, start, size in list(zip(KINDS, STARTS, SIZES))[1:]:
        block = pl.ds(start, size)
        halo.append(send(back_send.at[block], back_recv.at[block], neighbour(kind, 1)))
    back_recv[0 : SIZES[0], :] = back_send[0 : SIZES[0], :]

    def m_place(half, x_or_y_first, x_or_y_second):
        return core * 1024 + half * 512 + x_or_y_first * 128 + x_or_y_second * 32

    def m_fourth(half):
        first, second = orders[half]
        arrive(m_copies[half])
        high, lane = lax.div(z, 4), rows(lax.rem(z, 4), 128)
        total = m_acc2[half, rows(high, 16), lane]
        for step in range(7):
            total = total + m_in3[half, step]
        start = m_place(half, coordinate[first], coordinate[second]) + high * 16
        here = (pl.ds(pl.multiple_of(start, 16), 16), lane)
        d_merge_out[here] = (total * MERGE_SCALE).astype(BF16)
        place = d_merge_out.at[here]
        return [send(place, place, along("z", step)) for step in range(1, 8)]

    m_copies = [m_fourth(0), m_fourth(1)]

    q_chip.wait_recv()
    q_half[...] = q_sum[:, rows(core, 512)] + q_near[...]

    def q_first(half):
        axis = orders[half][0]
        copies = []
        for step in (1, 2, 3):
            chunk = half * 4 + lax.rem(coordinate[axis] + step, 4)
            copies.append(send(q_half.at[rows(chunk, 32)], q_in1.at[half, step - 1], along(axis, step)))
        return copies

    q_copies = [q_first(0), q_first(1)]
    g_chip.wait_recv()

    def g_start(total, into, axis, count):
        into[coordinate[axis]] = total
        mine = into.at[coordinate[axis]]
        return [send(mine, mine, along(axis, step)) for step in range(1, count)]

    def g_total(into, count):
        total = into[0]
        for i in range(1, count):
            total = total + into[i]
        return total

    g_copies = g_start(g_sum[...] + g_near[...], g_in1, "x", 4)

    def m_fifth(half):
        first, second = orders[half]
        arrive(m_copies[half])
        start = m_place(half, coordinate[first], coordinate[second])
        place = d_merge_out.at[pl.ds(pl.multiple_of(start, 32), 32)]
        return [send(place, place, along(second, step)) for step in (1, 2, 3)]

    m_copies = [m_fifth(0), m_fifth(1)]

    def q_second(half):
        first, second = orders[half]
        arrive(q_copies[half])
        own = q_half[rows(half * 4 + coordinate[first], 32), :]
        q_acc1[half] = own + q_in1[half, 0] + q_in1[half, 1] + q_in1[half, 2]
        copies = []
        for step in (1, 2, 3):
            lane = rows(lax.rem(coordinate[second] + step, 4), 128)
            copies.append(send(q_acc1.at[half, :, lane], q_in2.at[half, step - 1], along(second, step)))
        return copies

    q_copies = [q_second(0), q_second(1)]
    arrive(g_copies)
    g_copies = g_start(g_total(g_in1, 4), g_in2, "y", 4)

    def m_sixth(half):
        first = orders[half][0]
        arrive(m_copies[half])
        place = d_merge_out.at[rows(core * 8 + half * 4 + coordinate[first], 128)]
        return [send(place, place, along(first, step)) for step in (1, 2, 3)]

    m_copies = [m_sixth(0), m_sixth(1)]

    def q_third(half):
        second = orders[half][1]
        arrive(q_copies[half])
        own = q_acc1[half, :, rows(coordinate[second], 128)]
        q_acc2[half] = own + q_in2[half, 0] + q_in2[half, 1] + q_in2[half, 2]
        q_in3[half, z] = q_acc2[half, rows(lax.rem(z, 2), 16), :]
        copies = []
        for step in range(1, 8):
            chunk = q_acc2.at[half, rows(lax.rem(z + step, 2), 16)]
            copies.append(send(chunk, q_in3.at[half, z], along("z", step)))
        return copies

    q_copies = [q_third(0), q_third(1)]
    arrive(g_copies)
    g_copies = g_start(g_total(g_in2, 4), g_in3, "z", 8)

    loads["home"].wait()
    arrive(halo)
    placed = dot(home[...], back_recv[...]).astype(BF16)
    d_tokens_out[...] = placed[0:CELLS]
    merged_out[:, 0:WIDTH] = placed[CELLS : CELLS + GROUPS]
    merged_out[:, WIDTH:] = placed[CELLS + GROUPS :]

    def q_place(half, first_at):
        return half * 128 + first_at * 32

    def q_fourth(half):
        first, second = orders[half]
        arrive(q_copies[half])
        total = q_in3[half, 0]
        for i in range(1, 8):
            total = total + q_in3[half, i]
        start = q_place(half, coordinate[first]) + lax.rem(z, 2) * 16
        lane = rows(core * 4 + coordinate[second], 128)
        here = (pl.ds(pl.multiple_of(start, 16), 16), lane)
        q_out[here] = (total * TOKEN_SCALE).astype(BF16)
        place = q_out.at[here]
        return [send(place, place, device(x, y, z + 1 - 2 * lax.rem(z, 2), core))]

    q_copies = [q_fourth(0), q_fourth(1)]

    def q_fifth(half):
        first, second = orders[half]
        arrive(q_copies[half])
        start = pl.multiple_of(q_place(half, coordinate[first]), 32)
        place = q_out.at[pl.ds(start, 32), rows(core * 4 + coordinate[second], 128)]
        return [send(place, place, along(second, step)) for step in (1, 2, 3)]

    q_copies = [q_fifth(0), q_fifth(1)]
    arrive(m_copies[0])
    arrive(m_copies[1])
    place = d_merge_out.at[rows(core, 1024)]
    last = [send(place, place, partner)]

    def q_sixth(half):
        first = orders[half][0]
        arrive(q_copies[half])
        start = pl.multiple_of(q_place(half, coordinate[first]), 32)
        place = q_out.at[pl.ds(start, 32), rows(core, 512)]
        return [send(place, place, along(first, step)) for step in (1, 2, 3)]

    q_copies = [q_sixth(0), q_sixth(1)]
    arrive(g_copies)
    total = g_total(g_in3, 8)
    for o in range(8):
        d_gain_merge_out[:, o * WIDTH : (o + 1) * WIDTH] = total[o : o + 1] * MERGE_SCALE
    d_gain_attn_out[...] = total[8:9] * TOKEN_SCALE
    arrive(q_copies[0])
    arrive(q_copies[1])
    place = q_out.at[:, rows(core, 512)]
    last.append(send(place, place, partner))
    arrive(last)
    d_qkv_out[...] = q_out[:, 0 : 3 * WIDTH]
    d_proj_out[...] = q_out[:, 3 * WIDTH :]
    for copy in started:
        copy.wait_send()


def local(leave, enter, back, home, tokens, cotangent, gain_attn, w_qkv, w_proj, gain_merge, w_merge):
    vmem, anywhere = pl.BlockSpec(memory_space=pltpu.VMEM), pl.BlockSpec(memory_space=pl.ANY)
    copies = 200
    outs = pl.pallas_call(
        kernel,
        out_shape=(
            jax.ShapeDtypeStruct((GROUPS, 512), BF16),
            jax.ShapeDtypeStruct((CELLS, WIDTH), BF16),
            jax.ShapeDtypeStruct((1, WIDTH), F32),
            jax.ShapeDtypeStruct((WIDTH, 3 * WIDTH), BF16),
            jax.ShapeDtypeStruct((WIDTH, WIDTH), BF16),
            jax.ShapeDtypeStruct((1, 8 * WIDTH), F32),
            jax.ShapeDtypeStruct((8 * WIDTH, 512), BF16),
        ),
        in_specs=[vmem] * 4 + [anywhere] * 7,
        out_specs=[vmem] * 7,
        scratch_shapes=[
            pltpu.VMEM((WIDTH, 3 * WIDTH), BF16),
            pltpu.VMEM((WIDTH, WIDTH), BF16),
            pltpu.VMEM((8 * WIDTH, 512), BF16),
            pltpu.VMEM((HALO, ROWS), BF16),
            pltpu.VMEM((ROWS, HALO), BF16),
            pltpu.VMEM((HALO, ROWS), BF16),
            pltpu.VMEM((ROWS, HALO), BF16),
            pltpu.SemaphoreType.DMA((7,)),
            pltpu.VMEM((ROWS, WIDTH), BF16),
            pltpu.VMEM((HALO, WIDTH), BF16),
            pltpu.VMEM((HALO, WIDTH), BF16),
            pltpu.VMEM((HALO, WIDTH), BF16),
            pltpu.VMEM((HALO, WIDTH), BF16),
            pltpu.VMEM((CELLS, WIDTH), F32),
            pltpu.VMEM((CELLS, WIDTH), F32),
            pltpu.VMEM((CELLS, WIDTH), BF16),
            pltpu.VMEM((CELLS, 1), F32),
            pltpu.VMEM((CELLS, 3 * WIDTH), BF16),
            pltpu.VMEM((CELLS, 512), F32),
            pltpu.VMEM((CELLS, WIDTH), BF16),
            pltpu.VMEM((CELLS, WIDTH), F32),
            pltpu.VMEM((CELLS, WIDTH), BF16),
            pltpu.VMEM((CELLS, WIDTH), BF16),
            pltpu.VMEM((CELLS, 3 * WIDTH), BF16),
            pltpu.VMEM((CELLS, WIDTH), BF16),
            pltpu.VMEM((GROUPS, 512), BF16),
            pltpu.VMEM((GROUPS, 8 * WIDTH), BF16),
            pltpu.VMEM((GROUPS, 8 * WIDTH), F32),
            pltpu.VMEM((GROUPS, 1024), BF16),
            pltpu.VMEM((GROUPS, 512), BF16),
            pltpu.VMEM((2 * GROUPS, 1024), BF16),
            pltpu.VMEM((2 * GROUPS, 512), BF16),
            pltpu.VMEM((1024, 512), F32),
            pltpu.VMEM((2, 3, 128, 512), F32),
            pltpu.VMEM((2, 128, 512), F32),
            pltpu.VMEM((2, 3, 32, 512), F32),
            pltpu.VMEM((2, 32, 512), F32),
            pltpu.VMEM((2, 7, 16, 128), F32),
            pltpu.VMEM((WIDTH, 1024), F32),
            pltpu.VMEM((WIDTH, 512), F32),
            pltpu.VMEM((WIDTH, 512), F32),
            pltpu.VMEM((2, 3, 32, 512), F32),
            pltpu.VMEM((2, 32, 512), F32),
            pltpu.VMEM((2, 3, 32, 128), F32),
            pltpu.VMEM((2, 32, 128), F32),
            pltpu.VMEM((2, 8, 16, 128), F32),
            pltpu.VMEM((WIDTH, 1024), BF16),
            pltpu.VMEM((16, WIDTH), F32),
            pltpu.VMEM((16, WIDTH), F32),
            pltpu.VMEM((4, 16, WIDTH), F32),
            pltpu.VMEM((4, 16, WIDTH), F32),
            pltpu.VMEM((8, 16, WIDTH), F32),
            pltpu.SemaphoreType.DMA((copies,)),
            pltpu.SemaphoreType.DMA((copies,)),
        ],
        compiler_params=pltpu.CompilerParams(
            collective_id=0, has_side_effects=True, vmem_limit_bytes=48 * 1024 * 1024
        ),
        cost_estimate=pl.CostEstimate(flops=4 * 10**9, bytes_accessed=12 * 10**6, transcendentals=262144),
        name="window_step",
    )(
        tokens.reshape(CELLS, WIDTH), cotangent.reshape(GROUPS, 512),
        gain_attn.reshape(1, WIDTH), gain_merge.reshape(1, 8 * WIDTH),
        w_qkv, w_proj, w_merge, leave, enter, back, home,
    )
    merged, d_tokens, d_gain_attn, d_qkv, d_proj, d_gain_merge, d_merge = outs
    return (
        merged.reshape(cotangent.shape), d_tokens.reshape(tokens.shape), d_gain_attn.reshape(WIDTH),
        d_qkv, d_proj, d_gain_merge.reshape(8 * WIDTH), d_merge,
    )


def solution(mesh):
    leave, enter = orderings()
    constants = [jnp.asarray(m, BF16) for m in (leave, enter, enter.T, leave.T)]
    box, whole = P("gx", "gy", "gz", None), P()
    return jax.shard_map(
        functools.partial(local, *constants),
        mesh=mesh,
        in_specs=(box, box, whole, whole, whole, whole, whole),
        out_specs=(box, box, whole, whole, whole, whole, whole),
        check_vma=False,
    )
```

```python
import functools

import jax
import jax.numpy as jnp
import numpy as np
from jax import lax
from jax.experimental import pallas as pl
from jax.experimental.pallas import tpu as pltpu
from jax.sharding import PartitionSpec as P

MESH = pl.DeviceIdType.MESH
HEADS = 8
WIDTH = 256
CELLS = 512
GROUPS = 64
ROWS = CELLS + 2 * GROUPS
FACTOR = 32 ** -0.5
EPSILON = 1e-05
TOKENS = 131072
TOKEN_SCALE = float(TOKENS) ** (-0.5)
MERGE_SCALE = float(TOKENS // 8) ** (-0.5)
BF16, F32 = jnp.bfloat16, jnp.float32

KINDS = [(a, b, c) for a in (0, 1) for b in (0, 1) for c in (0, 1)]


def kind_groups(kind):
    a, b, c = kind
    return [
        (i, j, k)
        for i in ([0] if a else [1])
        for j in ([0] if b else [1, 2, 3])
        for k in ([0] if c else list(range(1, 8)))
    ]


SIZES = [-(-10 * len(kind_groups(kind)) // 16) * 16 for kind in KINDS]
STARTS = [sum(SIZES[:i]) for i in range(8)]
HALO = sum(SIZES)


def orderings():
    leave, enter = np.zeros((HALO, ROWS), np.float32), np.zeros((ROWS, HALO), np.float32)
    for kind, start in zip(KINDS, STARTS):
        for at, (i, j, k) in enumerate(kind_groups(kind)):
            si, sj, sk = (i - 1) % 2, (j - 1) % 4, (k - 1) % 8
            window, place = (sj // 2) * 4 + sk // 2, si * 4 + (sj % 2) * 2 + sk % 2
            for o in range(8):
                cell = ((2 * i + o // 4) * 8 + 2 * j + o // 2 % 2) * 16 + 2 * k + o % 2
                leave[start + at * 10 + o, cell] = 1
                enter[window * 64 + o * 8 + place, start + at * 10 + o] = 1
            for t in range(2):
                leave[start + at * 10 + 8 + t, CELLS + t * GROUPS + (i * 4 + j) * 8 + k] = 1
                enter[CELLS + t * GROUPS + window * 8 + place, start + at * 10 + 8 + t] = 1
    return leave, enter


def dot(left, right, left_dim=1, right_dim=0):
    return lax.dot_general(
        left, right, (((left_dim,), (right_dim,)), ((), ())), preferred_element_type=F32
    )


def norm_parts(parts, count):
    average = sum(jnp.sum(p, axis=-1, keepdims=True) for p in parts) * (1.0 / count)
    centred = [p - average for p in parts]
    variance = sum(jnp.sum(p * p, axis=-1, keepdims=True) for p in centred) * (1.0 / count)
    return centred, lax.rsqrt(variance + EPSILON)


def norm_back(hats, grads, inverse, count):
    first = sum(jnp.sum(g, axis=-1, keepdims=True) for g in grads) * (1.0 / count)
    second = sum(jnp.sum(g * h, axis=-1, keepdims=True) for g, h in zip(grads, hats)) * (1.0 / count)
    return [inverse * (g - first - h * second) for g, h in zip(grads, hats)]


def kernel(
    tokens_hbm, cotangent_hbm, gain_attn_hbm, gain_merge_hbm, w_qkv_hbm, w_proj_hbm, w_merge_hbm,
    leave_hbm, enter_hbm, back_hbm, home_hbm,
    merged_out, d_tokens_out, d_gain_attn_out, d_qkv_out, d_proj_out, d_gain_merge_out, d_merge_out,
    cotangent, gain_attn, gain_merge, w_qkv, w_proj, w_merge, leave, enter, back, home, local_sem,
    stacked, halo_send, halo_recv, back_send, back_recv,
    flat, hat, normal, inverse_a, qkv, probs, attended, summed, d_summed, d_attended, d_qkv, heads,
    cot, nm, hat_m, m_nm, m_cot, m_acc1, m_in2, m_acc2, m_in3,
    q_sum, q_near, q_half, q_in1, q_acc1, q_in2, q_acc2, q_in3, q_out,
    g_sum, g_near, g_in1, g_in2, g_in3,
    send_sem, recv_sem,
):
    gx, gy, gz = lax.axis_index("gx"), lax.axis_index("gy"), lax.axis_index("gz")
    x, y_low, z = lax.div(gx, 2), lax.rem(gx, 2), gy
    y_high, core = lax.div(gz, 2), lax.rem(gz, 2)
    y = y_high * 2 + y_low

    def device(x_at, y_at, z_at, core_at):
        return (x_at * 2 + lax.rem(y_at, 2), z_at, lax.div(y_at, 2) * 2 + core_at)

    other_core = 1 - core

    def along(axis, step, core_at=core):
        if axis == "x":
            return device(lax.rem(x + step, 4), y, z, core_at)
        if axis == "y":
            return device(x, lax.rem(y + step, 4), z, core_at)
        return device(x, y, lax.rem(z + step, 8), core_at)

    partner = device(x, y, z, other_core)
    coordinate = {"x": x, "y": y, "z": z}

    def neighbour(kind, sign):
        a, b, c = kind
        return (
            lax.rem(gx + (8 + sign * a), 8),
            lax.rem(gy + (8 + sign * b), 8),
            lax.rem(gz + (4 + sign * c), 4),
        )

    started = []

    def send(source, target, to):
        at = len(started)
        copy = pltpu.make_async_remote_copy(
            src_ref=source, dst_ref=target, send_sem=send_sem.at[at], recv_sem=recv_sem.at[at],
            device_id=to, device_id_type=MESH,
        )
        copy.start()
        started.append(copy)
        return copy

    def arrive(copies):
        for copy in copies:
            copy.wait_recv()

    def rows(at, count):
        return pl.ds(pl.multiple_of(at * count, count), count)

    barrier = pltpu.get_barrier_semaphore()
    partners = [neighbour(kind, sign) for kind in KINDS[1:] for sign in (-1, 1)]
    partners += [partner]
    partners += [along(axis, step) for axis in "xy" for step in (1, 2, 3)]
    partners += [along(axis, step, other_core) for axis in "xy" for step in (1, 2, 3)]
    partners += [along("z", step) for step in range(1, 8)]
    for there in partners:
        pl.semaphore_signal(barrier, inc=1, device_id=there, device_id_type=MESH)

    loads = {}
    for at, (name, source, target) in enumerate((
        ("leave", leave_hbm, leave), ("tokens", tokens_hbm, stacked.at[pl.ds(0, CELLS)]),
        ("cotangent", cotangent_hbm, cotangent), ("gain_attn", gain_attn_hbm, gain_attn),
        ("gain_merge", gain_merge_hbm, gain_merge),
        ("enter", enter_hbm, enter), ("w_qkv", w_qkv_hbm, w_qkv),
        ("w_proj", w_proj_hbm, w_proj), ("w_merge", w_merge_hbm, w_merge),
        ("back", back_hbm, back), ("home", home_hbm, home),
    )):
        loads[name] = pltpu.make_async_copy(source, target, local_sem.at[at])
        loads[name].start()

    loads["cotangent"].wait()
    stacked[CELLS : CELLS + GROUPS, :] = cotangent[:, 0:WIDTH]
    stacked[CELLS + GROUPS :, :] = cotangent[:, WIDTH:]
    loads["tokens"].wait()
    loads["leave"].wait()
    halo_send[...] = dot(leave[...], stacked[...]).astype(BF16)

    pl.semaphore_wait(barrier, len(partners))
    halo = []
    for kind, start, size in list(zip(KINDS, STARTS, SIZES))[1:]:
        block = pl.ds(start, size)
        halo.append(send(halo_send.at[block], halo_recv.at[block], neighbour(kind, -1)))
    halo_recv[0 : SIZES[0], :] = halo_send[0 : SIZES[0], :]
    head_of_lane = lax.div(lax.broadcasted_iota(jnp.int32, (64, WIDTH), 1), 32)
    for h in range(HEADS):
        heads[h * 64 : (h + 1) * 64, :] = jnp.where(head_of_lane == h, 1.0, 0.0).astype(BF16)
    loads["enter"].wait()
    loads["w_qkv"].wait()
    loads["gain_attn"].wait()
    loads["gain_merge"].wait()
    arrive(halo)

    flat[...] = dot(enter[0:CELLS, :], halo_recv[...])
    for t in range(2):
        part = dot(enter[CELLS + t * GROUPS : CELLS + (t + 1) * GROUPS, :], halo_recv[...])
        cot[:, t * WIDTH : (t + 1) * WIDTH] = part.astype(BF16)
    members = [(step, flip) for step in range(4) for flip in (0, 1)]
    orders = (("x", "y"), ("y", "x"))
    m_cot[0, 0:GROUPS, :] = cot[...]
    m_cot[1, 0:GROUPS, :] = cot[...]
    m_cots = []
    for at, (step, flip) in list(enumerate(members))[1:]:
        for half in (0, 1):
            there = along(orders[half][0], step, (core, other_core)[flip])
            m_cots.append(send(cot, m_cot.at[half, pl.ds(at * GROUPS, GROUPS)], there))
    (centred,), inverse = norm_parts([flat[...]], WIDTH)
    inverse_a[...] = inverse
    hat[...] = centred * inverse
    normal[...] = (hat[...] * gain_attn[...]).astype(BF16)
    qkv[...] = dot(normal[...], w_qkv[...]).astype(BF16)

    def spread(block):
        return jnp.concatenate([block] * HEADS, axis=0) * heads[...]

    def gather(wide):
        total = wide[0:64]
        for h in range(1, HEADS):
            total = jnp.where(head_of_lane == h, wide[h * 64 : (h + 1) * 64], total)
        return total

    def forward(w, carry):
        here = rows(w, 64)
        query, key, value = (qkv[here, i * WIDTH : (i + 1) * WIDTH] for i in range(3))
        scores = dot(key, spread(query), 1, 1) * FACTOR
        powers = jnp.exp(scores - jnp.max(scores, axis=0, keepdims=True))
        weights = powers * (1.0 / jnp.sum(powers, axis=0, keepdims=True))
        probs[here, :] = weights
        attended[here, :] = gather(dot(weights.astype(BF16), value, 0, 0)).astype(BF16)
        return carry

    lax.fori_loop(0, 8, forward, 0)
    loads["w_proj"].wait()
    summed[...] = (flat[...] + dot(attended[...], w_proj[...])).astype(BF16).astype(F32)

    shaped = summed[...].reshape(8, 8, 8, WIDTH)
    slabs = [shaped[:, o].reshape(GROUPS, WIDTH) for o in range(8)]
    centred, inverse = norm_parts(slabs, 8 * WIDTH)
    for o in range(8):
        lanes = slice(o * WIDTH, (o + 1) * WIDTH)
        hat_m[:, lanes] = centred[o] * inverse
        nm[:, lanes] = (hat_m[:, lanes] * gain_merge[:, lanes]).astype(BF16)
    m_rows = []
    for at, (step, flip) in enumerate(members):
        for half in (0, 1):
            axis, core_at = orders[half][0], (core, other_core)[flip]
            block = rows(half * 8 + core_at * 4 + lax.rem(coordinate[axis] + step, 4), 128)
            if at == 0:
                m_nm[half, 0:GROUPS, :] = nm[:, block]
            else:
                target = m_nm.at[half, pl.ds(at * GROUPS, GROUPS)]
                m_rows.append(send(nm.at[:, block], target, along(axis, step, core_at)))
    loads["w_merge"].wait()
    result = dot(nm[...], w_merge[...]).astype(BF16)
    for t in range(2):
        stacked[CELLS + t * GROUPS : CELLS + (t + 1) * GROUPS, :] = result[:, t * WIDTH : (t + 1) * WIDTH]
    hats, grads = [], []
    for o in range(8):
        lanes = slice(o * WIDTH, (o + 1) * WIDTH)
        grad = dot(cot[...], w_merge[lanes, :], 1, 1)
        hats.append(hat_m[:, lanes])
        grads.append(grad * gain_merge[:, lanes])
        g_sum[o : o + 1, :] = jnp.sum(grad * hats[o], axis=0, keepdims=True)
    grads = norm_back(hats, grads, inverse, 8 * WIDTH)
    joined = jnp.stack([g.reshape(8, 8, WIDTH) for g in grads], axis=1).reshape(CELLS, WIDTH)
    d_summed[...] = joined.astype(BF16)

    q_sum[:, 3 * WIDTH :] = dot(attended[...], d_summed[...], 0, 0)
    d_attended[...] = dot(d_summed[...], w_proj[...], 1, 1).astype(BF16)

    def backward(w, carry):
        here = rows(w, 64)
        query, key, value = (qkv[here, i * WIDTH : (i + 1) * WIDTH] for i in range(3))
        weights = probs[here, :]
        wide = spread(d_attended[here, :])
        d_probs = dot(value, wide, 1, 1)
        d_value = dot(weights.astype(BF16), wide)
        inner = jnp.sum(d_probs * weights, axis=0, keepdims=True)
        d_scores = (weights * (d_probs - inner) * FACTOR).astype(BF16)
        d_key = dot(d_scores, spread(query))
        d_query = gather(dot(d_scores, key, 0, 0))
        d_qkv[here, 0:WIDTH] = d_query.astype(BF16)
        d_qkv[here, WIDTH : 2 * WIDTH] = d_key.astype(BF16)
        d_qkv[here, 2 * WIDTH :] = d_value.astype(BF16)
        return carry

    arrive(m_cots)
    arrive(m_rows)

    def m_second(half):
        second = orders[half][1]
        m_acc1[half] = dot(m_nm[half], m_cot[half], 0, 0)
        copies = []
        for step in (1, 2, 3):
            chunk = rows(lax.rem(coordinate[second] + step, 4), 32)
            copies.append(send(m_acc1.at[half, chunk], m_in2.at[half, step - 1], along(second, step)))
        return copies

    m_copies = [m_second(0), m_second(1)]
    lax.fori_loop(0, 8, backward, 0)

    def m_third(half):
        second = orders[half][1]
        arrive(m_copies[half])
        own = m_acc1[half, rows(coordinate[second], 32), :]
        m_acc2[half] = own + m_in2[half, 0] + m_in2[half, 1] + m_in2[half, 2]
        copies = []
        for step in range(1, 8):
            there = lax.rem(z + step, 8)
            chunk = m_acc2.at[half, rows(lax.div(there, 4), 16), rows(lax.rem(there, 4), 128)]
            copies.append(send(chunk, m_in3.at[half, step - 1], along("z", step)))
        return copies

    m_copies = [m_third(0), m_third(1)]

    q_sum[:, 0 : 3 * WIDTH] = dot(normal[...], d_qkv[...], 0, 0)
    q_chip = send(q_sum.at[:, rows(other_core, 512)], q_near, partner)
    d_normal = dot(d_qkv[...], w_qkv[...], 1, 1)
    g_sum[8:16, :] = jnp.zeros((8, WIDTH), F32)
    g_sum[8:9, :] = jnp.sum(d_normal * hat[...], axis=0, keepdims=True)
    g_chip = send(g_sum, g_near, partner)
    (d_flat,) = norm_back([hat[...]], [d_normal * gain_attn[...]], inverse_a[...], WIDTH)
    stacked[0:CELLS, :] = (d_summed[...].astype(F32) + d_flat).astype(BF16)
    loads["back"].wait()
    back_send[...] = dot(back[...], stacked[...]).astype(BF16)
    halo = []
    for kind, start, size in list(zip(KINDS, STARTS, SIZES))[1:]:
        block = pl.ds(start, size)
        halo.append(send(back_send.at[block], back_recv.at[block], neighbour(kind, 1)))
    back_recv[0 : SIZES[0], :] = back_send[0 : SIZES[0], :]

    def m_place(half, x_or_y_first, x_or_y_second):
        return half * 1024 + core * 512 + x_or_y_first * 128 + x_or_y_second * 32

    def m_fourth(half):
        first, second = orders[half]
        arrive(m_copies[half])
        high, lane = lax.div(z, 4), rows(lax.rem(z, 4), 128)
        total = m_acc2[half, rows(high, 16), lane]
        for step in range(7):
            total = total + m_in3[half, step]
        start = m_place(half, coordinate[first], coordinate[second]) + high * 16
        here = (pl.ds(pl.multiple_of(start, 16), 16), lane)
        d_merge_out[here] = (total * MERGE_SCALE).astype(BF16)
        place = d_merge_out.at[here]
        return [send(place, place, along("z", step)) for step in range(1, 8)]

    m_copies = [m_fourth(0), m_fourth(1)]

    q_chip.wait_recv()
    q_half[...] = q_sum[:, rows(core, 512)] + q_near[...]

    def q_first(half):
        axis = orders[half][0]
        copies = []
        for step in (1, 2, 3):
            chunk = half * 4 + lax.rem(coordinate[axis] + step, 4)
            copies.append(send(q_half.at[rows(chunk, 32)], q_in1.at[half, step - 1], along(axis, step)))
        return copies

    q_copies = [q_first(0), q_first(1)]
    g_chip.wait_recv()

    def g_start(total, into, axis, count):
        into[coordinate[axis]] = total
        mine = into.at[coordinate[axis]]
        return [send(mine, mine, along(axis, step)) for step in range(1, count)]

    def g_total(into, count):
        total = into[0]
        for i in range(1, count):
            total = total + into[i]
        return total

    g_copies = g_start(g_sum[...] + g_near[...], g_in1, "x", 4)

    def m_fifth(half):
        first, second = orders[half]
        arrive(m_copies[half])
        start = m_place(half, coordinate[first], coordinate[second])
        place = d_merge_out.at[pl.ds(pl.multiple_of(start, 32), 32)]
        return [send(place, place, along(second, step)) for step in (1, 2, 3)]

    m_copies = [m_fifth(0), m_fifth(1)]

    def q_second(half):
        first, second = orders[half]
        arrive(q_copies[half])
        own = q_half[rows(half * 4 + coordinate[first], 32), :]
        q_acc1[half] = own + q_in1[half, 0] + q_in1[half, 1] + q_in1[half, 2]
        copies = []
        for step in (1, 2, 3):
            lane = rows(lax.rem(coordinate[second] + step, 4), 128)
            copies.append(send(q_acc1.at[half, :, lane], q_in2.at[half, step - 1], along(second, step)))
        return copies

    q_copies = [q_second(0), q_second(1)]
    arrive(g_copies)
    g_copies = g_start(g_total(g_in1, 4), g_in2, "y", 4)

    def m_sixth(half):
        first = orders[half][0]
        arrive(m_copies[half])
        place = d_merge_out.at[rows(half * 8 + core * 4 + coordinate[first], 128)]
        last.append(send(place, place, partner))
        return [send(place, place, along(first, step)) for step in (1, 3, 2)]

    last = []
    m_copies = [m_sixth(0), m_sixth(1)]

    def q_third(half):
        second = orders[half][1]
        arrive(q_copies[half])
        own = q_acc1[half, :, rows(coordinate[second], 128)]
        q_acc2[half] = own + q_in2[half, 0] + q_in2[half, 1] + q_in2[half, 2]
        q_in3[half, z] = q_acc2[half]
        return [send(q_acc2.at[half], q_in3.at[half, z], along("z", step)) for step in range(1, 8)]

    q_copies = [q_third(0), q_third(1)]
    arrive(g_copies)
    g_copies = g_start(g_total(g_in2, 4), g_in3, "z", 8)

    loads["home"].wait()
    arrive(halo)
    placed = dot(home[...], back_recv[...]).astype(BF16)
    d_tokens_out[...] = placed[0:CELLS]
    merged_out[:, 0:WIDTH] = placed[CELLS : CELLS + GROUPS]
    merged_out[:, WIDTH:] = placed[CELLS + GROUPS :]

    def q_place(half, first_at):
        return half * 128 + first_at * 32

    def q_fifth(half):
        first, second = orders[half]
        arrive(q_copies[half])
        total = q_in3[half, 0]
        for i in range(1, 8):
            total = total + q_in3[half, i]
        start = pl.multiple_of(q_place(half, coordinate[first]), 32)
        here = (pl.ds(start, 32), rows(core * 4 + coordinate[second], 128))
        q_out[here] = (total * TOKEN_SCALE).astype(BF16)
        place = q_out.at[here]
        return [send(place, place, along(second, step)) for step in (1, 2, 3)]

    q_copies = [q_fifth(0), q_fifth(1)]
    for at, step in enumerate((1, 3, 2)):
        for half in (0, 1):
            arrive([m_copies[half][at]])
            came = lax.rem(coordinate[orders[half][0]] + 4 - step, 4)
            place = d_merge_out.at[rows(half * 8 + core * 4 + came, 128)]
            last.append(send(place, place, partner))

    def q_sixth(half):
        first = orders[half][0]
        arrive(q_copies[half])
        start = pl.multiple_of(q_place(half, coordinate[first]), 32)
        place = q_out.at[pl.ds(start, 32), rows(core, 512)]
        return [send(place, place, along(first, step)) for step in (1, 2, 3)]

    q_copies = [q_sixth(0), q_sixth(1)]
    arrive(g_copies)
    total = g_total(g_in3, 8)
    for o in range(8):
        d_gain_merge_out[:, o * WIDTH : (o + 1) * WIDTH] = total[o : o + 1] * MERGE_SCALE
    d_gain_attn_out[...] = total[8:9] * TOKEN_SCALE
    arrive(q_copies[0])
    arrive(q_copies[1])
    place = q_out.at[:, rows(core, 512)]
    last.append(send(place, place, partner))
    arrive(last)
    d_qkv_out[...] = q_out[:, 0 : 3 * WIDTH]
    d_proj_out[...] = q_out[:, 3 * WIDTH :]
    for copy in started:
        copy.wait_send()


def hand_out(*refs):
    given, outs, held, sems = refs[:7], refs[7:14], refs[14:21], refs[21]
    parts = [(i, None) for i in range(6)] + [(6, pl.ds(at * 512, 512)) for at in range(4)]
    both = []
    for at, (i, part) in enumerate(parts):
        source, stage, target = (r[i] if part is None else r[i].at[part] for r in (given, held, outs))
        both.append((
            pltpu.make_async_copy(source, stage, sems.at[0, at]),
            pltpu.make_async_copy(stage, target, sems.at[1, at]),
        ))
    for copy_in, _ in both[::-1]:
        copy_in.start()
    for copy_in, copy_out in both[::-1]:
        copy_in.wait()
        copy_out.start()
    for _, copy_out in both:
        copy_out.wait()


def local(leave, enter, back, home, tokens, cotangent, gain_attn, w_qkv, w_proj, gain_merge, w_merge):
    vmem, hbm = pl.BlockSpec(memory_space=pltpu.VMEM), pl.BlockSpec(memory_space=pltpu.HBM)
    copies = 200
    held = pl.pallas_call(
        kernel,
        out_shape=(
            jax.ShapeDtypeStruct((GROUPS, 512), BF16),
            jax.ShapeDtypeStruct((CELLS, WIDTH), BF16),
            jax.ShapeDtypeStruct((1, WIDTH), F32),
            jax.ShapeDtypeStruct((WIDTH, 3 * WIDTH), BF16),
            jax.ShapeDtypeStruct((WIDTH, WIDTH), BF16),
            jax.ShapeDtypeStruct((1, 8 * WIDTH), F32),
            jax.ShapeDtypeStruct((8 * WIDTH, 512), BF16),
        ),
        in_specs=[hbm] * 11,
        out_specs=[vmem] * 7,
        scratch_shapes=[
            pltpu.VMEM((GROUPS, 512), BF16),
            pltpu.VMEM((1, WIDTH), F32),
            pltpu.VMEM((1, 8 * WIDTH), F32),
            pltpu.VMEM((WIDTH, 3 * WIDTH), BF16),
            pltpu.VMEM((WIDTH, WIDTH), BF16),
            pltpu.VMEM((8 * WIDTH, 512), BF16),
            pltpu.VMEM((HALO, ROWS), BF16),
            pltpu.VMEM((ROWS, HALO), BF16),
            pltpu.VMEM((HALO, ROWS), BF16),
            pltpu.VMEM((ROWS, HALO), BF16),
            pltpu.SemaphoreType.DMA((11,)),
            pltpu.VMEM((ROWS, WIDTH), BF16),
            pltpu.VMEM((HALO, WIDTH), BF16),
            pltpu.VMEM((HALO, WIDTH), BF16),
            pltpu.VMEM((HALO, WIDTH), BF16),
            pltpu.VMEM((HALO, WIDTH), BF16),
            pltpu.VMEM((CELLS, WIDTH), F32),
            pltpu.VMEM((CELLS, WIDTH), F32),
            pltpu.VMEM((CELLS, WIDTH), BF16),
            pltpu.VMEM((CELLS, 1), F32),
            pltpu.VMEM((CELLS, 3 * WIDTH), BF16),
            pltpu.VMEM((CELLS, 512), F32),
            pltpu.VMEM((CELLS, WIDTH), BF16),
            pltpu.VMEM((CELLS, WIDTH), F32),
            pltpu.VMEM((CELLS, WIDTH), BF16),
            pltpu.VMEM((CELLS, WIDTH), BF16),
            pltpu.VMEM((CELLS, 3 * WIDTH), BF16),
            pltpu.VMEM((CELLS, WIDTH), BF16),
            pltpu.VMEM((GROUPS, 512), BF16),
            pltpu.VMEM((GROUPS, 8 * WIDTH), BF16),
            pltpu.VMEM((GROUPS, 8 * WIDTH), F32),
            pltpu.VMEM((2, 8 * GROUPS, 128), BF16),
            pltpu.VMEM((2, 8 * GROUPS, 512), BF16),
            pltpu.VMEM((2, 128, 512), F32),
            pltpu.VMEM((2, 3, 32, 512), F32),
            pltpu.VMEM((2, 32, 512), F32),
            pltpu.VMEM((2, 7, 16, 128), F32),
            pltpu.VMEM((WIDTH, 1024), F32),
            pltpu.VMEM((WIDTH, 512), F32),
            pltpu.VMEM((WIDTH, 512), F32),
            pltpu.VMEM((2, 3, 32, 512), F32),
            pltpu.VMEM((2, 32, 512), F32),
            pltpu.VMEM((2, 3, 32, 128), F32),
            pltpu.VMEM((2, 32, 128), F32),
            pltpu.VMEM((2, 8, 32, 128), F32),
            pltpu.VMEM((WIDTH, 1024), BF16),
            pltpu.VMEM((16, WIDTH), F32),
            pltpu.VMEM((16, WIDTH), F32),
            pltpu.VMEM((4, 16, WIDTH), F32),
            pltpu.VMEM((4, 16, WIDTH), F32),
            pltpu.VMEM((8, 16, WIDTH), F32),
            pltpu.SemaphoreType.DMA((copies,)),
            pltpu.SemaphoreType.DMA((copies,)),
        ],
        compiler_params=pltpu.CompilerParams(
            collective_id=0, has_side_effects=True, vmem_limit_bytes=60 * 1024 * 1024
        ),
        cost_estimate=pl.CostEstimate(flops=4 * 10**9, bytes_accessed=12 * 10**6, transcendentals=262144),
        name="window_step",
    )(
        tokens.reshape(CELLS, WIDTH), cotangent.reshape(GROUPS, 512),
        gain_attn.reshape(1, WIDTH), gain_merge.reshape(1, 8 * WIDTH),
        w_qkv, w_proj, w_merge, leave, enter, back, home,
    )
    outs = pl.pallas_call(
        hand_out,
        out_shape=[jax.ShapeDtypeStruct(h.shape, h.dtype) for h in held],
        in_specs=[pl.BlockSpec(memory_space=pl.ANY)] * 7,
        out_specs=[hbm] * 7,
        scratch_shapes=[pltpu.VMEM(h.shape, h.dtype) for h in held] + [pltpu.SemaphoreType.DMA((2, 10))],
        compiler_params=pltpu.CompilerParams(vmem_limit_bytes=60 * 1024 * 1024),
        name="hand_out",
    )(*held)
    merged, d_tokens, d_gain_attn, d_qkv, d_proj, d_gain_merge, d_merge = outs
    return (
        merged.reshape(cotangent.shape), d_tokens.reshape(tokens.shape), d_gain_attn.reshape(WIDTH),
        d_qkv, d_proj, d_gain_merge.reshape(8 * WIDTH), d_merge,
    )


def solution(mesh):
    leave, enter = orderings()
    constants = [jnp.asarray(m, BF16) for m in (leave, enter, enter.T, leave.T)]
    box, whole = P("gx", "gy", "gz", None), P()
    return jax.shard_map(
        functools.partial(local, *constants),
        mesh=mesh,
        in_specs=(box, box, whole, whole, whole, whole, whole),
        out_specs=(box, box, whole, whole, whole, whole, whole),
        check_vma=False,
    )
```

```python
import functools

import jax
import jax.numpy as jnp
import numpy as np
from jax import lax
from jax.experimental import pallas as pl
from jax.experimental.pallas import tpu as pltpu
from jax.sharding import PartitionSpec as P

MESH = pl.DeviceIdType.MESH
HEADS = 8
WIDTH = 256
CELLS = 512
GROUPS = 64
ROWS = CELLS + 2 * GROUPS
FACTOR = 32 ** -0.5
EPSILON = 1e-05
TOGETHER = 2
TOKENS = 131072
TOKEN_SCALE = float(TOKENS) ** (-0.5)
MERGE_SCALE = float(TOKENS // 8) ** (-0.5)
BF16, F32 = jnp.bfloat16, jnp.float32

KINDS = [(a, b, c) for a in (0, 1) for b in (0, 1) for c in (0, 1)]


def kind_groups(kind):
    a, b, c = kind
    return [
        (i, j, k)
        for i in ([0] if a else [1])
        for j in ([0] if b else [1, 2, 3])
        for k in ([0] if c else list(range(1, 8)))
    ]


SIZES = [-(-10 * len(kind_groups(kind)) // 16) * 16 for kind in KINDS]
STARTS = [sum(SIZES[:i]) for i in range(8)]
HALO = sum(SIZES)


def orderings():
    leave, enter = np.full(ROWS, -1, np.int32), np.full(HALO, -1, np.int32)
    back, home = np.full(ROWS, -1, np.int32), np.full(HALO, -1, np.int32)

    def pair(natural, place, windowed):
        leave[natural], enter[place] = place, windowed
        back[windowed], home[place] = place, natural

    for kind, start in zip(KINDS, STARTS):
        for at, (i, j, k) in enumerate(kind_groups(kind)):
            si, sj, sk = (i - 1) % 2, (j - 1) % 4, (k - 1) % 8
            window, place = (sj // 2) * 4 + sk // 2, si * 4 + (sj % 2) * 2 + sk % 2
            for o in range(8):
                cell = ((2 * i + o // 4) * 8 + 2 * j + o // 2 % 2) * 16 + 2 * k + o % 2
                pair(cell, start + at * 10 + o, window * 64 + o * 8 + place)
            for t in range(2):
                base = CELLS + t * GROUPS
                pair(base + (i * 4 + j) * 8 + k, start + at * 10 + 8 + t, base + window * 8 + place)
    return leave, enter, back, home


def one_hot(rows_of_columns, height):
    width = rows_of_columns.shape[1]
    ids = lax.broadcasted_iota(jnp.int32, (height, width), 0)
    return jnp.where(ids == rows_of_columns, 1.0, 0.0).astype(BF16)


def dot(left, right, left_dim=1, right_dim=0):
    return lax.dot_general(
        left, right, (((left_dim,), (right_dim,)), ((), ())), preferred_element_type=F32
    )


def norm_parts(parts, count):
    average = sum(jnp.sum(p, axis=-1, keepdims=True) for p in parts) * (1.0 / count)
    centred = [p - average for p in parts]
    variance = sum(jnp.sum(p * p, axis=-1, keepdims=True) for p in centred) * (1.0 / count)
    return centred, lax.rsqrt(variance + EPSILON)


def norm_back(hats, grads, inverse, count):
    first = sum(jnp.sum(g, axis=-1, keepdims=True) for g in grads) * (1.0 / count)
    second = sum(jnp.sum(g * h, axis=-1, keepdims=True) for g, h in zip(grads, hats)) * (1.0 / count)
    return [inverse * (g - first - h * second) for g, h in zip(grads, hats)]


def kernel(
    tokens_hbm, cotangent_hbm, gain_attn_hbm, gain_merge_hbm, w_qkv_hbm, w_proj_hbm, w_merge_hbm,
    leave_map, enter_map, back_map, home_map,
    merged_out, d_tokens_out, d_gain_attn_out, d_qkv_out, d_proj_out, d_gain_merge_out, d_merge_out,
    cotangent, gain_attn, gain_merge, w_qkv, w_proj, w_merge, leave, enter, back, home, local_sem,
    stacked, halo_send, halo_recv, back_send, back_recv,
    flat, hat, normal, inverse_a, qkv, probs, attended, summed, d_summed, d_attended, d_qkv, heads,
    cot, nm, hat_m, m_nm, m_cot, m_acc1, m_in2, m_acc2, m_in3,
    q_sum, q_near, q_half, q_in1, q_acc1, q_in2, q_in3, q_out,
    g_sum, g_near, g_in1, g_in2, g_in3,
    merged, d_tokens, d_gain_attn, d_gain_merge, d_merge, out_sem,
    send_sem, recv_sem,
):
    gx, gy, gz = lax.axis_index("gx"), lax.axis_index("gy"), lax.axis_index("gz")
    x, y_low, z = lax.div(gx, 2), lax.rem(gx, 2), gy
    y_high, core = lax.div(gz, 2), lax.rem(gz, 2)
    y = y_high * 2 + y_low

    def device(x_at, y_at, z_at, core_at):
        return (x_at * 2 + lax.rem(y_at, 2), z_at, lax.div(y_at, 2) * 2 + core_at)

    other_core = 1 - core

    def along(axis, step, core_at=core):
        if axis == "x":
            return device(lax.rem(x + step, 4), y, z, core_at)
        if axis == "y":
            return device(x, lax.rem(y + step, 4), z, core_at)
        return device(x, y, lax.rem(z + step, 8), core_at)

    partner = device(x, y, z, other_core)
    coordinate = {"x": x, "y": y, "z": z}

    def neighbour(kind, sign):
        a, b, c = kind
        return (
            lax.rem(gx + (8 + sign * a), 8),
            lax.rem(gy + (8 + sign * b), 8),
            lax.rem(gz + (4 + sign * c), 4),
        )

    started = []

    def send(source, target, to):
        at = len(started)
        copy = pltpu.make_async_remote_copy(
            src_ref=source, dst_ref=target, send_sem=send_sem.at[at], recv_sem=recv_sem.at[at],
            device_id=to, device_id_type=MESH,
        )
        copy.start()
        started.append(copy)
        return copy

    def arrive(copies):
        for copy in copies:
            copy.wait_recv()

    def rows(at, count):
        return pl.ds(pl.multiple_of(at * count, count), count)

    barrier = pltpu.get_barrier_semaphore()
    partners = [neighbour(kind, sign) for kind in KINDS[1:] for sign in (-1, 1)]
    partners += [partner]
    partners += [along(axis, step) for axis in "xy" for step in (1, 2, 3)]
    partners += [along(axis, step, other_core) for axis in "xy" for step in (1, 2, 3)]
    partners += [along("z", step) for step in range(1, 8)]
    for there in partners:
        pl.semaphore_signal(barrier, inc=1, device_id=there, device_id_type=MESH)

    loads = {}
    for at, (name, source, target) in enumerate((
        ("tokens", tokens_hbm, stacked.at[pl.ds(0, CELLS)]),
        ("cotangent", cotangent_hbm, cotangent), ("gain_attn", gain_attn_hbm, gain_attn),
        ("gain_merge", gain_merge_hbm, gain_merge),
        ("w_qkv", w_qkv_hbm, w_qkv),
        ("w_proj", w_proj_hbm, w_proj), ("w_merge", w_merge_hbm, w_merge),
    )):
        loads[name] = pltpu.make_async_copy(source, target, local_sem.at[at])
        loads[name].start()

    leave[...] = one_hot(leave_map[...], HALO)
    loads["cotangent"].wait()
    stacked[CELLS : CELLS + GROUPS, :] = cotangent[:, 0:WIDTH]
    stacked[CELLS + GROUPS :, :] = cotangent[:, WIDTH:]
    loads["tokens"].wait()
    halo_send[...] = dot(leave[...], stacked[...]).astype(BF16)

    pl.semaphore_wait(barrier, len(partners))
    halo = []
    for kind, start, size in list(zip(KINDS, STARTS, SIZES))[1:]:
        block = pl.ds(start, size)
        halo.append(send(halo_send.at[block], halo_recv.at[block], neighbour(kind, -1)))
    halo_recv[0 : SIZES[0], :] = halo_send[0 : SIZES[0], :]
    head_of_lane = lax.div(lax.broadcasted_iota(jnp.int32, (64, WIDTH), 1), 32)
    for h in range(HEADS):
        heads[h * 64 : (h + 1) * 64, :] = jnp.where(head_of_lane == h, 1.0, 0.0).astype(BF16)
    enter[...] = one_hot(enter_map[...], ROWS)
    loads["w_qkv"].wait()
    loads["gain_attn"].wait()
    loads["gain_merge"].wait()
    arrive(halo)

    flat[...] = dot(enter[0:CELLS, :], halo_recv[...])
    for t in range(2):
        part = dot(enter[CELLS + t * GROUPS : CELLS + (t + 1) * GROUPS, :], halo_recv[...])
        cot[:, t * WIDTH : (t + 1) * WIDTH] = part.astype(BF16)
    members = [(step, flip) for step in range(4) for flip in (0, 1)]
    orders = (("x", "y"), ("y", "x"))
    m_cot[0, 0:GROUPS, :] = cot[...]
    m_cot[1, 0:GROUPS, :] = cot[...]
    m_cots = []
    for at, (step, flip) in list(enumerate(members))[1:]:
        for half in (0, 1):
            there = along(orders[half][0], step, (core, other_core)[flip])
            m_cots.append(send(cot, m_cot.at[half, pl.ds(at * GROUPS, GROUPS)], there))
    (centred,), inverse = norm_parts([flat[...]], WIDTH)
    inverse_a[...] = inverse
    hat[...] = centred * inverse
    normal[...] = (hat[...] * gain_attn[...]).astype(BF16)
    qkv[...] = dot(normal[...], w_qkv[...]).astype(BF16)

    def spread(block):
        return jnp.concatenate([block] * HEADS, axis=0) * heads[...]

    def gather(wide):
        total = wide[0:64]
        for h in range(1, HEADS):
            total = jnp.where(head_of_lane == h, wide[h * 64 : (h + 1) * 64], total)
        return total

    def over_windows(body):
        def step(i, carry):
            for w in range(TOGETHER):
                body(rows(i * TOGETHER + w, 64))
            return carry

        lax.fori_loop(0, 8 // TOGETHER, step, 0)

    def forward(here):
        query, key, value = (qkv[here, i * WIDTH : (i + 1) * WIDTH] for i in range(3))
        scores = dot(key, spread(query), 1, 1) * FACTOR
        powers = jnp.exp(scores - jnp.max(scores, axis=0, keepdims=True))
        weights = powers * (1.0 / jnp.sum(powers, axis=0, keepdims=True))
        probs[here, :] = weights
        attended[here, :] = gather(dot(weights.astype(BF16), value, 0, 0)).astype(BF16)

    over_windows(forward)
    loads["w_proj"].wait()
    summed[...] = (flat[...] + dot(attended[...], w_proj[...])).astype(BF16).astype(F32)

    shaped = summed[...].reshape(8, 8, 8, WIDTH)
    slabs = [shaped[:, o].reshape(GROUPS, WIDTH) for o in range(8)]
    centred, inverse = norm_parts(slabs, 8 * WIDTH)
    for o in range(8):
        lanes = slice(o * WIDTH, (o + 1) * WIDTH)
        hat_m[:, lanes] = centred[o] * inverse
        nm[:, lanes] = (hat_m[:, lanes] * gain_merge[:, lanes]).astype(BF16)
    m_rows = []
    for at, (step, flip) in enumerate(members):
        for half in (0, 1):
            axis, core_at = orders[half][0], (core, other_core)[flip]
            block = rows(half * 8 + core_at * 4 + lax.rem(coordinate[axis] + step, 4), 128)
            if at == 0:
                m_nm[half, 0:GROUPS, :] = nm[:, block]
            else:
                target = m_nm.at[half, pl.ds(at * GROUPS, GROUPS)]
                m_rows.append(send(nm.at[:, block], target, along(axis, step, core_at)))
    loads["w_merge"].wait()
    result = dot(nm[...], w_merge[...]).astype(BF16)
    for t in range(2):
        stacked[CELLS + t * GROUPS : CELLS + (t + 1) * GROUPS, :] = result[:, t * WIDTH : (t + 1) * WIDTH]
    hats, grads = [], []
    for o in range(8):
        lanes = slice(o * WIDTH, (o + 1) * WIDTH)
        grad = dot(cot[...], w_merge[lanes, :], 1, 1)
        hats.append(hat_m[:, lanes])
        grads.append(grad * gain_merge[:, lanes])
        g_sum[o : o + 1, :] = jnp.sum(grad * hats[o], axis=0, keepdims=True)
    grads = norm_back(hats, grads, inverse, 8 * WIDTH)
    joined = jnp.stack([g.reshape(8, 8, WIDTH) for g in grads], axis=1).reshape(CELLS, WIDTH)
    d_summed[...] = joined.astype(BF16)

    q_sum[0, :, WIDTH:] = dot(attended[...], d_summed[...], 0, 0)
    d_attended[...] = dot(d_summed[...], w_proj[...], 1, 1).astype(BF16)

    def backward_value(here):
        wide = spread(d_attended[here, :])
        d_qkv[here, 2 * WIDTH :] = dot(probs[here, :].astype(BF16), wide).astype(BF16)

    over_windows(backward_value)
    q_sum[0, :, 0:WIDTH] = dot(normal[...], d_qkv[:, 2 * WIDTH :], 0, 0)

    def q_start(part):
        return send(q_sum.at[part, :, rows(other_core, WIDTH)], q_near.at[part], partner)

    q_chips = [q_start(0)]

    def backward(here):
        query, key, value = (qkv[here, i * WIDTH : (i + 1) * WIDTH] for i in range(3))
        weights = probs[here, :]
        wide = spread(d_attended[here, :])
        d_probs = dot(value, wide, 1, 1)
        inner = jnp.sum(d_probs * weights, axis=0, keepdims=True)
        d_scores = (weights * (d_probs - inner) * FACTOR).astype(BF16)
        d_key = dot(d_scores, spread(query))
        d_query = gather(dot(d_scores, key, 0, 0))
        d_qkv[here, 0:WIDTH] = d_query.astype(BF16)
        d_qkv[here, WIDTH : 2 * WIDTH] = d_key.astype(BF16)

    arrive(m_cots)
    arrive(m_rows)

    def m_second(half):
        second = orders[half][1]
        m_acc1[half] = dot(m_nm[half], m_cot[half], 0, 0)
        copies = []
        for step in (1, 2, 3):
            chunk = rows(lax.rem(coordinate[second] + step, 4), 32)
            copies.append(send(m_acc1.at[half, chunk], m_in2.at[half, step - 1], along(second, step)))
        return copies

    m_copies = [m_second(0), m_second(1)]

    def q_first(part):
        q_chips[part].wait_recv()
        q_half[part] = q_sum[part, :, rows(core, WIDTH)] + q_near[part]
        copies = []
        for half in (0, 1):
            axis = orders[half][0]
            for step in (1, 2, 3):
                chunk = rows(half * 4 + lax.rem(coordinate[axis] + step, 4), 32)
                target = q_in1.at[part, half, step - 1]
                copies.append(send(q_half.at[part, chunk], target, along(axis, step)))
        return copies

    def q_tile(at):
        return rows(lax.div(at, 2), 16), rows(lax.rem(at, 2), 128)

    def q_second(part, came):
        arrive(came)
        copies = []
        for half in (0, 1):
            first, second = orders[half]
            own = q_half[part, rows(half * 4 + coordinate[first], 32), :]
            q_acc1[part, half] = own + q_in1[part, half, 0] + q_in1[part, half, 1] + q_in1[part, half, 2]
            for step in (1, 2, 3):
                chunk = q_acc1.at[(part, half) + q_tile(lax.rem(coordinate[second] + step, 4))]
                copies.append(send(chunk, q_in2.at[part, half, step - 1], along(second, step)))
        return copies

    def q_third(part, came):
        arrive(came)
        for half in (0, 1):
            own = q_acc1[(part, half) + q_tile(coordinate[orders[half][1]])]
            total = own + q_in2[part, half, 0] + q_in2[part, half, 1] + q_in2[part, half, 2]
            q_in3[part, z, half * 16 : (half + 1) * 16, :] = total
        mine = q_in3.at[part, z]
        return [send(mine, mine, along("z", step)) for step in range(1, 8)]

    def q_lanes(part, at, count):
        return rows((1 - part) * (512 // count) + core * (WIDTH // count) + at, count)

    def q_fourth(part, came):
        arrive(came)
        total = q_in3[part, 0]
        for i in range(1, 8):
            total = total + q_in3[part, i]
        copies = []
        for half in (0, 1):
            first, second = orders[half]
            high, low = lax.div(coordinate[second], 2), lax.rem(coordinate[second], 2)
            here = (rows(half * 8 + coordinate[first] * 2 + high, 16), q_lanes(part, low, 128))
            q_out[here] = (total[half * 16 : (half + 1) * 16] * TOKEN_SCALE).astype(BF16)
            place = q_out.at[here]
            copies += [send(place, place, along(second, step)) for step in (1, 2, 3)]
        return copies

    def q_fifth(part, came):
        arrive(came)
        copies = []
        for half in (0, 1):
            first = orders[half][0]
            place = q_out.at[rows(half * 4 + coordinate[first], 32), q_lanes(part, 0, WIDTH)]
            copies += [send(place, place, along(first, step)) for step in (1, 2, 3)]
        return copies

    def q_sixth(part, came):
        arrive(came)
        place = q_out.at[:, q_lanes(part, 0, WIDTH)]
        return send(place, place, partner)

    last, handed = [], []

    def hand(source, target):
        copy = pltpu.make_async_copy(source, target, out_sem.at[len(handed)])
        copy.start()
        handed.append(copy)

    def m_third(half):
        second = orders[half][1]
        arrive(m_copies[half])
        own = m_acc1[half, rows(coordinate[second], 32), :]
        m_acc2[half] = own + m_in2[half, 0] + m_in2[half, 1] + m_in2[half, 2]
        copies = []
        for step in range(1, 8):
            there = lax.rem(z + step, 8)
            chunk = m_acc2.at[half, rows(lax.div(there, 4), 16), rows(lax.rem(there, 4), 128)]
            copies.append(send(chunk, m_in3.at[half, step - 1], along("z", step)))
        return copies

    def g_start(total, into, axis, count):
        into[coordinate[axis]] = total
        mine = into.at[coordinate[axis]]
        return [send(mine, mine, along(axis, step)) for step in range(1, count)]

    def g_total(into, count):
        total = into[0]
        for i in range(1, count):
            total = total + into[i]
        return total

    def m_place(half, x_or_y_first, x_or_y_second):
        return half * 1024 + core * 512 + x_or_y_first * 128 + x_or_y_second * 32

    def m_fourth(half):
        first, second = orders[half]
        arrive(m_copies[half])
        high, lane = lax.div(z, 4), rows(lax.rem(z, 4), 128)
        total = m_acc2[half, rows(high, 16), lane]
        for step in range(7):
            total = total + m_in3[half, step]
        start = m_place(half, coordinate[first], coordinate[second]) + high * 16
        here = (pl.ds(pl.multiple_of(start, 16), 16), lane)
        d_merge[here] = (total * MERGE_SCALE).astype(BF16)
        place = d_merge.at[here]
        return [send(place, place, along("z", step)) for step in range(1, 8)]

    def m_pass(half, came):
        mine, theirs = (rows(half * 8 + c * 4 + came, 128) for c in (core, other_core))
        place = d_merge.at[mine]
        last.append((send(place, place, partner), theirs))
        hand(place, d_merge_out.at[mine])

    def m_fifth(half):
        first, second = orders[half]
        arrive(m_copies[half])
        start = m_place(half, coordinate[first], coordinate[second])
        place = d_merge.at[pl.ds(pl.multiple_of(start, 32), 32)]
        return [send(place, place, along(second, step)) for step in (1, 3, 2)]

    def m_sixth(half):
        first = orders[half][0]
        arrive(m_copies[half])
        place = d_merge.at[rows(half * 8 + core * 4 + coordinate[first], 128)]
        copies = [send(place, place, along(first, step)) for step in (1, 3, 2)]
        m_pass(half, coordinate[first])
        return copies

    early = q_first(0)
    over_windows(backward)
    m_copies = [m_third(0), m_third(1)]
    q_sum[1] = dot(normal[...], d_qkv[:, 0 : 2 * WIDTH], 0, 0)
    q_chips.append(q_start(1))
    d_normal = dot(d_qkv[...], w_qkv[...], 1, 1)
    g_sum[8:16, :] = jnp.zeros((8, WIDTH), F32)
    g_sum[8:9, :] = jnp.sum(d_normal * hat[...], axis=0, keepdims=True)
    g_chip = send(g_sum, g_near, partner)
    late = q_first(1)
    (d_flat,) = norm_back([hat[...]], [d_normal * gain_attn[...]], inverse_a[...], WIDTH)
    stacked[0:CELLS, :] = (d_summed[...].astype(F32) + d_flat).astype(BF16)
    back[...] = one_hot(back_map[...], HALO)
    back_send[...] = dot(back[...], stacked[...]).astype(BF16)
    halo = []
    for kind, start, size in list(zip(KINDS, STARTS, SIZES))[1:]:
        block = pl.ds(start, size)
        halo.append(send(back_send.at[block], back_recv.at[block], neighbour(kind, 1)))
    back_recv[0 : SIZES[0], :] = back_send[0 : SIZES[0], :]
    early = q_second(0, early)
    g_chip.wait_recv()
    g_copies = g_start(g_sum[...] + g_near[...], g_in1, "x", 4)
    home[...] = one_hot(home_map[...], ROWS)

    m_copies = [m_fourth(0), m_fourth(1)]
    late = q_second(1, late)
    early = q_third(0, early)
    arrive(g_copies)
    g_copies = g_start(g_total(g_in1, 4), g_in2, "y", 4)

    arrive(halo)
    placed = dot(home[...], back_recv[...]).astype(BF16)
    d_tokens[...] = placed[0:CELLS]
    merged[:, 0:WIDTH] = placed[CELLS : CELLS + GROUPS]
    merged[:, WIDTH:] = placed[CELLS + GROUPS :]
    hand(d_tokens, d_tokens_out)
    hand(merged, merged_out)
    late = q_third(1, late)
    m_copies = [m_fifth(0), m_fifth(1)]
    arrive(g_copies)
    g_copies = g_start(g_total(g_in2, 4), g_in3, "z", 8)
    early = q_fourth(0, early)
    m_copies = [m_sixth(0), m_sixth(1)]
    late = q_fourth(1, late)
    early = q_fifth(0, early)
    arrive(g_copies)
    total = g_total(g_in3, 8)
    for o in range(8):
        d_gain_merge[:, o * WIDTH : (o + 1) * WIDTH] = total[o : o + 1] * MERGE_SCALE
    d_gain_attn[...] = total[8:9] * TOKEN_SCALE
    hand(d_gain_merge, d_gain_merge_out)
    hand(d_gain_attn, d_gain_attn_out)
    late = q_fifth(1, late)
    early = q_sixth(0, early)
    for at, step in enumerate((1, 3, 2)):
        for half in (0, 1):
            arrive([m_copies[half][at]])
            m_pass(half, lax.rem(coordinate[orders[half][0]] + 4 - step, 4))
    late = q_sixth(1, late)
    arrive([early])
    hand(q_out.at[:, pl.ds(2 * WIDTH, WIDTH)], d_qkv_out.at[:, pl.ds(2 * WIDTH, WIDTH)])
    hand(q_out.at[:, pl.ds(3 * WIDTH, WIDTH)], d_proj_out)
    for copy, theirs in last:
        arrive([copy])
        hand(d_merge.at[theirs], d_merge_out.at[theirs])
    arrive([late])
    hand(q_out.at[:, pl.ds(0, 2 * WIDTH)], d_qkv_out.at[:, pl.ds(0, 2 * WIDTH)])
    for copy in handed:
        copy.wait()
    for copy in started:
        copy.wait_send()


def hand_out(*refs):
    given, outs, held, sems = refs[:7], refs[7:14], refs[14:21], refs[21]
    parts = [(i, None) for i in range(6)] + [(6, pl.ds(at * 512, 512)) for at in range(4)]
    both = []
    for at, (i, part) in enumerate(parts):
        source, stage, target = (r[i] if part is None else r[i].at[part] for r in (given, held, outs))
        both.append((
            pltpu.make_async_copy(source, stage, sems.at[0, at]),
            pltpu.make_async_copy(stage, target, sems.at[1, at]),
        ))
    for copy_in, _ in both[::-1]:
        copy_in.start()
    for copy_in, copy_out in both[::-1]:
        copy_in.wait()
        copy_out.start()
    for _, copy_out in both:
        copy_out.wait()


def local(leave, enter, back, home, tokens, cotangent, gain_attn, w_qkv, w_proj, gain_merge, w_merge):
    vmem, hbm = pl.BlockSpec(memory_space=pltpu.VMEM), pl.BlockSpec(memory_space=pltpu.HBM)
    copies = 200
    held = pl.pallas_call(
        kernel,
        out_shape=(
            jax.ShapeDtypeStruct((GROUPS, 512), BF16),
            jax.ShapeDtypeStruct((CELLS, WIDTH), BF16),
            jax.ShapeDtypeStruct((1, WIDTH), F32),
            jax.ShapeDtypeStruct((WIDTH, 3 * WIDTH), BF16),
            jax.ShapeDtypeStruct((WIDTH, WIDTH), BF16),
            jax.ShapeDtypeStruct((1, 8 * WIDTH), F32),
            jax.ShapeDtypeStruct((8 * WIDTH, 512), BF16),
        ),
        in_specs=[hbm] * 7 + [vmem] * 4,
        out_specs=[hbm] * 7,
        scratch_shapes=[
            pltpu.VMEM((GROUPS, 512), BF16),
            pltpu.VMEM((1, WIDTH), F32),
            pltpu.VMEM((1, 8 * WIDTH), F32),
            pltpu.VMEM((WIDTH, 3 * WIDTH), BF16),
            pltpu.VMEM((WIDTH, WIDTH), BF16),
            pltpu.VMEM((8 * WIDTH, 512), BF16),
            pltpu.VMEM((HALO, ROWS), BF16),
            pltpu.VMEM((ROWS, HALO), BF16),
            pltpu.VMEM((HALO, ROWS), BF16),
            pltpu.VMEM((ROWS, HALO), BF16),
            pltpu.SemaphoreType.DMA((7,)),
            pltpu.VMEM((ROWS, WIDTH), BF16),
            pltpu.VMEM((HALO, WIDTH), BF16),
            pltpu.VMEM((HALO, WIDTH), BF16),
            pltpu.VMEM((HALO, WIDTH), BF16),
            pltpu.VMEM((HALO, WIDTH), BF16),
            pltpu.VMEM((CELLS, WIDTH), F32),
            pltpu.VMEM((CELLS, WIDTH), F32),
            pltpu.VMEM((CELLS, WIDTH), BF16),
            pltpu.VMEM((CELLS, 1), F32),
            pltpu.VMEM((CELLS, 3 * WIDTH), BF16),
            pltpu.VMEM((CELLS, 512), F32),
            pltpu.VMEM((CELLS, WIDTH), BF16),
            pltpu.VMEM((CELLS, WIDTH), F32),
            pltpu.VMEM((CELLS, WIDTH), BF16),
            pltpu.VMEM((CELLS, WIDTH), BF16),
            pltpu.VMEM((CELLS, 3 * WIDTH), BF16),
            pltpu.VMEM((CELLS, WIDTH), BF16),
            pltpu.VMEM((GROUPS, 512), BF16),
            pltpu.VMEM((GROUPS, 8 * WIDTH), BF16),
            pltpu.VMEM((GROUPS, 8 * WIDTH), F32),
            pltpu.VMEM((2, 8 * GROUPS, 128), BF16),
            pltpu.VMEM((2, 8 * GROUPS, 512), BF16),
            pltpu.VMEM((2, 128, 512), F32),
            pltpu.VMEM((2, 3, 32, 512), F32),
            pltpu.VMEM((2, 32, 512), F32),
            pltpu.VMEM((2, 7, 16, 128), F32),
            pltpu.VMEM((2, WIDTH, 512), F32),
            pltpu.VMEM((2, WIDTH, WIDTH), F32),
            pltpu.VMEM((2, WIDTH, WIDTH), F32),
            pltpu.VMEM((2, 2, 3, 32, WIDTH), F32),
            pltpu.VMEM((2, 2, 32, WIDTH), F32),
            pltpu.VMEM((2, 2, 3, 16, 128), F32),
            pltpu.VMEM((2, 8, 32, 128), F32),
            pltpu.VMEM((WIDTH, 1024), BF16),
            pltpu.VMEM((16, WIDTH), F32),
            pltpu.VMEM((16, WIDTH), F32),
            pltpu.VMEM((4, 16, WIDTH), F32),
            pltpu.VMEM((4, 16, WIDTH), F32),
            pltpu.VMEM((8, 16, WIDTH), F32),
            pltpu.VMEM((GROUPS, 512), BF16),
            pltpu.VMEM((CELLS, WIDTH), BF16),
            pltpu.VMEM((1, WIDTH), F32),
            pltpu.VMEM((1, 8 * WIDTH), F32),
            pltpu.VMEM((8 * WIDTH, 512), BF16),
            pltpu.SemaphoreType.DMA((32,)),
            pltpu.SemaphoreType.DMA((copies,)),
            pltpu.SemaphoreType.DMA((copies,)),
        ],
        compiler_params=pltpu.CompilerParams(
            collective_id=0, has_side_effects=True, vmem_limit_bytes=60 * 1024 * 1024
        ),
        cost_estimate=pl.CostEstimate(flops=4 * 10**9, bytes_accessed=12 * 10**6, transcendentals=262144),
        name="window_step",
    )(
        tokens.reshape(CELLS, WIDTH), cotangent.reshape(GROUPS, 512),
        gain_attn.reshape(1, WIDTH), gain_merge.reshape(1, 8 * WIDTH),
        w_qkv, w_proj, w_merge, leave, enter, back, home,
    )
    outs = pl.pallas_call(
        hand_out,
        out_shape=[jax.ShapeDtypeStruct(h.shape, h.dtype) for h in held],
        in_specs=[pl.BlockSpec(memory_space=pl.ANY)] * 7,
        out_specs=[hbm] * 7,
        scratch_shapes=[pltpu.VMEM(h.shape, h.dtype) for h in held] + [pltpu.SemaphoreType.DMA((2, 10))],
        compiler_params=pltpu.CompilerParams(vmem_limit_bytes=60 * 1024 * 1024),
        name="hand_out",
    )(*held)
    merged, d_tokens, d_gain_attn, d_qkv, d_proj, d_gain_merge, d_merge = outs
    return (
        merged.reshape(cotangent.shape), d_tokens.reshape(tokens.shape), d_gain_attn.reshape(WIDTH),
        d_qkv, d_proj, d_gain_merge.reshape(8 * WIDTH), d_merge,
    )


def solution(mesh):
    constants = [jnp.asarray(m).reshape(1, -1) for m in orderings()]
    box, whole = P("gx", "gy", "gz", None), P()
    return jax.shard_map(
        functools.partial(local, *constants),
        mesh=mesh,
        in_specs=(box, box, whole, whole, whole, whole, whole),
        out_specs=(box, box, whole, whole, whole, whole, whole),
        check_vma=False,
    )
```

```python
import functools

import jax
import jax.numpy as jnp
import numpy as np
from jax import lax
from jax.experimental import pallas as pl
from jax.experimental.pallas import tpu as pltpu
from jax.sharding import PartitionSpec as P

MESH = pl.DeviceIdType.MESH
HEADS = 8
WIDTH = 256
CELLS = 512
GROUPS = 64
ROWS = CELLS + 2 * GROUPS
FACTOR = 32 ** -0.5
EPSILON = 1e-05
TOGETHER = 8
COPIES = 171
SENDING = 64
TOKENS = 131072
TOKEN_SCALE = float(TOKENS) ** (-0.5)
MERGE_SCALE = float(TOKENS // 8) ** (-0.5)
BF16, F32 = jnp.bfloat16, jnp.float32

KINDS = [(a, b, c) for a in (0, 1) for b in (0, 1) for c in (0, 1)]


def kind_groups(kind):
    a, b, c = kind
    return [
        (i, j, k)
        for i in ([0] if a else [1])
        for j in ([0] if b else [1, 2, 3])
        for k in ([0] if c else list(range(1, 8)))
    ]


SIZES = [-(-10 * len(kind_groups(kind)) // 16) * 16 for kind in KINDS]
STARTS = [sum(SIZES[:i]) for i in range(8)]
HALO = sum(SIZES)


def orderings():
    leave, enter = np.full(ROWS, -1, np.int32), np.full(HALO, -1, np.int32)
    back, home = np.full(ROWS, -1, np.int32), np.full(HALO, -1, np.int32)

    def pair(natural, place, windowed):
        leave[natural], enter[place] = place, windowed
        back[windowed], home[place] = place, natural

    for kind, start in zip(KINDS, STARTS):
        for at, (i, j, k) in enumerate(kind_groups(kind)):
            si, sj, sk = (i - 1) % 2, (j - 1) % 4, (k - 1) % 8
            window, place = (sj // 2) * 4 + sk // 2, si * 4 + (sj % 2) * 2 + sk % 2
            for o in range(8):
                cell = ((2 * i + o // 4) * 8 + 2 * j + o // 2 % 2) * 16 + 2 * k + o % 2
                pair(cell, start + at * 10 + o, window * 64 + o * 8 + place)
            for t in range(2):
                base = CELLS + t * GROUPS
                pair(base + (i * 4 + j) * 8 + k, start + at * 10 + 8 + t, base + window * 8 + place)
    return leave, enter, back, home


def one_hot(rows_of_columns, height):
    width = rows_of_columns.shape[1]
    ids = lax.broadcasted_iota(jnp.int32, (height, width), 0)
    return jnp.where(ids == rows_of_columns, 1.0, 0.0).astype(BF16)


def dot(left, right, left_dim=1, right_dim=0):
    return lax.dot_general(
        left, right, (((left_dim,), (right_dim,)), ((), ())), preferred_element_type=F32
    )


def norm_parts(parts, count):
    average = sum(jnp.sum(p, axis=-1, keepdims=True) for p in parts) * (1.0 / count)
    centred = [p - average for p in parts]
    variance = sum(jnp.sum(p * p, axis=-1, keepdims=True) for p in centred) * (1.0 / count)
    return centred, lax.rsqrt(variance + EPSILON)


def norm_back(hats, grads, inverse, count):
    first = sum(jnp.sum(g, axis=-1, keepdims=True) for g in grads) * (1.0 / count)
    second = sum(jnp.sum(g * h, axis=-1, keepdims=True) for g, h in zip(grads, hats)) * (1.0 / count)
    return [inverse * (g - first - h * second) for g, h in zip(grads, hats)]


def kernel(
    tokens_hbm, cotangent_hbm, gain_attn_hbm, gain_merge_hbm, w_qkv_hbm, w_proj_hbm, w_merge_hbm,
    leave_map, enter_map, back_map, home_map,
    merged_out, d_tokens_out, d_gain_attn_out, d_qkv_out, d_proj_out, d_gain_merge_out, d_merge_out,
    cotangent, gain_attn, gain_merge, w_qkv, w_proj, w_merge, leave, enter, back, home, local_sem,
    stacked, halo_send, halo_recv, back_send, back_recv,
    flat, hat, normal, inverse_a, qkv, probs, attended, summed, d_summed, d_attended, d_qkv, heads,
    cot, nm, hat_m, m_nm, m_cot, m_acc1, m_in2, m_acc2, m_in3,
    q_sum, q_near, q_half, q_in1, q_acc1, q_in2, q_in3, q_out,
    g_sum, g_near, g_in1, g_in2, g_in3, g_all,
    merged, d_tokens, d_gain_attn, d_gain_merge, d_merge, out_sem,
    send_sem, recv_sem,
):
    gx, gy, gz = lax.axis_index("gx"), lax.axis_index("gy"), lax.axis_index("gz")
    x, y_low, z = lax.div(gx, 2), lax.rem(gx, 2), gy
    y_high, core = lax.div(gz, 2), lax.rem(gz, 2)
    y = y_high * 2 + y_low

    def device(x_at, y_at, z_at, core_at):
        return (x_at * 2 + lax.rem(y_at, 2), z_at, lax.div(y_at, 2) * 2 + core_at)

    other_core = 1 - core

    def along(axis, step, core_at=core):
        if axis == "x":
            return device(lax.rem(x + step, 4), y, z, core_at)
        if axis == "y":
            return device(x, lax.rem(y + step, 4), z, core_at)
        return device(x, y, lax.rem(z + step, 8), core_at)

    partner = device(x, y, z, other_core)
    coordinate = {"x": x, "y": y, "z": z}

    def neighbour(kind, sign):
        a, b, c = kind
        return (
            lax.rem(gx + (8 + sign * a), 8),
            lax.rem(gy + (8 + sign * b), 8),
            lax.rem(gz + (4 + sign * c), 4),
        )

    started = []

    def send(source, target, to):
        at = len(started)
        if at >= SENDING:
            started[at - SENDING].wait_send()
        copy = pltpu.make_async_remote_copy(
            src_ref=source, dst_ref=target, send_sem=send_sem.at[at % SENDING], recv_sem=recv_sem.at[at],
            device_id=to, device_id_type=MESH,
        )
        copy.start()
        started.append(copy)
        return copy

    def arrive(copies):
        for copy in copies:
            copy.wait_recv()

    def rows(at, count):
        return pl.ds(pl.multiple_of(at * count, count), count)

    barrier = pltpu.get_barrier_semaphore()
    partners = [neighbour(kind, sign) for kind in KINDS[1:] for sign in (-1, 1)]
    partners += [along(axis, step) for axis in "xy" for step in (1, 2, 3)]
    partners += [along(axis, step, other_core) for axis in "xy" for step in (1, 2, 3)]
    partners += [along("z", step) for step in range(2, 7)]
    for there in partners:
        pl.semaphore_signal(barrier, inc=1, device_id=there, device_id_type=MESH)

    loads = {}
    for at, (name, source, target) in enumerate((
        ("tokens", tokens_hbm, stacked.at[pl.ds(0, CELLS)]),
        ("cotangent", cotangent_hbm, cotangent), ("gain_attn", gain_attn_hbm, gain_attn),
        ("gain_merge", gain_merge_hbm, gain_merge),
        ("w_qkv", w_qkv_hbm, w_qkv),
        ("w_proj", w_proj_hbm, w_proj), ("w_merge", w_merge_hbm, w_merge),
    )):
        loads[name] = pltpu.make_async_copy(source, target, local_sem.at[at])
        loads[name].start()

    leave[...] = one_hot(leave_map[...], HALO)
    loads["cotangent"].wait()
    stacked[CELLS : CELLS + GROUPS, :] = cotangent[:, 0:WIDTH]
    stacked[CELLS + GROUPS :, :] = cotangent[:, WIDTH:]
    loads["tokens"].wait()
    halo_send[...] = dot(leave[...], stacked[...]).astype(BF16)

    pl.semaphore_wait(barrier, len(partners))
    halo = []
    for kind, start, size in list(zip(KINDS, STARTS, SIZES))[1:]:
        block = pl.ds(start, size)
        halo.append(send(halo_send.at[block], halo_recv.at[block], neighbour(kind, -1)))
    halo_recv[0 : SIZES[0], :] = halo_send[0 : SIZES[0], :]
    head_of_lane = lax.div(lax.broadcasted_iota(jnp.int32, (64, WIDTH), 1), 32)
    for h in range(HEADS):
        heads[h * 64 : (h + 1) * 64, :] = jnp.where(head_of_lane == h, 1.0, 0.0).astype(BF16)
    enter[...] = one_hot(enter_map[...], ROWS)
    loads["w_qkv"].wait()
    loads["gain_attn"].wait()
    loads["gain_merge"].wait()
    arrive(halo)

    flat[...] = dot(enter[0:CELLS, :], halo_recv[...])
    for t in range(2):
        part = dot(enter[CELLS + t * GROUPS : CELLS + (t + 1) * GROUPS, :], halo_recv[...])
        cot[:, t * WIDTH : (t + 1) * WIDTH] = part.astype(BF16)
    members = [(step, flip) for flip in (0, 1) for step in range(4)]
    orders = (("x", "y"), ("y", "x"))
    m_cot[0, 0:GROUPS, :] = cot[...]
    m_cot[1, 0:GROUPS, :] = cot[...]
    m_cots = []
    for step in (1, 2, 3):
        for half in (0, 1):
            target = m_cot.at[half, pl.ds(step * GROUPS, GROUPS)]
            m_cots.append(send(cot, target, along(orders[half][0], step)))
    (centred,), inverse = norm_parts([flat[...]], WIDTH)
    inverse_a[...] = inverse
    hat[...] = centred * inverse
    normal[...] = (hat[...] * gain_attn[...]).astype(BF16)
    qkv[...] = dot(normal[...], w_qkv[...]).astype(BF16)

    def spread(block):
        return jnp.concatenate([block] * HEADS, axis=0) * heads[...]

    def gather(wide):
        total = wide[0:64]
        for h in range(1, HEADS):
            total = jnp.where(head_of_lane == h, wide[h * 64 : (h + 1) * 64], total)
        return total

    def over_windows(body):
        def step(i, carry):
            for w in range(TOGETHER):
                body(rows(i * TOGETHER + w, 64))
            return carry

        lax.fori_loop(0, 8 // TOGETHER, step, 0)

    def forward(here):
        query, key, value = (qkv[here, i * WIDTH : (i + 1) * WIDTH] for i in range(3))
        scores = dot(key, spread(query), 1, 1) * FACTOR
        powers = jnp.exp(scores - jnp.max(scores, axis=0, keepdims=True))
        weights = powers * (1.0 / jnp.sum(powers, axis=0, keepdims=True))
        probs[here, :] = weights
        attended[here, :] = gather(dot(weights.astype(BF16), value, 0, 0)).astype(BF16)

    over_windows(forward)
    loads["w_proj"].wait()
    summed[...] = (flat[...] + dot(attended[...], w_proj[...])).astype(BF16).astype(F32)

    shaped = summed[...].reshape(8, 8, 8, WIDTH)
    slabs = [shaped[:, o].reshape(GROUPS, WIDTH) for o in range(8)]
    centred, inverse = norm_parts(slabs, 8 * WIDTH)
    for o in range(8):
        lanes = slice(o * WIDTH, (o + 1) * WIDTH)
        hat_m[:, lanes] = centred[o] * inverse
        nm[:, lanes] = (hat_m[:, lanes] * gain_merge[:, lanes]).astype(BF16)
    m_rows = []
    for at, (step, flip) in enumerate(members):
        for half in (0, 1):
            axis, core_at = orders[half][0], (core, other_core)[flip]
            block = rows(half * 8 + core_at * 4 + lax.rem(coordinate[axis] + step, 4), 128)
            if at == 0:
                m_nm[half, 0:GROUPS, :] = nm[:, block]
            else:
                target = m_nm.at[half, pl.ds(at * GROUPS, GROUPS)]
                m_rows.append(send(nm.at[:, block], target, along(axis, step, core_at)))
    loads["w_merge"].wait()
    result = dot(nm[...], w_merge[...]).astype(BF16)
    for t in range(2):
        stacked[CELLS + t * GROUPS : CELLS + (t + 1) * GROUPS, :] = result[:, t * WIDTH : (t + 1) * WIDTH]
    hats, grads = [], []
    for o in range(8):
        lanes = slice(o * WIDTH, (o + 1) * WIDTH)
        grad = dot(cot[...], w_merge[lanes, :], 1, 1)
        hats.append(hat_m[:, lanes])
        grads.append(grad * gain_merge[:, lanes])
        g_sum[o : o + 1, :] = jnp.sum(grad * hats[o], axis=0, keepdims=True)
    grads = norm_back(hats, grads, inverse, 8 * WIDTH)
    joined = jnp.stack([g.reshape(8, 8, WIDTH) for g in grads], axis=1).reshape(CELLS, WIDTH)
    d_summed[...] = joined.astype(BF16)

    arrive(m_cots)
    m_pairs = []
    for half in (0, 1):
        source = m_cot.at[half, pl.ds(0, 4 * GROUPS)]
        m_pairs.append(send(source, m_cot.at[half, pl.ds(4 * GROUPS, 4 * GROUPS)], partner))

    q_sum[0, :, WIDTH:] = dot(attended[...], d_summed[...], 0, 0)
    d_attended[...] = dot(d_summed[...], w_proj[...], 1, 1).astype(BF16)

    def backward_value(here):
        wide = spread(d_attended[here, :])
        d_qkv[here, 2 * WIDTH :] = dot(probs[here, :].astype(BF16), wide).astype(BF16)

    over_windows(backward_value)
    q_sum[0, :, 0:WIDTH] = dot(normal[...], d_qkv[:, 2 * WIDTH :], 0, 0)

    def q_start(part):
        return send(q_sum.at[part, :, rows(other_core, WIDTH)], q_near.at[part], partner)

    q_chips = [q_start(0)]

    def backward(here):
        query, key, value = (qkv[here, i * WIDTH : (i + 1) * WIDTH] for i in range(3))
        weights = probs[here, :]
        wide = spread(d_attended[here, :])
        d_probs = dot(value, wide, 1, 1)
        inner = jnp.sum(d_probs * weights, axis=0, keepdims=True)
        d_scores = (weights * (d_probs - inner) * FACTOR).astype(BF16)
        d_key = dot(d_scores, spread(query))
        d_query = gather(dot(d_scores, key, 0, 0))
        d_qkv[here, 0:WIDTH] = d_query.astype(BF16)
        d_qkv[here, WIDTH : 2 * WIDTH] = d_key.astype(BF16)

    arrive(m_pairs)
    arrive(m_rows)

    def m_second(half):
        second = orders[half][1]
        m_acc1[half] = dot(m_nm[half], m_cot[half], 0, 0)
        copies = []
        for step in (1, 2, 3):
            chunk = rows(lax.rem(coordinate[second] + step, 4), 32)
            copies.append(send(m_acc1.at[half, chunk], m_in2.at[half, step - 1], along(second, step)))
        return copies

    m_copies = [m_second(0), m_second(1)]

    def q_first(part):
        q_chips[part].wait_recv()
        q_half[part] = q_sum[part, :, rows(core, WIDTH)] + q_near[part]
        copies = []
        for half in (0, 1):
            axis = orders[half][0]
            for step in (1, 2, 3):
                chunk = rows(half * 4 + lax.rem(coordinate[axis] + step, 4), 32)
                target = q_in1.at[part, half, step - 1]
                copies.append(send(q_half.at[part, chunk], target, along(axis, step)))
        return copies

    def q_tile(at):
        return rows(lax.div(at, 2), 16), rows(lax.rem(at, 2), 128)

    def q_second(part, came):
        arrive(came)
        copies = []
        for half in (0, 1):
            first, second = orders[half]
            own = q_half[part, rows(half * 4 + coordinate[first], 32), :]
            q_acc1[part, half] = own + q_in1[part, half, 0] + q_in1[part, half, 1] + q_in1[part, half, 2]
            for step in (1, 2, 3):
                chunk = q_acc1.at[(part, half) + q_tile(lax.rem(coordinate[second] + step, 4))]
                copies.append(send(chunk, q_in2.at[part, half, step - 1], along(second, step)))
        return copies

    def q_third(part, came):
        arrive(came)
        for half in (0, 1):
            own = q_acc1[(part, half) + q_tile(coordinate[orders[half][1]])]
            total = own + q_in2[part, half, 0] + q_in2[part, half, 1] + q_in2[part, half, 2]
            q_in3[part, z, half * 16 : (half + 1) * 16, :] = total
        mine = q_in3.at[part, z]
        return [send(mine, mine, along("z", step)) for step in range(1, 8)]

    def q_lanes(part, at, count):
        return rows((1 - part) * (512 // count) + core * (WIDTH // count) + at, count)

    def q_fourth(part, came):
        arrive(came)
        total = q_in3[part, 0]
        for i in range(1, 8):
            total = total + q_in3[part, i]
        copies = []
        for half in (0, 1):
            first, second = orders[half]
            high, low = lax.div(coordinate[second], 2), lax.rem(coordinate[second], 2)
            here = (rows(half * 8 + coordinate[first] * 2 + high, 16), q_lanes(part, low, 128))
            q_out[here] = (total[half * 16 : (half + 1) * 16] * TOKEN_SCALE).astype(BF16)
            place = q_out.at[here]
            copies += [send(place, place, along(second, step)) for step in (1, 2, 3)]
        return copies

    def q_fifth(part, came):
        arrive(came)
        copies = []
        for half in (0, 1):
            first = orders[half][0]
            place = q_out.at[rows(half * 4 + coordinate[first], 32), q_lanes(part, 0, WIDTH)]
            copies += [send(place, place, along(first, step)) for step in (1, 2, 3)]
        return copies

    def q_sixth(part, came):
        arrive(came)
        place = q_out.at[:, q_lanes(part, 0, WIDTH)]
        return send(place, place, partner)

    last, handed = [], []

    def hand(source, target):
        copy = pltpu.make_async_copy(source, target, out_sem.at[len(handed)])
        copy.start()
        handed.append(copy)

    def m_third(half):
        second = orders[half][1]
        arrive(m_copies[half])
        own = m_acc1[half, rows(coordinate[second], 32), :]
        m_acc2[half] = own + m_in2[half, 0] + m_in2[half, 1] + m_in2[half, 2]
        copies = []
        for step in range(1, 8):
            there = lax.rem(z + step, 8)
            chunk = m_acc2.at[half, rows(lax.div(there, 4), 16), rows(lax.rem(there, 4), 128)]
            copies.append(send(chunk, m_in3.at[half, step - 1], along("z", step)))
        return copies

    def g_start(total, into, axis, count):
        into[coordinate[axis]] = total
        mine = into.at[coordinate[axis]]
        return [send(mine, mine, along(axis, step)) for step in range(1, count)]

    def g_total(into, count):
        total = into[0]
        for i in range(1, count):
            total = total + into[i]
        return total

    def m_place(half, x_or_y_first, x_or_y_second):
        return half * 1024 + core * 512 + x_or_y_first * 128 + x_or_y_second * 32

    def m_fourth(half):
        first, second = orders[half]
        arrive(m_copies[half])
        high, lane = lax.div(z, 4), rows(lax.rem(z, 4), 128)
        total = m_acc2[half, rows(high, 16), lane]
        for step in range(7):
            total = total + m_in3[half, step]
        start = m_place(half, coordinate[first], coordinate[second]) + high * 16
        here = (pl.ds(pl.multiple_of(start, 16), 16), lane)
        d_merge[here] = (total * MERGE_SCALE).astype(BF16)
        place = d_merge.at[here]
        return [send(place, place, along("z", step)) for step in range(1, 8)]

    def m_pass(half, came):
        mine, theirs = (rows(half * 8 + c * 4 + came, 128) for c in (core, other_core))
        place = d_merge.at[mine]
        last.append((send(place, place, partner), theirs))
        hand(place, d_merge_out.at[mine])

    def m_fifth(half):
        first, second = orders[half]
        arrive(m_copies[half])
        start = m_place(half, coordinate[first], coordinate[second])
        place = d_merge.at[pl.ds(pl.multiple_of(start, 32), 32)]
        return [send(place, place, along(second, step)) for step in (1, 3, 2)]

    def m_sixth(half):
        first = orders[half][0]
        arrive(m_copies[half])
        place = d_merge.at[rows(half * 8 + core * 4 + coordinate[first], 128)]
        copies = [send(place, place, along(first, step)) for step in (1, 3, 2)]
        m_pass(half, coordinate[first])
        return copies

    early = q_first(0)
    over_windows(backward)
    q_sum[1] = dot(normal[...], d_qkv[:, 0 : 2 * WIDTH], 0, 0)
    q_chips.append(q_start(1))
    d_normal = dot(d_qkv[...], w_qkv[...], 1, 1)
    g_sum[8:16, :] = jnp.zeros((8, WIDTH), F32)
    g_sum[8:9, :] = jnp.sum(d_normal * hat[...], axis=0, keepdims=True)
    g_chip = send(g_sum.at[:, rows(other_core, 128)], g_near, partner)
    late = q_first(1)
    (d_flat,) = norm_back([hat[...]], [d_normal * gain_attn[...]], inverse_a[...], WIDTH)
    stacked[0:CELLS, :] = (d_summed[...].astype(F32) + d_flat).astype(BF16)
    back[...] = one_hot(back_map[...], HALO)
    back_send[...] = dot(back[...], stacked[...]).astype(BF16)
    halo = []
    for kind, start, size in list(zip(KINDS, STARTS, SIZES))[1:]:
        block = pl.ds(start, size)
        halo.append(send(back_send.at[block], back_recv.at[block], neighbour(kind, 1)))
    back_recv[0 : SIZES[0], :] = back_send[0 : SIZES[0], :]
    early = q_second(0, early)
    m_copies = [m_third(0), m_third(1)]
    g_chip.wait_recv()
    g_copies = g_start(g_sum[:, rows(core, 128)] + g_near[...], g_in1, "x", 4)
    home[...] = one_hot(home_map[...], ROWS)

    m_copies = [m_fourth(0), m_fourth(1)]
    late = q_second(1, late)
    early = q_third(0, early)
    arrive(g_copies)
    g_copies = g_start(g_total(g_in1, 4), g_in2, "y", 4)

    arrive(halo)
    placed = dot(home[...], back_recv[...]).astype(BF16)
    d_tokens[...] = placed[0:CELLS]
    merged[:, 0:WIDTH] = placed[CELLS : CELLS + GROUPS]
    merged[:, WIDTH:] = placed[CELLS + GROUPS :]
    hand(d_tokens, d_tokens_out)
    hand(merged, merged_out)
    late = q_third(1, late)
    m_copies = [m_fifth(0), m_fifth(1)]
    arrive(g_copies)
    g_copies = g_start(g_total(g_in2, 4), g_in3, "z", 8)
    early = q_fourth(0, early)
    m_copies = [m_sixth(0), m_sixth(1)]
    late = q_fourth(1, late)
    early = q_fifth(0, early)
    arrive(g_copies)
    g_all[:, rows(core, 128)] = g_total(g_in3, 8)
    g_mine = g_all.at[:, rows(core, 128)]
    g_last = send(g_mine, g_mine, partner)
    late = q_fifth(1, late)
    early = q_sixth(0, early)
    g_last.wait_recv()
    total = g_all[...]
    for o in range(8):
        d_gain_merge[:, o * WIDTH : (o + 1) * WIDTH] = total[o : o + 1] * MERGE_SCALE
    d_gain_attn[...] = total[8:9] * TOKEN_SCALE
    hand(d_gain_merge, d_gain_merge_out)
    hand(d_gain_attn, d_gain_attn_out)
    for at, step in enumerate((1, 3, 2)):
        for half in (0, 1):
            arrive([m_copies[half][at]])
            m_pass(half, lax.rem(coordinate[orders[half][0]] + 4 - step, 4))
    late = q_sixth(1, late)
    arrive([early])
    hand(q_out.at[:, pl.ds(2 * WIDTH, WIDTH)], d_qkv_out.at[:, pl.ds(2 * WIDTH, WIDTH)])
    hand(q_out.at[:, pl.ds(3 * WIDTH, WIDTH)], d_proj_out)
    for copy, theirs in last:
        arrive([copy])
        hand(d_merge.at[theirs], d_merge_out.at[theirs])
    arrive([late])
    hand(q_out.at[:, pl.ds(0, 2 * WIDTH)], d_qkv_out.at[:, pl.ds(0, 2 * WIDTH)])
    for copy in handed:
        copy.wait()
    for copy in started[-SENDING:]:
        copy.wait_send()


def hand_out(*refs):
    given, outs, held, sems = refs[:7], refs[7:14], refs[14:21], refs[21]
    parts = [(i, None) for i in range(6)] + [(6, pl.ds(at * 512, 512)) for at in range(4)]
    both = []
    for at, (i, part) in enumerate(parts):
        source, stage, target = (r[i] if part is None else r[i].at[part] for r in (given, held, outs))
        both.append((
            pltpu.make_async_copy(source, stage, sems.at[0, at]),
            pltpu.make_async_copy(stage, target, sems.at[1, at]),
        ))
    for copy_in, _ in both[::-1]:
        copy_in.start()
    for copy_in, copy_out in both[::-1]:
        copy_in.wait()
        copy_out.start()
    for _, copy_out in both:
        copy_out.wait()


def local(leave, enter, back, home, tokens, cotangent, gain_attn, w_qkv, w_proj, gain_merge, w_merge):
    vmem, hbm = pl.BlockSpec(memory_space=pltpu.VMEM), pl.BlockSpec(memory_space=pltpu.HBM)
    held = pl.pallas_call(
        kernel,
        out_shape=(
            jax.ShapeDtypeStruct((GROUPS, 512), BF16),
            jax.ShapeDtypeStruct((CELLS, WIDTH), BF16),
            jax.ShapeDtypeStruct((1, WIDTH), F32),
            jax.ShapeDtypeStruct((WIDTH, 3 * WIDTH), BF16),
            jax.ShapeDtypeStruct((WIDTH, WIDTH), BF16),
            jax.ShapeDtypeStruct((1, 8 * WIDTH), F32),
            jax.ShapeDtypeStruct((8 * WIDTH, 512), BF16),
        ),
        in_specs=[hbm] * 7 + [vmem] * 4,
        out_specs=[hbm] * 7,
        scratch_shapes=[
            pltpu.VMEM((GROUPS, 512), BF16),
            pltpu.VMEM((1, WIDTH), F32),
            pltpu.VMEM((1, 8 * WIDTH), F32),
            pltpu.VMEM((WIDTH, 3 * WIDTH), BF16),
            pltpu.VMEM((WIDTH, WIDTH), BF16),
            pltpu.VMEM((8 * WIDTH, 512), BF16),
            pltpu.VMEM((HALO, ROWS), BF16),
            pltpu.VMEM((ROWS, HALO), BF16),
            pltpu.VMEM((HALO, ROWS), BF16),
            pltpu.VMEM((ROWS, HALO), BF16),
            pltpu.SemaphoreType.DMA((7,)),
            pltpu.VMEM((ROWS, WIDTH), BF16),
            pltpu.VMEM((HALO, WIDTH), BF16),
            pltpu.VMEM((HALO, WIDTH), BF16),
            pltpu.VMEM((HALO, WIDTH), BF16),
            pltpu.VMEM((HALO, WIDTH), BF16),
            pltpu.VMEM((CELLS, WIDTH), F32),
            pltpu.VMEM((CELLS, WIDTH), F32),
            pltpu.VMEM((CELLS, WIDTH), BF16),
            pltpu.VMEM((CELLS, 1), F32),
            pltpu.VMEM((CELLS, 3 * WIDTH), BF16),
            pltpu.VMEM((CELLS, 512), F32),
            pltpu.VMEM((CELLS, WIDTH), BF16),
            pltpu.VMEM((CELLS, WIDTH), F32),
            pltpu.VMEM((CELLS, WIDTH), BF16),
            pltpu.VMEM((CELLS, WIDTH), BF16),
            pltpu.VMEM((CELLS, 3 * WIDTH), BF16),
            pltpu.VMEM((CELLS, WIDTH), BF16),
            pltpu.VMEM((GROUPS, 512), BF16),
            pltpu.VMEM((GROUPS, 8 * WIDTH), BF16),
            pltpu.VMEM((GROUPS, 8 * WIDTH), F32),
            pltpu.VMEM((2, 8 * GROUPS, 128), BF16),
            pltpu.VMEM((2, 8 * GROUPS, 512), BF16),
            pltpu.VMEM((2, 128, 512), F32),
            pltpu.VMEM((2, 3, 32, 512), F32),
            pltpu.VMEM((2, 32, 512), F32),
            pltpu.VMEM((2, 7, 16, 128), F32),
            pltpu.VMEM((2, WIDTH, 512), F32),
            pltpu.VMEM((2, WIDTH, WIDTH), F32),
            pltpu.VMEM((2, WIDTH, WIDTH), F32),
            pltpu.VMEM((2, 2, 3, 32, WIDTH), F32),
            pltpu.VMEM((2, 2, 32, WIDTH), F32),
            pltpu.VMEM((2, 2, 3, 16, 128), F32),
            pltpu.VMEM((2, 8, 32, 128), F32),
            pltpu.VMEM((WIDTH, 1024), BF16),
            pltpu.VMEM((16, WIDTH), F32),
            pltpu.VMEM((16, 128), F32),
            pltpu.VMEM((4, 16, 128), F32),
            pltpu.VMEM((4, 16, 128), F32),
            pltpu.VMEM((8, 16, 128), F32),
            pltpu.VMEM((16, WIDTH), F32),
            pltpu.VMEM((GROUPS, 512), BF16),
            pltpu.VMEM((CELLS, WIDTH), BF16),
            pltpu.VMEM((1, WIDTH), F32),
            pltpu.VMEM((1, 8 * WIDTH), F32),
            pltpu.VMEM((8 * WIDTH, 512), BF16),
            pltpu.SemaphoreType.DMA((23,)),
            pltpu.SemaphoreType.DMA((SENDING,)),
            pltpu.SemaphoreType.DMA((COPIES,)),
        ],
        compiler_params=pltpu.CompilerParams(
            collective_id=0, has_side_effects=True, vmem_limit_bytes=60 * 1024 * 1024
        ),
        cost_estimate=pl.CostEstimate(flops=4 * 10**9, bytes_accessed=12 * 10**6, transcendentals=262144),
        name="window_step",
    )(
        tokens.reshape(CELLS, WIDTH), cotangent.reshape(GROUPS, 512),
        gain_attn.reshape(1, WIDTH), gain_merge.reshape(1, 8 * WIDTH),
        w_qkv, w_proj, w_merge, leave, enter, back, home,
    )
    outs = pl.pallas_call(
        hand_out,
        out_shape=[jax.ShapeDtypeStruct(h.shape, h.dtype) for h in held],
        in_specs=[pl.BlockSpec(memory_space=pl.ANY)] * 7,
        out_specs=[hbm] * 7,
        scratch_shapes=[pltpu.VMEM(h.shape, h.dtype) for h in held] + [pltpu.SemaphoreType.DMA((2, 10))],
        compiler_params=pltpu.CompilerParams(vmem_limit_bytes=60 * 1024 * 1024),
        name="hand_out",
    )(*held)
    merged, d_tokens, d_gain_attn, d_qkv, d_proj, d_gain_merge, d_merge = outs
    return (
        merged.reshape(cotangent.shape), d_tokens.reshape(tokens.shape), d_gain_attn.reshape(WIDTH),
        d_qkv, d_proj, d_gain_merge.reshape(8 * WIDTH), d_merge,
    )


def solution(mesh):
    constants = [jnp.asarray(m).reshape(1, -1) for m in orderings()]
    box, whole = P("gx", "gy", "gz", None), P()
    return jax.shard_map(
        functools.partial(local, *constants),
        mesh=mesh,
        in_specs=(box, box, whole, whole, whole, whole, whole),
        out_specs=(box, box, whole, whole, whole, whole, whole),
        check_vma=False,
    )
```

```python
import functools

import jax
import jax.numpy as jnp
import numpy as np
from jax import lax
from jax.experimental import pallas as pl
from jax.experimental.pallas import tpu as pltpu
from jax.sharding import PartitionSpec as P

MESH = pl.DeviceIdType.MESH
HEADS = 8
WIDTH = 256
CELLS = 512
GROUPS = 64
ROWS = CELLS + 2 * GROUPS
FACTOR = 32 ** -0.5
EPSILON = 1e-05
TOGETHER = 8
COPIES = 171
SENDING = 48
TOKENS = 131072
TOKEN_SCALE = float(TOKENS) ** (-0.5)
MERGE_SCALE = float(TOKENS // 8) ** (-0.5)
BF16, F32 = jnp.bfloat16, jnp.float32

KINDS = [(a, b, c) for a in (0, 1) for b in (0, 1) for c in (0, 1)]


def kind_groups(kind):
    a, b, c = kind
    return [
        (i, j, k)
        for i in ([0] if a else [1])
        for j in ([0] if b else [1, 2, 3])
        for k in ([0] if c else list(range(1, 8)))
    ]


SIZES = [-(-10 * len(kind_groups(kind)) // 16) * 16 for kind in KINDS]
STARTS = [sum(SIZES[:i]) for i in range(8)]
HALO = sum(SIZES)


def orderings():
    leave, enter = np.full(ROWS, -1, np.int32), np.full(HALO, -1, np.int32)
    back, home = np.full(ROWS, -1, np.int32), np.full(HALO, -1, np.int32)

    def pair(natural, place, windowed):
        leave[natural], enter[place] = place, windowed
        back[windowed], home[place] = place, natural

    for kind, start in zip(KINDS, STARTS):
        for at, (i, j, k) in enumerate(kind_groups(kind)):
            si, sj, sk = (i - 1) % 2, (j - 1) % 4, (k - 1) % 8
            window, place = (sj // 2) * 4 + sk // 2, si * 4 + (sj % 2) * 2 + sk % 2
            for o in range(8):
                cell = ((2 * i + o // 4) * 8 + 2 * j + o // 2 % 2) * 16 + 2 * k + o % 2
                pair(cell, start + at * 10 + o, window * 64 + o * 8 + place)
            for t in range(2):
                base = CELLS + t * GROUPS
                pair(base + (i * 4 + j) * 8 + k, start + at * 10 + 8 + t, base + window * 8 + place)
    return leave, enter, back, home


def one_hot(rows_of_columns, height):
    width = rows_of_columns.shape[1]
    ids = lax.broadcasted_iota(jnp.int32, (height, width), 0)
    return jnp.where(ids == rows_of_columns, 1.0, 0.0).astype(BF16)


def dot(left, right, left_dim=1, right_dim=0):
    return lax.dot_general(
        left, right, (((left_dim,), (right_dim,)), ((), ())), preferred_element_type=F32
    )


def norm_parts(parts, count):
    average = sum(jnp.sum(p, axis=-1, keepdims=True) for p in parts) * (1.0 / count)
    centred = [p - average for p in parts]
    variance = sum(jnp.sum(p * p, axis=-1, keepdims=True) for p in centred) * (1.0 / count)
    return centred, lax.rsqrt(variance + EPSILON)


def norm_back(hats, grads, inverse, count):
    first = sum(jnp.sum(g, axis=-1, keepdims=True) for g in grads) * (1.0 / count)
    second = sum(jnp.sum(g * h, axis=-1, keepdims=True) for g, h in zip(grads, hats)) * (1.0 / count)
    return [inverse * (g - first - h * second) for g, h in zip(grads, hats)]


def kernel(
    tokens_hbm, cotangent_hbm, gain_attn_hbm, gain_merge_hbm, w_qkv_hbm, w_proj_hbm, w_merge_hbm,
    leave_map, enter_map, back_map, home_map,
    merged_out, d_tokens_out, d_gain_attn_out, d_qkv_out, d_proj_out, d_gain_merge_out, d_merge_out,
    cotangent, gain_attn, gain_merge, w_qkv, w_proj, w_merge, leave, enter, back, home, local_sem,
    stacked, halo_send, halo_recv, back_send, back_recv,
    flat, hat, normal, inverse_a, qkv, probs, attended, summed, d_summed, d_attended, d_qkv, heads,
    cot, nm, hat_m, m_nm, m_cot, m_acc1, m_in2, m_acc2, m_in3,
    q_sum, q_near, q_half, q_in1, q_acc1, q_in2, q_in3, q_out,
    g_sum, g_near, g_in1, g_in2, g_in3, g_all,
    merged, d_tokens, d_gain_attn, d_gain_merge, d_merge, out_sem,
    send_sem, recv_sem,
):
    gx, gy, gz = lax.axis_index("gx"), lax.axis_index("gy"), lax.axis_index("gz")
    x, y_low, z = lax.div(gx, 2), lax.rem(gx, 2), gy
    y_high, core = lax.div(gz, 2), lax.rem(gz, 2)
    y = y_high * 2 + y_low

    def device(x_at, y_at, z_at, core_at):
        return (x_at * 2 + lax.rem(y_at, 2), z_at, lax.div(y_at, 2) * 2 + core_at)

    other_core = 1 - core

    def along(axis, step, core_at=core):
        if axis == "x":
            return device(lax.rem(x + step, 4), y, z, core_at)
        if axis == "y":
            return device(x, lax.rem(y + step, 4), z, core_at)
        return device(x, y, lax.rem(z + step, 8), core_at)

    partner = device(x, y, z, other_core)
    coordinate = {"x": x, "y": y, "z": z}

    def neighbour(kind, sign):
        a, b, c = kind
        return (
            lax.rem(gx + (8 + sign * a), 8),
            lax.rem(gy + (8 + sign * b), 8),
            lax.rem(gz + (4 + sign * c), 4),
        )

    started = []

    def send(source, target, to):
        at = len(started)
        if at >= SENDING:
            started[at - SENDING].wait_send()
        copy = pltpu.make_async_remote_copy(
            src_ref=source, dst_ref=target, send_sem=send_sem.at[at % SENDING], recv_sem=recv_sem.at[at],
            device_id=to, device_id_type=MESH,
        )
        copy.start()
        started.append(copy)
        return copy

    def arrive(copies):
        for copy in copies:
            copy.wait_recv()

    def rows(at, count):
        return pl.ds(pl.multiple_of(at * count, count), count)

    barrier = pltpu.get_barrier_semaphore()
    partners = [neighbour(kind, sign) for kind in KINDS[1:] for sign in (-1, 1)]
    partners += [along(axis, step) for axis in "xy" for step in (1, 2, 3)]
    partners += [along(axis, step, other_core) for axis in "xy" for step in (1, 2, 3)]
    partners += [along("z", step) for step in range(2, 7)]
    for there in partners:
        pl.semaphore_signal(barrier, inc=1, device_id=there, device_id_type=MESH)

    loads = {}
    for at, (name, source, target) in enumerate((
        ("tokens", tokens_hbm, stacked.at[pl.ds(0, CELLS)]),
        ("cotangent", cotangent_hbm, cotangent), ("gain_attn", gain_attn_hbm, gain_attn),
        ("gain_merge", gain_merge_hbm, gain_merge),
        ("w_qkv", w_qkv_hbm, w_qkv),
        ("w_proj", w_proj_hbm, w_proj), ("w_merge", w_merge_hbm, w_merge),
    )):
        loads[name] = pltpu.make_async_copy(source, target, local_sem.at[at])
        loads[name].start()

    leave[...] = one_hot(leave_map[...], HALO)
    loads["cotangent"].wait()
    stacked[CELLS : CELLS + GROUPS, :] = cotangent[:, 0:WIDTH]
    stacked[CELLS + GROUPS :, :] = cotangent[:, WIDTH:]
    loads["tokens"].wait()
    halo_send[...] = dot(leave[...], stacked[...]).astype(BF16)

    pl.semaphore_wait(barrier, len(partners))
    halo = []
    for kind, start, size in list(zip(KINDS, STARTS, SIZES))[1:]:
        block = pl.ds(start, size)
        halo.append(send(halo_send.at[block], halo_recv.at[block], neighbour(kind, -1)))
    halo_recv[0 : SIZES[0], :] = halo_send[0 : SIZES[0], :]
    head_of_lane = lax.div(lax.broadcasted_iota(jnp.int32, (64, WIDTH), 1), 32)
    for h in range(HEADS):
        heads[h * 64 : (h + 1) * 64, :] = jnp.where(head_of_lane == h, 1.0, 0.0).astype(BF16)
    enter[...] = one_hot(enter_map[...], ROWS)
    loads["w_qkv"].wait()
    loads["gain_attn"].wait()
    loads["gain_merge"].wait()
    arrive(halo)

    for t in range(2):
        part = dot(enter[CELLS + t * GROUPS : CELLS + (t + 1) * GROUPS, :], halo_recv[...])
        cot[:, t * WIDTH : (t + 1) * WIDTH] = part.astype(BF16)
    members = [(step, flip) for flip in (0, 1) for step in range(4)]
    orders = (("x", "y"), ("y", "x"))
    m_cot[0, 0:GROUPS, :] = cot[...]
    m_cot[1, 0:GROUPS, :] = cot[...]
    m_cots = []
    for step in (1, 2, 3):
        for half in (0, 1):
            target = m_cot.at[half, pl.ds(step * GROUPS, GROUPS)]
            m_cots.append(send(cot, target, along(orders[half][0], step)))
    flat[...] = dot(enter[0:CELLS, :], halo_recv[...])
    (centred,), inverse = norm_parts([flat[...]], WIDTH)
    inverse_a[...] = inverse
    hat[...] = centred * inverse
    normal[...] = (hat[...] * gain_attn[...]).astype(BF16)
    qkv[...] = dot(normal[...], w_qkv[...]).astype(BF16)

    def spread(block):
        return jnp.concatenate([block] * HEADS, axis=0) * heads[...]

    def gather(wide):
        total = wide[0:64]
        for h in range(1, HEADS):
            total = jnp.where(head_of_lane == h, wide[h * 64 : (h + 1) * 64], total)
        return total

    def over_windows(body):
        def step(i, carry):
            for w in range(TOGETHER):
                body(rows(i * TOGETHER + w, 64))
            return carry

        lax.fori_loop(0, 8 // TOGETHER, step, 0)

    def forward(here):
        query, key, value = (qkv[here, i * WIDTH : (i + 1) * WIDTH] for i in range(3))
        scores = dot(key, spread(query), 1, 1) * FACTOR
        powers = jnp.exp(scores - jnp.max(scores, axis=0, keepdims=True))
        weights = powers * (1.0 / jnp.sum(powers, axis=0, keepdims=True))
        probs[here, :] = weights
        attended[here, :] = gather(dot(weights.astype(BF16), value, 0, 0)).astype(BF16)

    over_windows(forward)
    loads["w_proj"].wait()
    summed[...] = (flat[...] + dot(attended[...], w_proj[...])).astype(BF16).astype(F32)

    shaped = summed[...].reshape(8, 8, 8, WIDTH)
    slabs = [shaped[:, o].reshape(GROUPS, WIDTH) for o in range(8)]
    centred, inverse = norm_parts(slabs, 8 * WIDTH)
    for o in range(8):
        lanes = slice(o * WIDTH, (o + 1) * WIDTH)
        hat_m[:, lanes] = centred[o] * inverse
        nm[:, lanes] = (hat_m[:, lanes] * gain_merge[:, lanes]).astype(BF16)
    m_rows = []
    for at, (step, flip) in enumerate(members):
        for half in (0, 1):
            axis, core_at = orders[half][0], (core, other_core)[flip]
            block = rows(half * 8 + core_at * 4 + lax.rem(coordinate[axis] + step, 4), 128)
            if at == 0:
                m_nm[half, 0:GROUPS, :] = nm[:, block]
            else:
                target = m_nm.at[half, pl.ds(at * GROUPS, GROUPS)]
                m_rows.append(send(nm.at[:, block], target, along(axis, step, core_at)))
    loads["w_merge"].wait()
    result = dot(nm[...], w_merge[...]).astype(BF16)
    for t in range(2):
        stacked[CELLS + t * GROUPS : CELLS + (t + 1) * GROUPS, :] = result[:, t * WIDTH : (t + 1) * WIDTH]
    hats, grads = [], []
    for o in range(8):
        lanes = slice(o * WIDTH, (o + 1) * WIDTH)
        grad = dot(cot[...], w_merge[lanes, :], 1, 1)
        hats.append(hat_m[:, lanes])
        grads.append(grad * gain_merge[:, lanes])
        g_sum[o : o + 1, :] = jnp.sum(grad * hats[o], axis=0, keepdims=True)
    grads = norm_back(hats, grads, inverse, 8 * WIDTH)
    joined = jnp.stack([g.reshape(8, 8, WIDTH) for g in grads], axis=1).reshape(CELLS, WIDTH)
    d_summed[...] = joined.astype(BF16)

    q_sum[0, :, WIDTH:] = dot(attended[...], d_summed[...], 0, 0)
    d_attended[...] = dot(d_summed[...], w_proj[...], 1, 1).astype(BF16)

    def backward_value(here):
        wide = spread(d_attended[here, :])
        d_qkv[here, 2 * WIDTH :] = dot(probs[here, :].astype(BF16), wide).astype(BF16)

    over_windows(backward_value)
    q_sum[0, :, 0:WIDTH] = dot(normal[...], d_qkv[:, 2 * WIDTH :], 0, 0)

    def q_start(part):
        return send(q_sum.at[part, :, rows(other_core, WIDTH)], q_near.at[part], partner)

    q_chips = [q_start(0)]

    def backward(here):
        query, key, value = (qkv[here, i * WIDTH : (i + 1) * WIDTH] for i in range(3))
        weights = probs[here, :]
        wide = spread(d_attended[here, :])
        d_probs = dot(value, wide, 1, 1)
        inner = jnp.sum(d_probs * weights, axis=0, keepdims=True)
        d_scores = (weights * (d_probs - inner) * FACTOR).astype(BF16)
        d_key = dot(d_scores, spread(query))
        d_query = gather(dot(d_scores, key, 0, 0))
        d_qkv[here, 0:WIDTH] = d_query.astype(BF16)
        d_qkv[here, WIDTH : 2 * WIDTH] = d_key.astype(BF16)

    def m_second(half):
        second = orders[half][1]
        m_acc1[half] = dot(m_nm[half], m_cot[half], 0, 0)
        copies = []
        for step in (1, 2, 3):
            chunk = rows(lax.rem(coordinate[second] + step, 4), 32)
            copies.append(send(m_acc1.at[half, chunk], m_in2.at[half, step - 1], along(second, step)))
        return copies


    def q_first(part):
        q_chips[part].wait_recv()
        q_half[part] = q_sum[part, :, rows(core, WIDTH)] + q_near[part]
        copies = []
        for half in (0, 1):
            axis = orders[half][0]
            for step in (1, 2, 3):
                chunk = rows(half * 4 + lax.rem(coordinate[axis] + step, 4), 32)
                target = q_in1.at[part, half, step - 1]
                copies.append(send(q_half.at[part, chunk], target, along(axis, step)))
        return copies

    def q_tile(at):
        return rows(lax.div(at, 2), 16), rows(lax.rem(at, 2), 128)

    def q_second(part, came):
        arrive(came)
        copies = []
        for half in (0, 1):
            first, second = orders[half]
            own = q_half[part, rows(half * 4 + coordinate[first], 32), :]
            q_acc1[part, half] = own + q_in1[part, half, 0] + q_in1[part, half, 1] + q_in1[part, half, 2]
            for step in (1, 2, 3):
                chunk = q_acc1.at[(part, half) + q_tile(lax.rem(coordinate[second] + step, 4))]
                copies.append(send(chunk, q_in2.at[part, half, step - 1], along(second, step)))
        return copies

    def q_third(part, came):
        arrive(came)
        for half in (0, 1):
            own = q_acc1[(part, half) + q_tile(coordinate[orders[half][1]])]
            total = own + q_in2[part, half, 0] + q_in2[part, half, 1] + q_in2[part, half, 2]
            q_in3[part, z, half * 16 : (half + 1) * 16, :] = total
        mine = q_in3.at[part, z]
        return [send(mine, mine, along("z", step)) for step in range(1, 8)]

    def q_lanes(part, at, count):
        return rows((1 - part) * (512 // count) + core * (WIDTH // count) + at, count)

    def q_fourth(part, came):
        arrive(came)
        total = q_in3[part, 0]
        for i in range(1, 8):
            total = total + q_in3[part, i]
        copies = []
        for half in (0, 1):
            first, second = orders[half]
            high, low = lax.div(coordinate[second], 2), lax.rem(coordinate[second], 2)
            here = (rows(half * 8 + coordinate[first] * 2 + high, 16), q_lanes(part, low, 128))
            q_out[here] = (total[half * 16 : (half + 1) * 16] * TOKEN_SCALE).astype(BF16)
            place = q_out.at[here]
            copies += [send(place, place, along(second, step)) for step in (1, 2, 3)]
        return copies

    def q_fifth(part, came):
        arrive(came)
        copies = []
        for half in (0, 1):
            first = orders[half][0]
            place = q_out.at[rows(half * 4 + coordinate[first], 32), q_lanes(part, 0, WIDTH)]
            copies += [send(place, place, along(first, step)) for step in (1, 2, 3)]
        return copies

    def q_sixth(part, came):
        arrive(came)
        place = q_out.at[:, q_lanes(part, 0, WIDTH)]
        return send(place, place, partner)

    last, handed = [], []

    def hand(source, target):
        copy = pltpu.make_async_copy(source, target, out_sem.at[len(handed)])
        copy.start()
        handed.append(copy)

    def m_third(half):
        second = orders[half][1]
        arrive(m_copies[half])
        own = m_acc1[half, rows(coordinate[second], 32), :]
        m_acc2[half] = own + m_in2[half, 0] + m_in2[half, 1] + m_in2[half, 2]
        copies = []
        for step in range(1, 8):
            there = lax.rem(z + step, 8)
            chunk = m_acc2.at[half, rows(lax.div(there, 4), 16), rows(lax.rem(there, 4), 128)]
            copies.append(send(chunk, m_in3.at[half, step - 1], along("z", step)))
        return copies

    def g_start(total, into, axis, count):
        into[coordinate[axis]] = total
        mine = into.at[coordinate[axis]]
        return [send(mine, mine, along(axis, step)) for step in range(1, count)]

    def g_total(into, count):
        total = into[0]
        for i in range(1, count):
            total = total + into[i]
        return total

    def m_place(half, x_or_y_first, x_or_y_second):
        return half * 1024 + core * 512 + x_or_y_first * 128 + x_or_y_second * 32

    def m_fourth(half):
        first, second = orders[half]
        arrive(m_copies[half])
        high, lane = lax.div(z, 4), rows(lax.rem(z, 4), 128)
        total = m_acc2[half, rows(high, 16), lane]
        for step in range(7):
            total = total + m_in3[half, step]
        start = m_place(half, coordinate[first], coordinate[second]) + high * 16
        here = (pl.ds(pl.multiple_of(start, 16), 16), lane)
        d_merge[here] = (total * MERGE_SCALE).astype(BF16)
        place = d_merge.at[here]
        return [send(place, place, along("z", step)) for step in range(1, 8)]

    def m_pass(half, came):
        mine, theirs = (rows(half * 8 + c * 4 + came, 128) for c in (core, other_core))
        place = d_merge.at[mine]
        last.append((send(place, place, partner), theirs))
        hand(place, d_merge_out.at[mine])

    def m_fifth(half):
        first, second = orders[half]
        arrive(m_copies[half])
        start = m_place(half, coordinate[first], coordinate[second])
        place = d_merge.at[pl.ds(pl.multiple_of(start, 32), 32)]
        return [send(place, place, along(second, step)) for step in (1, 3, 2)]

    def m_sixth(half):
        first = orders[half][0]
        arrive(m_copies[half])
        place = d_merge.at[rows(half * 8 + core * 4 + coordinate[first], 128)]
        copies = [send(place, place, along(first, step)) for step in (1, 3, 2)]
        m_pass(half, coordinate[first])
        return copies

    arrive(m_cots)
    m_pairs = []
    for half in (0, 1):
        source = m_cot.at[half, pl.ds(0, 4 * GROUPS)]
        m_pairs.append(send(source, m_cot.at[half, pl.ds(4 * GROUPS, 4 * GROUPS)], partner))
    early = q_first(0)
    arrive(m_pairs)
    arrive(m_rows)
    m_copies = [m_second(0), m_second(1)]
    over_windows(backward)
    q_sum[1] = dot(normal[...], d_qkv[:, 0 : 2 * WIDTH], 0, 0)
    q_chips.append(q_start(1))
    d_normal = dot(d_qkv[...], w_qkv[...], 1, 1)
    g_sum[8:16, :] = jnp.zeros((8, WIDTH), F32)
    g_sum[8:9, :] = jnp.sum(d_normal * hat[...], axis=0, keepdims=True)
    g_chip = send(g_sum.at[:, rows(other_core, 128)], g_near, partner)
    late = q_first(1)
    g_chip.wait_recv()
    g_copies = g_start(g_sum[:, rows(core, 128)] + g_near[...], g_in1, "x", 4)
    (d_flat,) = norm_back([hat[...]], [d_normal * gain_attn[...]], inverse_a[...], WIDTH)
    stacked[0:CELLS, :] = (d_summed[...].astype(F32) + d_flat).astype(BF16)
    back[...] = one_hot(back_map[...], HALO)
    back_send[...] = dot(back[...], stacked[...]).astype(BF16)
    halo = []
    for kind, start, size in list(zip(KINDS, STARTS, SIZES))[1:]:
        block = pl.ds(start, size)
        halo.append(send(back_send.at[block], back_recv.at[block], neighbour(kind, 1)))
    back_recv[0 : SIZES[0], :] = back_send[0 : SIZES[0], :]
    m_copies = [m_third(0), m_third(1)]
    early = q_second(0, early)
    home[...] = one_hot(home_map[...], ROWS)
    arrive(g_copies)
    g_copies = g_start(g_total(g_in1, 4), g_in2, "y", 4)
    late = q_second(1, late)
    early = q_third(0, early)

    arrive(halo)
    placed = dot(home[...], back_recv[...]).astype(BF16)
    d_tokens[...] = placed[0:CELLS]
    merged[:, 0:WIDTH] = placed[CELLS : CELLS + GROUPS]
    merged[:, WIDTH:] = placed[CELLS + GROUPS :]
    hand(d_tokens, d_tokens_out)
    hand(merged, merged_out)

    m_copies = [m_fourth(0), m_fourth(1)]
    late = q_third(1, late)
    arrive(g_copies)
    g_copies = g_start(g_total(g_in2, 4), g_in3, "z", 8)
    early = q_fourth(0, early)
    m_copies = [m_fifth(0), m_fifth(1)]
    late = q_fourth(1, late)
    early = q_fifth(0, early)
    m_copies = [m_sixth(0), m_sixth(1)]
    late = q_fifth(1, late)
    arrive(g_copies)
    g_all[:, rows(core, 128)] = g_total(g_in3, 8)
    g_mine = g_all.at[:, rows(core, 128)]
    g_last = send(g_mine, g_mine, partner)
    early = q_sixth(0, early)
    g_last.wait_recv()
    total = g_all[...]
    for o in range(8):
        d_gain_merge[:, o * WIDTH : (o + 1) * WIDTH] = total[o : o + 1] * MERGE_SCALE
    d_gain_attn[...] = total[8:9] * TOKEN_SCALE
    hand(d_gain_merge, d_gain_merge_out)
    hand(d_gain_attn, d_gain_attn_out)
    for at, step in enumerate((1, 3, 2)):
        for half in (0, 1):
            arrive([m_copies[half][at]])
            m_pass(half, lax.rem(coordinate[orders[half][0]] + 4 - step, 4))
    late = q_sixth(1, late)
    arrive([early])
    hand(q_out.at[:, pl.ds(2 * WIDTH, WIDTH)], d_qkv_out.at[:, pl.ds(2 * WIDTH, WIDTH)])
    hand(q_out.at[:, pl.ds(3 * WIDTH, WIDTH)], d_proj_out)
    for copy, theirs in last:
        arrive([copy])
        hand(d_merge.at[theirs], d_merge_out.at[theirs])
    arrive([late])
    hand(q_out.at[:, pl.ds(0, 2 * WIDTH)], d_qkv_out.at[:, pl.ds(0, 2 * WIDTH)])
    for copy in handed:
        copy.wait()
    for copy in started[-SENDING:]:
        copy.wait_send()


def hand_out(*refs):
    given, outs, held, sems = refs[:7], refs[7:14], refs[14:21], refs[21]
    parts = [(i, None) for i in range(6)] + [(6, pl.ds(at * 512, 512)) for at in range(4)]
    both = []
    for at, (i, part) in enumerate(parts):
        source, stage, target = (r[i] if part is None else r[i].at[part] for r in (given, held, outs))
        both.append((
            pltpu.make_async_copy(source, stage, sems.at[0, at]),
            pltpu.make_async_copy(stage, target, sems.at[1, at]),
        ))
    for copy_in, _ in both[::-1]:
        copy_in.start()
    for copy_in, copy_out in both[::-1]:
        copy_in.wait()
        copy_out.start()
    for _, copy_out in both:
        copy_out.wait()


def local(leave, enter, back, home, tokens, cotangent, gain_attn, w_qkv, w_proj, gain_merge, w_merge):
    vmem, hbm = pl.BlockSpec(memory_space=pltpu.VMEM), pl.BlockSpec(memory_space=pltpu.HBM)
    held = pl.pallas_call(
        kernel,
        out_shape=(
            jax.ShapeDtypeStruct((GROUPS, 512), BF16),
            jax.ShapeDtypeStruct((CELLS, WIDTH), BF16),
            jax.ShapeDtypeStruct((1, WIDTH), F32),
            jax.ShapeDtypeStruct((WIDTH, 3 * WIDTH), BF16),
            jax.ShapeDtypeStruct((WIDTH, WIDTH), BF16),
            jax.ShapeDtypeStruct((1, 8 * WIDTH), F32),
            jax.ShapeDtypeStruct((8 * WIDTH, 512), BF16),
        ),
        in_specs=[hbm] * 7 + [vmem] * 4,
        out_specs=[hbm] * 7,
        scratch_shapes=[
            pltpu.VMEM((GROUPS, 512), BF16),
            pltpu.VMEM((1, WIDTH), F32),
            pltpu.VMEM((1, 8 * WIDTH), F32),
            pltpu.VMEM((WIDTH, 3 * WIDTH), BF16),
            pltpu.VMEM((WIDTH, WIDTH), BF16),
            pltpu.VMEM((8 * WIDTH, 512), BF16),
            pltpu.VMEM((HALO, ROWS), BF16),
            pltpu.VMEM((ROWS, HALO), BF16),
            pltpu.VMEM((HALO, ROWS), BF16),
            pltpu.VMEM((ROWS, HALO), BF16),
            pltpu.SemaphoreType.DMA((7,)),
            pltpu.VMEM((ROWS, WIDTH), BF16),
            pltpu.VMEM((HALO, WIDTH), BF16),
            pltpu.VMEM((HALO, WIDTH), BF16),
            pltpu.VMEM((HALO, WIDTH), BF16),
            pltpu.VMEM((HALO, WIDTH), BF16),
            pltpu.VMEM((CELLS, WIDTH), F32),
            pltpu.VMEM((CELLS, WIDTH), F32),
            pltpu.VMEM((CELLS, WIDTH), BF16),
            pltpu.VMEM((CELLS, 1), F32),
            pltpu.VMEM((CELLS, 3 * WIDTH), BF16),
            pltpu.VMEM((CELLS, 512), F32),
            pltpu.VMEM((CELLS, WIDTH), BF16),
            pltpu.VMEM((CELLS, WIDTH), F32),
            pltpu.VMEM((CELLS, WIDTH), BF16),
            pltpu.VMEM((CELLS, WIDTH), BF16),
            pltpu.VMEM((CELLS, 3 * WIDTH), BF16),
            pltpu.VMEM((CELLS, WIDTH), BF16),
            pltpu.VMEM((GROUPS, 512), BF16),
            pltpu.VMEM((GROUPS, 8 * WIDTH), BF16),
            pltpu.VMEM((GROUPS, 8 * WIDTH), F32),
            pltpu.VMEM((2, 8 * GROUPS, 128), BF16),
            pltpu.VMEM((2, 8 * GROUPS, 512), BF16),
            pltpu.VMEM((2, 128, 512), F32),
            pltpu.VMEM((2, 3, 32, 512), F32),
            pltpu.VMEM((2, 32, 512), F32),
            pltpu.VMEM((2, 7, 16, 128), F32),
            pltpu.VMEM((2, WIDTH, 512), F32),
            pltpu.VMEM((2, WIDTH, WIDTH), F32),
            pltpu.VMEM((2, WIDTH, WIDTH), F32),
            pltpu.VMEM((2, 2, 3, 32, WIDTH), F32),
            pltpu.VMEM((2, 2, 32, WIDTH), F32),
            pltpu.VMEM((2, 2, 3, 16, 128), F32),
            pltpu.VMEM((2, 8, 32, 128), F32),
            pltpu.VMEM((WIDTH, 1024), BF16),
            pltpu.VMEM((16, WIDTH), F32),
            pltpu.VMEM((16, 128), F32),
            pltpu.VMEM((4, 16, 128), F32),
            pltpu.VMEM((4, 16, 128), F32),
            pltpu.VMEM((8, 16, 128), F32),
            pltpu.VMEM((16, WIDTH), F32),
            pltpu.VMEM((GROUPS, 512), BF16),
            pltpu.VMEM((CELLS, WIDTH), BF16),
            pltpu.VMEM((1, WIDTH), F32),
            pltpu.VMEM((1, 8 * WIDTH), F32),
            pltpu.VMEM((8 * WIDTH, 512), BF16),
            pltpu.SemaphoreType.DMA((23,)),
            pltpu.SemaphoreType.DMA((SENDING,)),
            pltpu.SemaphoreType.DMA((COPIES,)),
        ],
        compiler_params=pltpu.CompilerParams(
            collective_id=0, has_side_effects=True, vmem_limit_bytes=60 * 1024 * 1024
        ),
        cost_estimate=pl.CostEstimate(flops=4 * 10**9, bytes_accessed=12 * 10**6, transcendentals=262144),
        name="window_step",
    )(
        tokens.reshape(CELLS, WIDTH), cotangent.reshape(GROUPS, 512),
        gain_attn.reshape(1, WIDTH), gain_merge.reshape(1, 8 * WIDTH),
        w_qkv, w_proj, w_merge, leave, enter, back, home,
    )
    outs = pl.pallas_call(
        hand_out,
        out_shape=[jax.ShapeDtypeStruct(h.shape, h.dtype) for h in held],
        in_specs=[pl.BlockSpec(memory_space=pl.ANY)] * 7,
        out_specs=[hbm] * 7,
        scratch_shapes=[pltpu.VMEM(h.shape, h.dtype) for h in held] + [pltpu.SemaphoreType.DMA((2, 10))],
        compiler_params=pltpu.CompilerParams(vmem_limit_bytes=60 * 1024 * 1024),
        name="hand_out",
    )(*held)
    merged, d_tokens, d_gain_attn, d_qkv, d_proj, d_gain_merge, d_merge = outs
    return (
        merged.reshape(cotangent.shape), d_tokens.reshape(tokens.shape), d_gain_attn.reshape(WIDTH),
        d_qkv, d_proj, d_gain_merge.reshape(8 * WIDTH), d_merge,
    )


def solution(mesh):
    constants = [jnp.asarray(m).reshape(1, -1) for m in orderings()]
    box, whole = P("gx", "gy", "gz", None), P()
    return jax.shard_map(
        functools.partial(local, *constants),
        mesh=mesh,
        in_specs=(box, box, whole, whole, whole, whole, whole),
        out_specs=(box, box, whole, whole, whole, whole, whole),
        check_vma=False,
    )
```

```python
import functools

import jax
import jax.numpy as jnp
import numpy as np
from jax import lax
from jax.experimental import pallas as pl
from jax.experimental.pallas import tpu as pltpu
from jax.sharding import PartitionSpec as P

MESH = pl.DeviceIdType.MESH
HEADS = 8
WIDTH = 256
CELLS = 512
GROUPS = 64
ROWS = CELLS + 2 * GROUPS
FACTOR = 32 ** -0.5
EPSILON = 1e-05
TOGETHER = 8
COPIES = 164
SENDING = 48
TOKENS = 131072
TOKEN_SCALE = float(TOKENS) ** (-0.5)
MERGE_SCALE = float(TOKENS // 8) ** (-0.5)
BF16, F32 = jnp.bfloat16, jnp.float32

KINDS = [(a, b, c) for a in (0, 1) for b in (0, 1) for c in (0, 1)]


def kind_groups(kind):
    a, b, c = kind
    return [
        (i, j, k)
        for i in ([0] if a else [1])
        for j in ([0] if b else [1, 2, 3])
        for k in ([0] if c else list(range(1, 8)))
    ]


SIZES = [-(-10 * len(kind_groups(kind)) // 16) * 16 for kind in KINDS]
STARTS = [sum(SIZES[:i]) for i in range(8)]
HALO = sum(SIZES)


def orderings():
    leave, enter = np.full(ROWS, -1, np.int32), np.full(HALO, -1, np.int32)
    back, home = np.full(ROWS, -1, np.int32), np.full(HALO, -1, np.int32)

    def pair(natural, place, windowed):
        leave[natural], enter[place] = place, windowed
        back[windowed], home[place] = place, natural

    for kind, start in zip(KINDS, STARTS):
        for at, (i, j, k) in enumerate(kind_groups(kind)):
            si, sj, sk = (i - 1) % 2, (j - 1) % 4, (k - 1) % 8
            window, place = (sj // 2) * 4 + sk // 2, si * 4 + (sj % 2) * 2 + sk % 2
            for o in range(8):
                cell = ((2 * i + o // 4) * 8 + 2 * j + o // 2 % 2) * 16 + 2 * k + o % 2
                pair(cell, start + at * 10 + o, window * 64 + o * 8 + place)
            for t in range(2):
                base = CELLS + t * GROUPS
                pair(base + (i * 4 + j) * 8 + k, start + at * 10 + 8 + t, base + window * 8 + place)
    return leave, enter, back, home


def one_hot(rows_of_columns, height):
    width = rows_of_columns.shape[1]
    ids = lax.broadcasted_iota(jnp.int32, (height, width), 0)
    return jnp.where(ids == rows_of_columns, 1.0, 0.0).astype(BF16)


def dot(left, right, left_dim=1, right_dim=0):
    return lax.dot_general(
        left, right, (((left_dim,), (right_dim,)), ((), ())), preferred_element_type=F32
    )


def norm_parts(parts, count):
    average = sum(jnp.sum(p, axis=-1, keepdims=True) for p in parts) * (1.0 / count)
    centred = [p - average for p in parts]
    variance = sum(jnp.sum(p * p, axis=-1, keepdims=True) for p in centred) * (1.0 / count)
    return centred, lax.rsqrt(variance + EPSILON)


def norm_back(hats, grads, inverse, count):
    first = sum(jnp.sum(g, axis=-1, keepdims=True) for g in grads) * (1.0 / count)
    second = sum(jnp.sum(g * h, axis=-1, keepdims=True) for g, h in zip(grads, hats)) * (1.0 / count)
    return [inverse * (g - first - h * second) for g, h in zip(grads, hats)]


def kernel(
    tokens_hbm, cotangent_hbm, gain_attn_hbm, gain_merge_hbm, w_qkv_hbm, w_proj_hbm, w_merge_hbm,
    maps_hbm,
    merged_out, d_tokens_out, d_gain_attn_out, d_qkv_out, d_proj_out, d_gain_merge_out, d_merge_out,
    cotangent, gain_attn, gain_merge, w_qkv, w_proj, w_merge, leave, enter, back, home, maps, local_sem,
    stacked, halo_send, halo_recv, back_send, back_recv,
    flat, hat, normal, inverse_a, qkv, probs, attended, summed, d_summed, d_attended, d_qkv, heads,
    cot, nm, hat_m, m_nm, m_cot, m_acc1, m_in2, m_acc2, m_in3,
    q_sum, q_near, q_half, q_in1, q_acc1, q_in2, q_in3, q_out,
    g_sum, g_near, g_in1, g_in2, g_in3, g_all,
    merged, d_tokens, d_gain_attn, d_gain_merge, d_merge, out_sem,
    send_sem, recv_sem,
):
    gx, gy, gz = lax.axis_index("gx"), lax.axis_index("gy"), lax.axis_index("gz")
    x, y_low, z = lax.div(gx, 2), lax.rem(gx, 2), gy
    y_high, core = lax.div(gz, 2), lax.rem(gz, 2)
    y = y_high * 2 + y_low

    def device(x_at, y_at, z_at, core_at):
        return (x_at * 2 + lax.rem(y_at, 2), z_at, lax.div(y_at, 2) * 2 + core_at)

    other_core = 1 - core

    def along(axis, step, core_at=core):
        if axis == "x":
            return device(lax.rem(x + step, 4), y, z, core_at)
        if axis == "y":
            return device(x, lax.rem(y + step, 4), z, core_at)
        return device(x, y, lax.rem(z + step, 8), core_at)

    partner = device(x, y, z, other_core)
    coordinate = {"x": x, "y": y, "z": z}

    def neighbour(kind, sign):
        a, b, c = kind
        return (
            lax.rem(gx + (8 + sign * a), 8),
            lax.rem(gy + (8 + sign * b), 8),
            lax.rem(gz + (4 + sign * c), 4),
        )

    started = []

    def send(source, target, to):
        at = len(started)
        if at >= SENDING:
            started[at - SENDING].wait_send()
        copy = pltpu.make_async_remote_copy(
            src_ref=source, dst_ref=target, send_sem=send_sem.at[at % SENDING], recv_sem=recv_sem.at[at],
            device_id=to, device_id_type=MESH,
        )
        copy.start()
        started.append(copy)
        return copy

    def arrive(copies):
        for copy in copies:
            copy.wait_recv()

    def rows(at, count):
        return pl.ds(pl.multiple_of(at * count, count), count)

    loads = {}

    def load(name, source, target):
        loads[name] = pltpu.make_async_copy(source, target, local_sem.at[len(loads)])
        loads[name].start()

    load("maps", maps_hbm, maps)
    load("tokens", tokens_hbm, stacked.at[pl.ds(0, CELLS)])
    load("cotangent", cotangent_hbm, cotangent)

    barrier = pltpu.get_barrier_semaphore()
    partners = [neighbour(kind, sign) for kind in KINDS[1:] for sign in (-1, 1)]
    partners += [along(axis, step) for axis in "xy" for step in (1, 2, 3)]
    partners += [along(axis, step, other_core) for axis in "xy" for step in (1, 2, 3)]
    partners += [along("z", step) for step in range(2, 7)]
    for there in partners:
        pl.semaphore_signal(barrier, inc=1, device_id=there, device_id_type=MESH)

    load("w_qkv", w_qkv_hbm, w_qkv)
    load("gain_attn", gain_attn_hbm, gain_attn)
    load("gain_merge", gain_merge_hbm, gain_merge)
    load("w_proj", w_proj_hbm, w_proj)
    load("w_merge", w_merge_hbm, w_merge)
    loads["maps"].wait()
    leave[...] = one_hot(maps[0:1, 0:ROWS], HALO)
    loads["cotangent"].wait()
    stacked[CELLS : CELLS + GROUPS, :] = cotangent[:, 0:WIDTH]
    stacked[CELLS + GROUPS :, :] = cotangent[:, WIDTH:]
    loads["tokens"].wait()
    halo_send[...] = dot(leave[...], stacked[...]).astype(BF16)

    pl.semaphore_wait(barrier, len(partners))
    halo = []
    for kind, start, size in list(zip(KINDS, STARTS, SIZES))[1:]:
        block = pl.ds(start, size)
        halo.append(send(halo_send.at[block], halo_recv.at[block], neighbour(kind, -1)))
    halo_recv[0 : SIZES[0], :] = halo_send[0 : SIZES[0], :]
    head_of_lane = lax.div(lax.broadcasted_iota(jnp.int32, (64, WIDTH), 1), 32)
    for h in range(HEADS):
        heads[h * 64 : (h + 1) * 64, :] = jnp.where(head_of_lane == h, 1.0, 0.0).astype(BF16)
    enter[...] = one_hot(maps[1:2, 0:HALO], ROWS)
    loads["w_qkv"].wait()
    loads["gain_attn"].wait()
    loads["gain_merge"].wait()
    arrive(halo)

    flat[...] = dot(enter[0:CELLS, :], halo_recv[...])
    for t in range(2):
        part = dot(enter[CELLS + t * GROUPS : CELLS + (t + 1) * GROUPS, :], halo_recv[...])
        cot[:, t * WIDTH : (t + 1) * WIDTH] = part.astype(BF16)
    members = [(step, flip) for flip in (0, 1) for step in range(4)]
    orders = (("x", "y"), ("y", "x"))
    m_cot[0, 0:GROUPS, :] = cot[...]
    m_cot[1, 0:GROUPS, :] = cot[...]
    m_cots = []
    for step in (1, 2, 3):
        for half in (0, 1):
            target = m_cot.at[half, pl.ds(step * GROUPS, GROUPS)]
            m_cots.append(send(cot, target, along(orders[half][0], step)))
    (centred,), inverse = norm_parts([flat[...]], WIDTH)
    inverse_a[...] = inverse
    hat[...] = centred * inverse
    normal[...] = (hat[...] * gain_attn[...]).astype(BF16)
    qkv[...] = dot(normal[...], w_qkv[...]).astype(BF16)

    def spread(block):
        return jnp.concatenate([block] * HEADS, axis=0) * heads[...]

    def gather(wide):
        total = wide[0:64]
        for h in range(1, HEADS):
            total = jnp.where(head_of_lane == h, wide[h * 64 : (h + 1) * 64], total)
        return total

    def over_windows(body):
        def step(i, carry):
            for w in range(TOGETHER):
                body(rows(i * TOGETHER + w, 64))
            return carry

        lax.fori_loop(0, 8 // TOGETHER, step, 0)

    def forward(here):
        query, key, value = (qkv[here, i * WIDTH : (i + 1) * WIDTH] for i in range(3))
        scores = dot(key, spread(query), 1, 1) * FACTOR
        powers = jnp.exp(scores - jnp.max(scores, axis=0, keepdims=True))
        weights = powers * (1.0 / jnp.sum(powers, axis=0, keepdims=True))
        probs[here, :] = weights
        attended[here, :] = gather(dot(weights.astype(BF16), value, 0, 0)).astype(BF16)

    over_windows(forward)
    loads["w_proj"].wait()
    summed[...] = (flat[...] + dot(attended[...], w_proj[...])).astype(BF16).astype(F32)

    shaped = summed[...].reshape(8, 8, 8, WIDTH)
    slabs = [shaped[:, o].reshape(GROUPS, WIDTH) for o in range(8)]
    centred, inverse = norm_parts(slabs, 8 * WIDTH)
    for o in range(8):
        lanes = slice(o * WIDTH, (o + 1) * WIDTH)
        hat_m[:, lanes] = centred[o] * inverse
        nm[:, lanes] = (hat_m[:, lanes] * gain_merge[:, lanes]).astype(BF16)
    m_rows = []
    for at, (step, flip) in enumerate(members):
        for half in (0, 1):
            axis, core_at = orders[half][0], (core, other_core)[flip]
            block = rows(half * 8 + core_at * 4 + lax.rem(coordinate[axis] + step, 4), 128)
            if at == 0:
                m_nm[half, 0:GROUPS, :] = nm[:, block]
            else:
                target = m_nm.at[half, pl.ds(at * GROUPS, GROUPS)]
                m_rows.append(send(nm.at[:, block], target, along(axis, step, core_at)))
    loads["w_merge"].wait()
    result = dot(nm[...], w_merge[...]).astype(BF16)
    for t in range(2):
        stacked[CELLS + t * GROUPS : CELLS + (t + 1) * GROUPS, :] = result[:, t * WIDTH : (t + 1) * WIDTH]
    hats, grads = [], []
    for o in range(8):
        lanes = slice(o * WIDTH, (o + 1) * WIDTH)
        grad = dot(cot[...], w_merge[lanes, :], 1, 1)
        hats.append(hat_m[:, lanes])
        grads.append(grad * gain_merge[:, lanes])
        g_sum[o : o + 1, :] = jnp.sum(grad * hats[o], axis=0, keepdims=True)
    grads = norm_back(hats, grads, inverse, 8 * WIDTH)
    joined = jnp.stack([g.reshape(8, 8, WIDTH) for g in grads], axis=1).reshape(CELLS, WIDTH)
    d_summed[...] = joined.astype(BF16)

    arrive(m_cots)
    m_pairs = []
    for half in (0, 1):
        source = m_cot.at[half, pl.ds(0, 4 * GROUPS)]
        m_pairs.append(send(source, m_cot.at[half, pl.ds(4 * GROUPS, 4 * GROUPS)], partner))

    q_sum[0, :, WIDTH:] = dot(attended[...], d_summed[...], 0, 0)
    d_attended[...] = dot(d_summed[...], w_proj[...], 1, 1).astype(BF16)

    def backward_value(here):
        wide = spread(d_attended[here, :])
        d_qkv[here, 2 * WIDTH :] = dot(probs[here, :].astype(BF16), wide).astype(BF16)

    over_windows(backward_value)
    q_sum[0, :, 0:WIDTH] = dot(normal[...], d_qkv[:, 2 * WIDTH :], 0, 0)

    def q_start(part):
        return send(q_sum.at[part, :, rows(other_core, WIDTH)], q_near.at[part], partner)

    q_chips = [q_start(0)]

    def backward(here):
        query, key, value = (qkv[here, i * WIDTH : (i + 1) * WIDTH] for i in range(3))
        weights = probs[here, :]
        wide = spread(d_attended[here, :])
        d_probs = dot(value, wide, 1, 1)
        inner = jnp.sum(d_probs * weights, axis=0, keepdims=True)
        d_scores = (weights * (d_probs - inner) * FACTOR).astype(BF16)
        d_key = dot(d_scores, spread(query))
        d_query = gather(dot(d_scores, key, 0, 0))
        d_qkv[here, 0:WIDTH] = d_query.astype(BF16)
        d_qkv[here, WIDTH : 2 * WIDTH] = d_key.astype(BF16)

    arrive(m_pairs)
    arrive(m_rows)

    def m_second(half):
        second = orders[half][1]
        m_acc1[half] = dot(m_nm[half], m_cot[half], 0, 0)
        copies = []
        for step in (1, 2, 3):
            chunk = rows(lax.rem(coordinate[second] + step, 4), 32)
            copies.append(send(m_acc1.at[half, chunk], m_in2.at[half, step - 1], along(second, step)))
        return copies

    m_copies = [m_second(0), m_second(1)]

    def q_first(part):
        q_chips[part].wait_recv()
        q_half[part] = q_sum[part, :, rows(core, WIDTH)] + q_near[part]
        copies = []
        for half in (0, 1):
            axis = orders[half][0]
            for step in (1, 2, 3):
                chunk = rows(half * 4 + lax.rem(coordinate[axis] + step, 4), 32)
                target = q_in1.at[part, half, step - 1]
                copies.append(send(q_half.at[part, chunk], target, along(axis, step)))
        return copies

    def q_tile(at):
        return rows(lax.div(at, 2), 16), rows(lax.rem(at, 2), 128)

    def q_second(part, came):
        arrive(came)
        copies = []
        for half in (0, 1):
            first, second = orders[half]
            own = q_half[part, rows(half * 4 + coordinate[first], 32), :]
            q_acc1[part, half] = own + q_in1[part, half, 0] + q_in1[part, half, 1] + q_in1[part, half, 2]
            for step in (1, 2, 3):
                chunk = q_acc1.at[(part, half) + q_tile(lax.rem(coordinate[second] + step, 4))]
                copies.append(send(chunk, q_in2.at[part, half, step - 1], along(second, step)))
        return copies

    def q_third(part, came):
        arrive(came)
        for half in (0, 1):
            own = q_acc1[(part, half) + q_tile(coordinate[orders[half][1]])]
            total = own + q_in2[part, half, 0] + q_in2[part, half, 1] + q_in2[part, half, 2]
            q_in3[part, z, half * 16 : (half + 1) * 16, :] = total
        mine = q_in3.at[part, z]
        return [send(mine, mine, along("z", step)) for step in range(1, 8)]

    def q_lanes(part, at, count):
        return rows((1 - part) * (512 // count) + core * (WIDTH // count) + at, count)

    def q_fourth(part, came):
        arrive(came)
        total = q_in3[part, 0]
        for i in range(1, 8):
            total = total + q_in3[part, i]
        copies = []
        for half in (0, 1):
            first, second = orders[half]
            high, low = lax.div(coordinate[second], 2), lax.rem(coordinate[second], 2)
            here = (rows(half * 8 + coordinate[first] * 2 + high, 16), q_lanes(part, low, 128))
            q_out[here] = (total[half * 16 : (half + 1) * 16] * TOKEN_SCALE).astype(BF16)
            place = q_out.at[here]
            copies += [send(place, place, along(second, step)) for step in (1, 2, 3)]
        return copies

    def q_fifth(part, came):
        arrive(came)
        copies = []
        for half in (0, 1):
            first = orders[half][0]
            place = q_out.at[rows(half * 4 + coordinate[first], 32), q_lanes(part, 0, WIDTH)]
            copies += [send(place, place, along(first, step)) for step in (1, 2, 3)]
        return copies

    def q_sixth(part, came):
        arrive(came)
        place = q_out.at[:, q_lanes(part, 0, WIDTH)]
        return send(place, place, partner)

    last, handed = [], []

    def hand(source, target):
        copy = pltpu.make_async_copy(source, target, out_sem.at[len(handed)])
        copy.start()
        handed.append(copy)

    def m_third(came):
        arrive(came)
        for half in (0, 1):
            own = m_acc1[half, rows(coordinate[orders[half][1]], 32), :]
            m_acc2[half] = own + m_in2[half, 0] + m_in2[half, 1] + m_in2[half, 2]
        copies = []
        for step in range(1, 8):
            there = lax.rem(z + step, 8)
            chunk = m_acc2.at[:, rows(lax.div(there, 4), 16), rows(lax.rem(there, 4), 128)]
            copies.append(send(chunk, m_in3.at[step - 1], along("z", step)))
        return copies

    def g_start(total, into, axis, count):
        into[coordinate[axis]] = total
        mine = into.at[coordinate[axis]]
        return [send(mine, mine, along(axis, step)) for step in range(1, count)]

    def g_total(into, count):
        total = into[0]
        for i in range(1, count):
            total = total + into[i]
        return total

    def m_place(half, x_or_y_first, x_or_y_second):
        return half * 1024 + core * 512 + x_or_y_first * 128 + x_or_y_second * 32

    def m_fourth(half):
        first, second = orders[half]
        high, lane = lax.div(z, 4), rows(lax.rem(z, 4), 128)
        total = m_acc2[half, rows(high, 16), lane]
        for step in range(7):
            total = total + m_in3[step, half]
        start = m_place(half, coordinate[first], coordinate[second]) + high * 16
        here = (pl.ds(pl.multiple_of(start, 16), 16), lane)
        d_merge[here] = (total * MERGE_SCALE).astype(BF16)
        place = d_merge.at[here]
        return [send(place, place, along("z", step)) for step in range(1, 8)]

    def m_pass(half, came):
        mine, theirs = (rows(half * 8 + c * 4 + came, 128) for c in (core, other_core))
        place = d_merge.at[mine]
        last.append((send(place, place, partner), theirs))
        hand(place, d_merge_out.at[mine])

    def m_fifth(half):
        first, second = orders[half]
        arrive(m_copies[half])
        start = m_place(half, coordinate[first], coordinate[second])
        place = d_merge.at[pl.ds(pl.multiple_of(start, 32), 32)]
        return [send(place, place, along(second, step)) for step in (1, 3, 2)]

    def m_sixth(half):
        first = orders[half][0]
        arrive(m_copies[half])
        place = d_merge.at[rows(half * 8 + core * 4 + coordinate[first], 128)]
        copies = [send(place, place, along(first, step)) for step in (1, 3, 2)]
        m_pass(half, coordinate[first])
        return copies

    early = q_first(0)
    over_windows(backward)
    q_sum[1] = dot(normal[...], d_qkv[:, 0 : 2 * WIDTH], 0, 0)
    q_chips.append(q_start(1))
    d_normal = dot(d_qkv[...], w_qkv[...], 1, 1)
    g_sum[8:16, :] = jnp.zeros((8, WIDTH), F32)
    g_sum[8:9, :] = jnp.sum(d_normal * hat[...], axis=0, keepdims=True)
    g_chip = send(g_sum.at[:, rows(other_core, 128)], g_near, partner)
    late = q_first(1)
    (d_flat,) = norm_back([hat[...]], [d_normal * gain_attn[...]], inverse_a[...], WIDTH)
    stacked[0:CELLS, :] = (d_summed[...].astype(F32) + d_flat).astype(BF16)
    back[...] = one_hot(maps[2:3, 0:ROWS], HALO)
    back_send[...] = dot(back[...], stacked[...]).astype(BF16)
    halo = []
    for kind, start, size in list(zip(KINDS, STARTS, SIZES))[1:]:
        block = pl.ds(start, size)
        halo.append(send(back_send.at[block], back_recv.at[block], neighbour(kind, 1)))
    back_recv[0 : SIZES[0], :] = back_send[0 : SIZES[0], :]
    early = q_second(0, early)
    m_copies = m_third(m_copies[0] + m_copies[1])
    g_chip.wait_recv()
    g_copies = g_start(g_sum[:, rows(core, 128)] + g_near[...], g_in1, "x", 4)
    home[...] = one_hot(maps[3:4, 0:HALO], ROWS)

    arrive(m_copies)
    m_copies = [m_fourth(0), m_fourth(1)]
    late = q_second(1, late)
    early = q_third(0, early)
    arrive(g_copies)
    g_copies = g_start(g_total(g_in1, 4), g_in2, "y", 4)

    arrive(halo)
    placed = dot(home[...], back_recv[...]).astype(BF16)
    d_tokens[...] = placed[0:CELLS]
    merged[:, 0:WIDTH] = placed[CELLS : CELLS + GROUPS]
    merged[:, WIDTH:] = placed[CELLS + GROUPS :]
    hand(d_tokens, d_tokens_out)
    hand(merged, merged_out)
    late = q_third(1, late)
    m_copies = [m_fifth(0), m_fifth(1)]
    arrive(g_copies)
    g_copies = g_start(g_total(g_in2, 4), g_in3, "z", 8)
    early = q_fourth(0, early)
    m_copies = [m_sixth(0), m_sixth(1)]
    late = q_fourth(1, late)
    early = q_fifth(0, early)
    arrive(g_copies)
    g_all[:, rows(core, 128)] = g_total(g_in3, 8)
    g_mine = g_all.at[:, rows(core, 128)]
    g_last = send(g_mine, g_mine, partner)
    late = q_fifth(1, late)
    early = q_sixth(0, early)
    g_last.wait_recv()
    total = g_all[...]
    for o in range(8):
        d_gain_merge[:, o * WIDTH : (o + 1) * WIDTH] = total[o : o + 1] * MERGE_SCALE
    d_gain_attn[...] = total[8:9] * TOKEN_SCALE
    hand(d_gain_merge, d_gain_merge_out)
    hand(d_gain_attn, d_gain_attn_out)
    for at, step in enumerate((1, 3, 2)):
        for half in (0, 1):
            arrive([m_copies[half][at]])
            m_pass(half, lax.rem(coordinate[orders[half][0]] + 4 - step, 4))
    late = q_sixth(1, late)
    arrive([early])
    hand(q_out.at[:, pl.ds(2 * WIDTH, WIDTH)], d_qkv_out.at[:, pl.ds(2 * WIDTH, WIDTH)])
    hand(q_out.at[:, pl.ds(3 * WIDTH, WIDTH)], d_proj_out)
    for copy, theirs in last:
        arrive([copy])
        hand(d_merge.at[theirs], d_merge_out.at[theirs])
    arrive([late])
    hand(q_out.at[:, pl.ds(0, 2 * WIDTH)], d_qkv_out.at[:, pl.ds(0, 2 * WIDTH)])
    for copy in handed:
        copy.wait()
    for copy in started[-SENDING:]:
        copy.wait_send()


def hand_out(*refs):
    given, outs, held, sems = refs[:7], refs[7:14], refs[14:21], refs[21]
    parts = [(i, None) for i in range(6)] + [(6, pl.ds(at * 512, 512)) for at in range(4)]
    both = []
    for at, (i, part) in enumerate(parts):
        source, stage, target = (r[i] if part is None else r[i].at[part] for r in (given, held, outs))
        both.append((
            pltpu.make_async_copy(source, stage, sems.at[0, at]),
            pltpu.make_async_copy(stage, target, sems.at[1, at]),
        ))
    for copy_in, _ in both[::-1]:
        copy_in.start()
    for copy_in, copy_out in both[::-1]:
        copy_in.wait()
        copy_out.start()
    for _, copy_out in both:
        copy_out.wait()


def local(maps, tokens, cotangent, gain_attn, w_qkv, w_proj, gain_merge, w_merge):
    hbm = pl.BlockSpec(memory_space=pltpu.HBM)
    held = pl.pallas_call(
        kernel,
        out_shape=(
            jax.ShapeDtypeStruct((GROUPS, 512), BF16),
            jax.ShapeDtypeStruct((CELLS, WIDTH), BF16),
            jax.ShapeDtypeStruct((1, WIDTH), F32),
            jax.ShapeDtypeStruct((WIDTH, 3 * WIDTH), BF16),
            jax.ShapeDtypeStruct((WIDTH, WIDTH), BF16),
            jax.ShapeDtypeStruct((1, 8 * WIDTH), F32),
            jax.ShapeDtypeStruct((8 * WIDTH, 512), BF16),
        ),
        in_specs=[hbm] * 8,
        out_specs=[hbm] * 7,
        scratch_shapes=[
            pltpu.VMEM((GROUPS, 512), BF16),
            pltpu.VMEM((1, WIDTH), F32),
            pltpu.VMEM((1, 8 * WIDTH), F32),
            pltpu.VMEM((WIDTH, 3 * WIDTH), BF16),
            pltpu.VMEM((WIDTH, WIDTH), BF16),
            pltpu.VMEM((8 * WIDTH, 512), BF16),
            pltpu.VMEM((HALO, ROWS), BF16),
            pltpu.VMEM((ROWS, HALO), BF16),
            pltpu.VMEM((HALO, ROWS), BF16),
            pltpu.VMEM((ROWS, HALO), BF16),
            pltpu.VMEM((8, 768), jnp.int32),
            pltpu.SemaphoreType.DMA((8,)),
            pltpu.VMEM((ROWS, WIDTH), BF16),
            pltpu.VMEM((HALO, WIDTH), BF16),
            pltpu.VMEM((HALO, WIDTH), BF16),
            pltpu.VMEM((HALO, WIDTH), BF16),
            pltpu.VMEM((HALO, WIDTH), BF16),
            pltpu.VMEM((CELLS, WIDTH), F32),
            pltpu.VMEM((CELLS, WIDTH), F32),
            pltpu.VMEM((CELLS, WIDTH), BF16),
            pltpu.VMEM((CELLS, 1), F32),
            pltpu.VMEM((CELLS, 3 * WIDTH), BF16),
            pltpu.VMEM((CELLS, 512), F32),
            pltpu.VMEM((CELLS, WIDTH), BF16),
            pltpu.VMEM((CELLS, WIDTH), F32),
            pltpu.VMEM((CELLS, WIDTH), BF16),
            pltpu.VMEM((CELLS, WIDTH), BF16),
            pltpu.VMEM((CELLS, 3 * WIDTH), BF16),
            pltpu.VMEM((CELLS, WIDTH), BF16),
            pltpu.VMEM((GROUPS, 512), BF16),
            pltpu.VMEM((GROUPS, 8 * WIDTH), BF16),
            pltpu.VMEM((GROUPS, 8 * WIDTH), F32),
            pltpu.VMEM((2, 8 * GROUPS, 128), BF16),
            pltpu.VMEM((2, 8 * GROUPS, 512), BF16),
            pltpu.VMEM((2, 128, 512), F32),
            pltpu.VMEM((2, 3, 32, 512), F32),
            pltpu.VMEM((2, 32, 512), F32),
            pltpu.VMEM((7, 2, 16, 128), F32),
            pltpu.VMEM((2, WIDTH, 512), F32),
            pltpu.VMEM((2, WIDTH, WIDTH), F32),
            pltpu.VMEM((2, WIDTH, WIDTH), F32),
            pltpu.VMEM((2, 2, 3, 32, WIDTH), F32),
            pltpu.VMEM((2, 2, 32, WIDTH), F32),
            pltpu.VMEM((2, 2, 3, 16, 128), F32),
            pltpu.VMEM((2, 8, 32, 128), F32),
            pltpu.VMEM((WIDTH, 1024), BF16),
            pltpu.VMEM((16, WIDTH), F32),
            pltpu.VMEM((16, 128), F32),
            pltpu.VMEM((4, 16, 128), F32),
            pltpu.VMEM((4, 16, 128), F32),
            pltpu.VMEM((8, 16, 128), F32),
            pltpu.VMEM((16, WIDTH), F32),
            pltpu.VMEM((GROUPS, 512), BF16),
            pltpu.VMEM((CELLS, WIDTH), BF16),
            pltpu.VMEM((1, WIDTH), F32),
            pltpu.VMEM((1, 8 * WIDTH), F32),
            pltpu.VMEM((8 * WIDTH, 512), BF16),
            pltpu.SemaphoreType.DMA((23,)),
            pltpu.SemaphoreType.DMA((SENDING,)),
            pltpu.SemaphoreType.DMA((COPIES,)),
        ],
        compiler_params=pltpu.CompilerParams(
            collective_id=0, has_side_effects=True, vmem_limit_bytes=60 * 1024 * 1024
        ),
        cost_estimate=pl.CostEstimate(flops=4 * 10**9, bytes_accessed=12 * 10**6, transcendentals=262144),
        name="window_step",
    )(
        tokens.reshape(CELLS, WIDTH), cotangent.reshape(GROUPS, 512),
        gain_attn.reshape(1, WIDTH), gain_merge.reshape(1, 8 * WIDTH),
        w_qkv, w_proj, w_merge, maps,
    )
    outs = pl.pallas_call(
        hand_out,
        out_shape=[jax.ShapeDtypeStruct(h.shape, h.dtype) for h in held],
        in_specs=[pl.BlockSpec(memory_space=pl.ANY)] * 7,
        out_specs=[hbm] * 7,
        scratch_shapes=[pltpu.VMEM(h.shape, h.dtype) for h in held] + [pltpu.SemaphoreType.DMA((2, 10))],
        compiler_params=pltpu.CompilerParams(vmem_limit_bytes=60 * 1024 * 1024),
        name="hand_out",
    )(*held)
    merged, d_tokens, d_gain_attn, d_qkv, d_proj, d_gain_merge, d_merge = outs
    return (
        merged.reshape(cotangent.shape), d_tokens.reshape(tokens.shape), d_gain_attn.reshape(WIDTH),
        d_qkv, d_proj, d_gain_merge.reshape(8 * WIDTH), d_merge,
    )


def solution(mesh):
    maps = np.full((8, 768), -1, np.int32)
    for at, rows_of_columns in enumerate(orderings()):
        maps[at, : len(rows_of_columns)] = rows_of_columns
    box, whole = P("gx", "gy", "gz", None), P()
    return jax.shard_map(
        functools.partial(local, jnp.asarray(maps)),
        mesh=mesh,
        in_specs=(box, box, whole, whole, whole, whole, whole),
        out_specs=(box, box, whole, whole, whole, whole, whole),
        check_vma=False,
    )
```

```python
import functools

import jax
import jax.numpy as jnp
import numpy as np
from jax import lax
from jax.experimental import pallas as pl
from jax.experimental.pallas import tpu as pltpu
from jax.sharding import PartitionSpec as P

MESH = pl.DeviceIdType.MESH
HEADS = 8
WIDTH = 256
CELLS = 512
GROUPS = 64
ROWS = CELLS + 2 * GROUPS
FACTOR = 32 ** -0.5
EPSILON = 1e-05
TOGETHER = 8
COPIES = 164
SENDING = 48
TOKENS = 131072
TOKEN_SCALE = float(TOKENS) ** (-0.5)
MERGE_SCALE = float(TOKENS // 8) ** (-0.5)
BF16, F32 = jnp.bfloat16, jnp.float32

KINDS = [(a, b, c) for a in (0, 1) for b in (0, 1) for c in (0, 1)]


def kind_groups(kind):
    a, b, c = kind
    return [
        (i, j, k)
        for i in ([0] if a else [1])
        for j in ([0] if b else [1, 2, 3])
        for k in ([0] if c else list(range(1, 8)))
    ]


SIZES = [-(-10 * len(kind_groups(kind)) // 16) * 16 for kind in KINDS]
STARTS = [sum(SIZES[:i]) for i in range(8)]
HALO = sum(SIZES)


def orderings():
    leave, enter = np.full(ROWS, -1, np.int32), np.full(HALO, -1, np.int32)
    back, home = np.full(ROWS, -1, np.int32), np.full(HALO, -1, np.int32)

    def pair(natural, place, windowed):
        leave[natural], enter[place] = place, windowed
        back[windowed], home[place] = place, natural

    for kind, start in zip(KINDS, STARTS):
        for at, (i, j, k) in enumerate(kind_groups(kind)):
            si, sj, sk = (i - 1) % 2, (j - 1) % 4, (k - 1) % 8
            window, place = (sj // 2) * 4 + sk // 2, si * 4 + (sj % 2) * 2 + sk % 2
            for o in range(8):
                cell = ((2 * i + o // 4) * 8 + 2 * j + o // 2 % 2) * 16 + 2 * k + o % 2
                pair(cell, start + at * 10 + o, window * 64 + o * 8 + place)
            for t in range(2):
                base = CELLS + t * GROUPS
                pair(base + (i * 4 + j) * 8 + k, start + at * 10 + 8 + t, base + window * 8 + place)
    return leave, enter, back, home


def one_hot(rows_of_columns, height):
    width = rows_of_columns.shape[1]
    ids = lax.broadcasted_iota(jnp.int32, (height, width), 0)
    return jnp.where(ids == rows_of_columns, 1.0, 0.0).astype(BF16)


def dot(left, right, left_dim=1, right_dim=0):
    return lax.dot_general(
        left, right, (((left_dim,), (right_dim,)), ((), ())), preferred_element_type=F32
    )


def norm_parts(parts, count):
    average = sum(jnp.sum(p, axis=-1, keepdims=True) for p in parts) * (1.0 / count)
    centred = [p - average for p in parts]
    variance = sum(jnp.sum(p * p, axis=-1, keepdims=True) for p in centred) * (1.0 / count)
    return centred, lax.rsqrt(variance + EPSILON)


def norm_back(hats, grads, inverse, count):
    first = sum(jnp.sum(g, axis=-1, keepdims=True) for g in grads) * (1.0 / count)
    second = sum(jnp.sum(g * h, axis=-1, keepdims=True) for g, h in zip(grads, hats)) * (1.0 / count)
    return [inverse * (g - first - h * second) for g, h in zip(grads, hats)]


def kernel(
    tokens_hbm, cotangent_hbm, gain_attn_hbm, gain_merge_hbm, w_qkv_hbm, w_proj_hbm, w_merge_hbm,
    maps_hbm,
    merged_out, d_tokens_out, d_gain_attn_out, d_qkv_out, d_proj_out, d_gain_merge_out, d_merge_out,
    cotangent, gain_attn, gain_merge, w_qkv, w_proj, w_merge, leave, enter, back, home, maps, local_sem,
    stacked, halo_send, halo_recv, back_send, back_recv,
    flat, hat, normal, inverse_a, qkv, probs, attended, summed, d_summed, d_attended, d_qkv, heads,
    cot, nm, hat_m, m_nm, m_cot, m_acc1, m_in2, m_acc2, m_in3,
    q_sum, q_near, q_half, q_in1, q_acc1, q_in2, q_in3, q_out,
    g_sum, g_near, g_in1, g_in2, g_in3, g_all,
    merged, d_tokens, d_gain_attn, d_gain_merge, d_merge, out_sem,
    send_sem, recv_sem,
):
    gx, gy, gz = lax.axis_index("gx"), lax.axis_index("gy"), lax.axis_index("gz")
    x, y_low, z = lax.div(gx, 2), lax.rem(gx, 2), gy
    y_high, core = lax.div(gz, 2), lax.rem(gz, 2)
    y = y_high * 2 + y_low

    def device(x_at, y_at, z_at, core_at):
        return (x_at * 2 + lax.rem(y_at, 2), z_at, lax.div(y_at, 2) * 2 + core_at)

    other_core = 1 - core

    def along(axis, step, core_at=core):
        if axis == "x":
            return device(lax.rem(x + step, 4), y, z, core_at)
        if axis == "y":
            return device(x, lax.rem(y + step, 4), z, core_at)
        return device(x, y, lax.rem(z + step, 8), core_at)

    partner = device(x, y, z, other_core)
    coordinate = {"x": x, "y": y, "z": z}

    def neighbour(kind, sign):
        a, b, c = kind
        return (
            lax.rem(gx + (8 + sign * a), 8),
            lax.rem(gy + (8 + sign * b), 8),
            lax.rem(gz + (4 + sign * c), 4),
        )

    started = []

    def send(source, target, to):
        at = len(started)
        if at >= SENDING:
            started[at - SENDING].wait_send()
        copy = pltpu.make_async_remote_copy(
            src_ref=source, dst_ref=target, send_sem=send_sem.at[at % SENDING], recv_sem=recv_sem.at[at],
            device_id=to, device_id_type=MESH,
        )
        copy.start()
        started.append(copy)
        return copy

    def arrive(copies):
        for copy in copies:
            copy.wait_recv()

    def rows(at, count):
        return pl.ds(pl.multiple_of(at * count, count), count)

    loads = {}

    def load(name, source, target):
        loads[name] = pltpu.make_async_copy(source, target, local_sem.at[len(loads)])
        loads[name].start()

    load("maps", maps_hbm, maps)
    load("tokens", tokens_hbm, stacked.at[pl.ds(0, CELLS)])
    load("cotangent", cotangent_hbm, cotangent)

    barrier = pltpu.get_barrier_semaphore()
    partners = [neighbour(kind, sign) for kind in KINDS[1:] for sign in (-1, 1)]
    partners += [along(axis, step) for axis in "xy" for step in (1, 2, 3)]
    partners += [along(axis, step, other_core) for axis in "xy" for step in (1, 2, 3)]
    partners += [along("z", step) for step in range(2, 7)]
    for there in partners:
        pl.semaphore_signal(barrier, inc=1, device_id=there, device_id_type=MESH)

    load("w_qkv", w_qkv_hbm, w_qkv)
    load("gain_attn", gain_attn_hbm, gain_attn)
    load("gain_merge", gain_merge_hbm, gain_merge)
    load("w_proj", w_proj_hbm, w_proj)
    load("w_merge", w_merge_hbm, w_merge)
    loads["maps"].wait()
    leave[...] = one_hot(maps[0:1, 0:ROWS], HALO)
    loads["cotangent"].wait()
    stacked[CELLS : CELLS + GROUPS, :] = cotangent[:, 0:WIDTH]
    stacked[CELLS + GROUPS :, :] = cotangent[:, WIDTH:]
    loads["tokens"].wait()
    halo_send[...] = dot(leave[...], stacked[...]).astype(BF16)

    pl.semaphore_wait(barrier, len(partners))
    halo = []
    for kind, start, size in list(zip(KINDS, STARTS, SIZES))[1:]:
        block = pl.ds(start, size)
        halo.append(send(halo_send.at[block], halo_recv.at[block], neighbour(kind, -1)))
    halo_recv[0 : SIZES[0], :] = halo_send[0 : SIZES[0], :]
    head_of_lane = lax.div(lax.broadcasted_iota(jnp.int32, (64, WIDTH), 1), 32)
    for h in range(HEADS):
        heads[h * 64 : (h + 1) * 64, :] = jnp.where(head_of_lane == h, 1.0, 0.0).astype(BF16)
    enter[...] = one_hot(maps[1:2, 0:HALO], ROWS)
    loads["w_qkv"].wait()
    loads["gain_attn"].wait()
    loads["gain_merge"].wait()
    arrive(halo)

    for t in range(2):
        part = dot(enter[CELLS + t * GROUPS : CELLS + (t + 1) * GROUPS, :], halo_recv[...])
        cot[:, t * WIDTH : (t + 1) * WIDTH] = part.astype(BF16)
    members = [(step, flip) for flip in (0, 1) for step in range(4)]
    orders = (("x", "y"), ("y", "x"))
    m_cot[0, 0:GROUPS, :] = cot[...]
    m_cot[1, 0:GROUPS, :] = cot[...]
    m_cots = []
    for step in (1, 2, 3):
        for half in (0, 1):
            target = m_cot.at[half, pl.ds(step * GROUPS, GROUPS)]
            m_cots.append(send(cot, target, along(orders[half][0], step)))
    flat[...] = dot(enter[0:CELLS, :], halo_recv[...])
    (centred,), inverse = norm_parts([flat[...]], WIDTH)
    inverse_a[...] = inverse
    hat[...] = centred * inverse
    normal[...] = (hat[...] * gain_attn[...]).astype(BF16)
    qkv[...] = dot(normal[...], w_qkv[...]).astype(BF16)

    def spread(block):
        return jnp.concatenate([block] * HEADS, axis=0) * heads[...]

    def gather(wide):
        total = wide[0:64]
        for h in range(1, HEADS):
            total = jnp.where(head_of_lane == h, wide[h * 64 : (h + 1) * 64], total)
        return total

    def over_windows(body):
        def step(i, carry):
            for w in range(TOGETHER):
                body(rows(i * TOGETHER + w, 64))
            return carry

        lax.fori_loop(0, 8 // TOGETHER, step, 0)

    def forward(here):
        query, key, value = (qkv[here, i * WIDTH : (i + 1) * WIDTH] for i in range(3))
        scores = dot(key, spread(query), 1, 1) * FACTOR
        powers = jnp.exp(scores - jnp.max(scores, axis=0, keepdims=True))
        weights = powers * (1.0 / jnp.sum(powers, axis=0, keepdims=True))
        probs[here, :] = weights
        attended[here, :] = gather(dot(weights.astype(BF16), value, 0, 0)).astype(BF16)

    over_windows(forward)
    loads["w_proj"].wait()
    summed[...] = (flat[...] + dot(attended[...], w_proj[...])).astype(BF16).astype(F32)

    shaped = summed[...].reshape(8, 8, 8, WIDTH)
    slabs = [shaped[:, o].reshape(GROUPS, WIDTH) for o in range(8)]
    centred, inverse = norm_parts(slabs, 8 * WIDTH)
    for o in range(8):
        lanes = slice(o * WIDTH, (o + 1) * WIDTH)
        hat_m[:, lanes] = centred[o] * inverse
        nm[:, lanes] = (hat_m[:, lanes] * gain_merge[:, lanes]).astype(BF16)
    m_rows = []
    for at, (step, flip) in enumerate(members):
        for half in (0, 1):
            axis, core_at = orders[half][0], (core, other_core)[flip]
            block = rows(half * 8 + core_at * 4 + lax.rem(coordinate[axis] + step, 4), 128)
            if at == 0:
                m_nm[half, 0:GROUPS, :] = nm[:, block]
            else:
                target = m_nm.at[half, pl.ds(at * GROUPS, GROUPS)]
                m_rows.append(send(nm.at[:, block], target, along(axis, step, core_at)))
    loads["w_merge"].wait()
    result = dot(nm[...], w_merge[...]).astype(BF16)
    for t in range(2):
        stacked[CELLS + t * GROUPS : CELLS + (t + 1) * GROUPS, :] = result[:, t * WIDTH : (t + 1) * WIDTH]
    hats, grads = [], []
    for o in range(8):
        lanes = slice(o * WIDTH, (o + 1) * WIDTH)
        grad = dot(cot[...], w_merge[lanes, :], 1, 1)
        hats.append(hat_m[:, lanes])
        grads.append(grad * gain_merge[:, lanes])
        g_sum[o : o + 1, :] = jnp.sum(grad * hats[o], axis=0, keepdims=True)
    grads = norm_back(hats, grads, inverse, 8 * WIDTH)
    joined = jnp.stack([g.reshape(8, 8, WIDTH) for g in grads], axis=1).reshape(CELLS, WIDTH)
    d_summed[...] = joined.astype(BF16)

    q_sum[0, :, WIDTH:] = dot(attended[...], d_summed[...], 0, 0)
    d_attended[...] = dot(d_summed[...], w_proj[...], 1, 1).astype(BF16)

    def backward_value(here):
        wide = spread(d_attended[here, :])
        d_qkv[here, 2 * WIDTH :] = dot(probs[here, :].astype(BF16), wide).astype(BF16)

    over_windows(backward_value)
    q_sum[0, :, 0:WIDTH] = dot(normal[...], d_qkv[:, 2 * WIDTH :], 0, 0)

    def q_start(part):
        return send(q_sum.at[part, :, rows(other_core, WIDTH)], q_near.at[part], partner)

    q_chips = [q_start(0)]

    def backward(here):
        query, key, value = (qkv[here, i * WIDTH : (i + 1) * WIDTH] for i in range(3))
        weights = probs[here, :]
        wide = spread(d_attended[here, :])
        d_probs = dot(value, wide, 1, 1)
        inner = jnp.sum(d_probs * weights, axis=0, keepdims=True)
        d_scores = (weights * (d_probs - inner) * FACTOR).astype(BF16)
        d_key = dot(d_scores, spread(query))
        d_query = gather(dot(d_scores, key, 0, 0))
        d_qkv[here, 0:WIDTH] = d_query.astype(BF16)
        d_qkv[here, WIDTH : 2 * WIDTH] = d_key.astype(BF16)

    def m_second(half):
        second = orders[half][1]
        m_acc1[half] = dot(m_nm[half], m_cot[half], 0, 0)
        copies = []
        for step in (1, 2, 3):
            chunk = rows(lax.rem(coordinate[second] + step, 4), 32)
            copies.append(send(m_acc1.at[half, chunk], m_in2.at[half, step - 1], along(second, step)))
        return copies


    def q_first(part):
        q_chips[part].wait_recv()
        q_half[part] = q_sum[part, :, rows(core, WIDTH)] + q_near[part]
        copies = []
        for half in (0, 1):
            axis = orders[half][0]
            for step in (1, 2, 3):
                chunk = rows(half * 4 + lax.rem(coordinate[axis] + step, 4), 32)
                target = q_in1.at[part, half, step - 1]
                copies.append(send(q_half.at[part, chunk], target, along(axis, step)))
        return copies

    def q_tile(at):
        return rows(lax.div(at, 2), 16), rows(lax.rem(at, 2), 128)

    def q_second(part, came):
        arrive(came)
        copies = []
        for half in (0, 1):
            first, second = orders[half]
            own = q_half[part, rows(half * 4 + coordinate[first], 32), :]
            q_acc1[part, half] = own + q_in1[part, half, 0] + q_in1[part, half, 1] + q_in1[part, half, 2]
            for step in (1, 2, 3):
                chunk = q_acc1.at[(part, half) + q_tile(lax.rem(coordinate[second] + step, 4))]
                copies.append(send(chunk, q_in2.at[part, half, step - 1], along(second, step)))
        return copies

    def q_third(part, came):
        arrive(came)
        for half in (0, 1):
            own = q_acc1[(part, half) + q_tile(coordinate[orders[half][1]])]
            total = own + q_in2[part, half, 0] + q_in2[part, half, 1] + q_in2[part, half, 2]
            q_in3[part, z, half * 16 : (half + 1) * 16, :] = total
        mine = q_in3.at[part, z]
        return [send(mine, mine, along("z", step)) for step in range(1, 8)]

    def q_lanes(part, at, count):
        return rows((1 - part) * (512 // count) + core * (WIDTH // count) + at, count)

    def q_fourth(part, came):
        arrive(came)
        total = q_in3[part, 0]
        for i in range(1, 8):
            total = total + q_in3[part, i]
        copies = []
        for half in (0, 1):
            first, second = orders[half]
            high, low = lax.div(coordinate[second], 2), lax.rem(coordinate[second], 2)
            here = (rows(half * 8 + coordinate[first] * 2 + high, 16), q_lanes(part, low, 128))
            q_out[here] = (total[half * 16 : (half + 1) * 16] * TOKEN_SCALE).astype(BF16)
            place = q_out.at[here]
            copies += [send(place, place, along(second, step)) for step in (1, 2, 3)]
        return copies

    def q_fifth(part, came):
        arrive(came)
        copies = []
        for half in (0, 1):
            first = orders[half][0]
            place = q_out.at[rows(half * 4 + coordinate[first], 32), q_lanes(part, 0, WIDTH)]
            copies += [send(place, place, along(first, step)) for step in (1, 2, 3)]
        return copies

    def q_sixth(part, came):
        arrive(came)
        place = q_out.at[:, q_lanes(part, 0, WIDTH)]
        return send(place, place, partner)

    last, handed = [], []

    def hand(source, target):
        copy = pltpu.make_async_copy(source, target, out_sem.at[len(handed)])
        copy.start()
        handed.append(copy)

    def m_third(came):
        arrive(came)
        for half in (0, 1):
            own = m_acc1[half, rows(coordinate[orders[half][1]], 32), :]
            m_acc2[half] = own + m_in2[half, 0] + m_in2[half, 1] + m_in2[half, 2]
        copies = []
        for step in range(1, 8):
            there = lax.rem(z + step, 8)
            chunk = m_acc2.at[:, rows(lax.div(there, 4), 16), rows(lax.rem(there, 4), 128)]
            copies.append(send(chunk, m_in3.at[step - 1], along("z", step)))
        return copies

    def g_start(total, into, axis, count):
        into[coordinate[axis]] = total
        mine = into.at[coordinate[axis]]
        return [send(mine, mine, along(axis, step)) for step in range(1, count)]

    def g_total(into, count):
        total = into[0]
        for i in range(1, count):
            total = total + into[i]
        return total

    def m_place(half, x_or_y_first, x_or_y_second):
        return half * 1024 + core * 512 + x_or_y_first * 128 + x_or_y_second * 32

    def m_fourth(half):
        first, second = orders[half]
        high, lane = lax.div(z, 4), rows(lax.rem(z, 4), 128)
        total = m_acc2[half, rows(high, 16), lane]
        for step in range(7):
            total = total + m_in3[step, half]
        start = m_place(half, coordinate[first], coordinate[second]) + high * 16
        here = (pl.ds(pl.multiple_of(start, 16), 16), lane)
        d_merge[here] = (total * MERGE_SCALE).astype(BF16)
        place = d_merge.at[here]
        return [send(place, place, along("z", step)) for step in range(1, 8)]

    def m_pass(half, came):
        mine, theirs = (rows(half * 8 + c * 4 + came, 128) for c in (core, other_core))
        place = d_merge.at[mine]
        last.append((send(place, place, partner), theirs))
        hand(place, d_merge_out.at[mine])

    def m_fifth(half):
        first, second = orders[half]
        arrive(m_copies[half])
        start = m_place(half, coordinate[first], coordinate[second])
        place = d_merge.at[pl.ds(pl.multiple_of(start, 32), 32)]
        return [send(place, place, along(second, step)) for step in (1, 3, 2)]

    def m_sixth(half):
        first = orders[half][0]
        arrive(m_copies[half])
        place = d_merge.at[rows(half * 8 + core * 4 + coordinate[first], 128)]
        copies = [send(place, place, along(first, step)) for step in (1, 3, 2)]
        m_pass(half, coordinate[first])
        return copies

    arrive(m_cots)
    m_pairs = []
    for half in (0, 1):
        source = m_cot.at[half, pl.ds(0, 4 * GROUPS)]
        m_pairs.append(send(source, m_cot.at[half, pl.ds(4 * GROUPS, 4 * GROUPS)], partner))
    early = q_first(0)
    arrive(m_pairs)
    arrive(m_rows)
    m_copies = [m_second(0), m_second(1)]
    over_windows(backward)
    q_sum[1] = dot(normal[...], d_qkv[:, 0 : 2 * WIDTH], 0, 0)
    q_chips.append(q_start(1))
    d_normal = dot(d_qkv[...], w_qkv[...], 1, 1)
    g_sum[8:16, :] = jnp.zeros((8, WIDTH), F32)
    g_sum[8:9, :] = jnp.sum(d_normal * hat[...], axis=0, keepdims=True)
    g_chip = send(g_sum.at[:, rows(other_core, 128)], g_near, partner)
    late = q_first(1)
    (d_flat,) = norm_back([hat[...]], [d_normal * gain_attn[...]], inverse_a[...], WIDTH)
    stacked[0:CELLS, :] = (d_summed[...].astype(F32) + d_flat).astype(BF16)
    back[...] = one_hot(maps[2:3, 0:ROWS], HALO)
    back_send[...] = dot(back[...], stacked[...]).astype(BF16)
    halo = []
    for kind, start, size in list(zip(KINDS, STARTS, SIZES))[1:]:
        block = pl.ds(start, size)
        halo.append(send(back_send.at[block], back_recv.at[block], neighbour(kind, 1)))
    back_recv[0 : SIZES[0], :] = back_send[0 : SIZES[0], :]
    early = q_second(0, early)
    m_copies = m_third(m_copies[0] + m_copies[1])
    g_chip.wait_recv()
    g_copies = g_start(g_sum[:, rows(core, 128)] + g_near[...], g_in1, "x", 4)
    home[...] = one_hot(maps[3:4, 0:HALO], ROWS)

    arrive(m_copies)
    m_copies = [m_fourth(0), m_fourth(1)]
    late = q_second(1, late)
    early = q_third(0, early)
    arrive(g_copies)
    g_copies = g_start(g_total(g_in1, 4), g_in2, "y", 4)

    arrive(halo)
    placed = dot(home[...], back_recv[...]).astype(BF16)
    d_tokens[...] = placed[0:CELLS]
    merged[:, 0:WIDTH] = placed[CELLS : CELLS + GROUPS]
    merged[:, WIDTH:] = placed[CELLS + GROUPS :]
    hand(d_tokens, d_tokens_out)
    hand(merged, merged_out)
    late = q_third(1, late)
    m_copies = [m_fifth(0), m_fifth(1)]
    arrive(g_copies)
    g_copies = g_start(g_total(g_in2, 4), g_in3, "z", 8)
    early = q_fourth(0, early)
    m_copies = [m_sixth(0), m_sixth(1)]
    late = q_fourth(1, late)
    early = q_fifth(0, early)
    arrive(g_copies)
    g_all[:, rows(core, 128)] = g_total(g_in3, 8)
    g_mine = g_all.at[:, rows(core, 128)]
    g_last = send(g_mine, g_mine, partner)
    late = q_fifth(1, late)
    early = q_sixth(0, early)
    g_last.wait_recv()
    total = g_all[...]
    for o in range(8):
        d_gain_merge[:, o * WIDTH : (o + 1) * WIDTH] = total[o : o + 1] * MERGE_SCALE
    d_gain_attn[...] = total[8:9] * TOKEN_SCALE
    hand(d_gain_merge, d_gain_merge_out)
    hand(d_gain_attn, d_gain_attn_out)
    for at, step in enumerate((1, 3, 2)):
        for half in (0, 1):
            arrive([m_copies[half][at]])
            m_pass(half, lax.rem(coordinate[orders[half][0]] + 4 - step, 4))
    late = q_sixth(1, late)
    arrive([early])
    hand(q_out.at[:, pl.ds(2 * WIDTH, WIDTH)], d_qkv_out.at[:, pl.ds(2 * WIDTH, WIDTH)])
    hand(q_out.at[:, pl.ds(3 * WIDTH, WIDTH)], d_proj_out)
    for copy, theirs in last:
        arrive([copy])
        hand(d_merge.at[theirs], d_merge_out.at[theirs])
    arrive([late])
    hand(q_out.at[:, pl.ds(0, 2 * WIDTH)], d_qkv_out.at[:, pl.ds(0, 2 * WIDTH)])
    for copy in handed:
        copy.wait()
    for copy in started[-SENDING:]:
        copy.wait_send()


def hand_out(*refs):
    given, outs, held, sems = refs[:7], refs[7:14], refs[14:21], refs[21]
    parts = [(i, None) for i in range(6)] + [(6, pl.ds(at * 512, 512)) for at in range(4)]
    both = []
    for at, (i, part) in enumerate(parts):
        source, stage, target = (r[i] if part is None else r[i].at[part] for r in (given, held, outs))
        both.append((
            pltpu.make_async_copy(source, stage, sems.at[0, at]),
            pltpu.make_async_copy(stage, target, sems.at[1, at]),
        ))
    for copy_in, _ in both[::-1]:
        copy_in.start()
    for copy_in, copy_out in both[::-1]:
        copy_in.wait()
        copy_out.start()
    for _, copy_out in both:
        copy_out.wait()


def local(maps, tokens, cotangent, gain_attn, w_qkv, w_proj, gain_merge, w_merge):
    hbm = pl.BlockSpec(memory_space=pltpu.HBM)
    held = pl.pallas_call(
        kernel,
        out_shape=(
            jax.ShapeDtypeStruct((GROUPS, 512), BF16),
            jax.ShapeDtypeStruct((CELLS, WIDTH), BF16),
            jax.ShapeDtypeStruct((1, WIDTH), F32),
            jax.ShapeDtypeStruct((WIDTH, 3 * WIDTH), BF16),
            jax.ShapeDtypeStruct((WIDTH, WIDTH), BF16),
            jax.ShapeDtypeStruct((1, 8 * WIDTH), F32),
            jax.ShapeDtypeStruct((8 * WIDTH, 512), BF16),
        ),
        in_specs=[hbm] * 8,
        out_specs=[hbm] * 7,
        scratch_shapes=[
            pltpu.VMEM((GROUPS, 512), BF16),
            pltpu.VMEM((1, WIDTH), F32),
            pltpu.VMEM((1, 8 * WIDTH), F32),
            pltpu.VMEM((WIDTH, 3 * WIDTH), BF16),
            pltpu.VMEM((WIDTH, WIDTH), BF16),
            pltpu.VMEM((8 * WIDTH, 512), BF16),
            pltpu.VMEM((HALO, ROWS), BF16),
            pltpu.VMEM((ROWS, HALO), BF16),
            pltpu.VMEM((HALO, ROWS), BF16),
            pltpu.VMEM((ROWS, HALO), BF16),
            pltpu.VMEM((8, 768), jnp.int32),
            pltpu.SemaphoreType.DMA((8,)),
            pltpu.VMEM((ROWS, WIDTH), BF16),
            pltpu.VMEM((HALO, WIDTH), BF16),
            pltpu.VMEM((HALO, WIDTH), BF16),
            pltpu.VMEM((HALO, WIDTH), BF16),
            pltpu.VMEM((HALO, WIDTH), BF16),
            pltpu.VMEM((CELLS, WIDTH), F32),
            pltpu.VMEM((CELLS, WIDTH), F32),
            pltpu.VMEM((CELLS, WIDTH), BF16),
            pltpu.VMEM((CELLS, 1), F32),
            pltpu.VMEM((CELLS, 3 * WIDTH), BF16),
            pltpu.VMEM((CELLS, 512), F32),
            pltpu.VMEM((CELLS, WIDTH), BF16),
            pltpu.VMEM((CELLS, WIDTH), F32),
            pltpu.VMEM((CELLS, WIDTH), BF16),
            pltpu.VMEM((CELLS, WIDTH), BF16),
            pltpu.VMEM((CELLS, 3 * WIDTH), BF16),
            pltpu.VMEM((CELLS, WIDTH), BF16),
            pltpu.VMEM((GROUPS, 512), BF16),
            pltpu.VMEM((GROUPS, 8 * WIDTH), BF16),
            pltpu.VMEM((GROUPS, 8 * WIDTH), F32),
            pltpu.VMEM((2, 8 * GROUPS, 128), BF16),
            pltpu.VMEM((2, 8 * GROUPS, 512), BF16),
            pltpu.VMEM((2, 128, 512), F32),
            pltpu.VMEM((2, 3, 32, 512), F32),
            pltpu.VMEM((2, 32, 512), F32),
            pltpu.VMEM((7, 2, 16, 128), F32),
            pltpu.VMEM((2, WIDTH, 512), F32),
            pltpu.VMEM((2, WIDTH, WIDTH), F32),
            pltpu.VMEM((2, WIDTH, WIDTH), F32),
            pltpu.VMEM((2, 2, 3, 32, WIDTH), F32),
            pltpu.VMEM((2, 2, 32, WIDTH), F32),
            pltpu.VMEM((2, 2, 3, 16, 128), F32),
            pltpu.VMEM((2, 8, 32, 128), F32),
            pltpu.VMEM((WIDTH, 1024), BF16),
            pltpu.VMEM((16, WIDTH), F32),
            pltpu.VMEM((16, 128), F32),
            pltpu.VMEM((4, 16, 128), F32),
            pltpu.VMEM((4, 16, 128), F32),
            pltpu.VMEM((8, 16, 128), F32),
            pltpu.VMEM((16, WIDTH), F32),
            pltpu.VMEM((GROUPS, 512), BF16),
            pltpu.VMEM((CELLS, WIDTH), BF16),
            pltpu.VMEM((1, WIDTH), F32),
            pltpu.VMEM((1, 8 * WIDTH), F32),
            pltpu.VMEM((8 * WIDTH, 512), BF16),
            pltpu.SemaphoreType.DMA((23,)),
            pltpu.SemaphoreType.DMA((SENDING,)),
            pltpu.SemaphoreType.DMA((COPIES,)),
        ],
        compiler_params=pltpu.CompilerParams(
            collective_id=0, has_side_effects=True, vmem_limit_bytes=60 * 1024 * 1024
        ),
        cost_estimate=pl.CostEstimate(flops=4 * 10**9, bytes_accessed=12 * 10**6, transcendentals=262144),
        name="window_step",
    )(
        tokens.reshape(CELLS, WIDTH), cotangent.reshape(GROUPS, 512),
        gain_attn.reshape(1, WIDTH), gain_merge.reshape(1, 8 * WIDTH),
        w_qkv, w_proj, w_merge, maps,
    )
    outs = pl.pallas_call(
        hand_out,
        out_shape=[jax.ShapeDtypeStruct(h.shape, h.dtype) for h in held],
        in_specs=[pl.BlockSpec(memory_space=pl.ANY)] * 7,
        out_specs=[hbm] * 7,
        scratch_shapes=[pltpu.VMEM(h.shape, h.dtype) for h in held] + [pltpu.SemaphoreType.DMA((2, 10))],
        compiler_params=pltpu.CompilerParams(vmem_limit_bytes=60 * 1024 * 1024),
        name="hand_out",
    )(*held)
    merged, d_tokens, d_gain_attn, d_qkv, d_proj, d_gain_merge, d_merge = outs
    return (
        merged.reshape(cotangent.shape), d_tokens.reshape(tokens.shape), d_gain_attn.reshape(WIDTH),
        d_qkv, d_proj, d_gain_merge.reshape(8 * WIDTH), d_merge,
    )


def solution(mesh):
    maps = np.full((8, 768), -1, np.int32)
    for at, rows_of_columns in enumerate(orderings()):
        maps[at, : len(rows_of_columns)] = rows_of_columns
    box, whole = P("gx", "gy", "gz", None), P()
    return jax.shard_map(
        functools.partial(local, jnp.asarray(maps)),
        mesh=mesh,
        in_specs=(box, box, whole, whole, whole, whole, whole),
        out_specs=(box, box, whole, whole, whole, whole, whole),
        check_vma=False,
    )
```
